512 devices in a mesh: emb: 16 (over y_hi, x, core), dense: 32 (over y_lo, z).
Axes of the slice: x: 4, y: 4 (y_hi: 2, y_lo: 2; y = y_hi * 2 + y_lo), z: 16, core: 2. Of those that a mesh axis runs over, the one named last changes fastest.
Arguments:
- codes: int32 [16, 98304, 16], P('emb', 'dense'), may hold values from 0 to 255
- row_bag: int32 [16, 98304], P('emb', 'dense'), may hold values from 0 to 255
- codebook: bfloat16 [16, 256, 128], P('emb'), may hold values from -3 to 3
- w_in: bfloat16 [2048, 4096], P('emb'), may hold values from -0.125 to 0.125
- w_out: float32 [4096], replicated, may hold values from -0.09375 to 0.09375
- labels: float32 [8192], P('dense'), may hold values from 0 to 1
Outputs:
- grad_codebook: float32 [16, 256, 128], P('emb')
- grad_w_in: float32 [2048, 4096], P('emb')
- grad_w_out: float32 [4096], replicated
The draws below stay inside these ranges and needn't reach their ends.
Inputs may be any that keep to these rules, and one draw needn't show every extreme that they name: `row_bag`: bags are ragged and may be empty.
All inputs are finite; a program needn't handle non-finite values.
Results may differ from the reference program's by a relative error of at most 0.0025.
Values may be sent and summed in bfloat16 or wider, within the bound.
A program may use at most 64 MiB of HBM per device.

```python
import jax
import jax.numpy as jnp
from jax import lax

D_FIELD = 128
SUB = 16
CENT = 256
SUBW = 8
HID = 4096
SAMP = 256
ROWS_DEV = 3072
FIELDS = 16
SAMPLES = 8192
BATCH_ROWS = 98304


def touch_ends(array, key, smallest, largest):
    spot = [jax.random.randint(jax.random.fold_in(key, axis), (), 0, length) for axis, length in enumerate(array.shape)]
    main_axis = array.shape.index(max(array.shape))
    next_to = spot[:main_axis] + [(spot[main_axis] + 1) % array.shape[main_axis]] + spot[main_axis + 1:]
    return array.at[tuple(spot)].set(smallest).at[tuple(next_to)].set(largest)


def level_of(own_key, shape, split, low, largest):
    factor_of = 1.0
    for axis_at, shards_of in split:
        draws = jax.random.uniform(jax.random.fold_in(jax.random.fold_in(own_key, 6), axis_at), (shards_of,), jnp.float32, low / len(split), largest / len(split))
        factor_of = factor_of * jnp.repeat(jnp.exp(draws), shape[axis_at] // shards_of).reshape((-1,) + (1,) * (len(shape) - 1 - axis_at))
    return factor_of


def normal_values(own_key, extent, deviation, most, shards=(), kind=jnp.bfloat16):
    level = level_of(own_key, extent, shards, -0.22, 0.18) if shards else 1.0
    result = jax.random.normal(own_key, extent, jnp.float32) * deviation * level
    return jnp.minimum(jnp.maximum(result, -most), most).astype(kind)


def setup_inputs(seed: int = 0) -> dict:
    seeds = jax.random.split(jax.random.key(seed), 7)
    return {
        "codes": touch_ends(jax.random.randint(seeds[0], (FIELDS, BATCH_ROWS, SUB), 0, CENT), jax.random.fold_in(seeds[0], 1), 0, CENT - 1).astype(jnp.int32),
        "row_bag": touch_ends(jax.random.randint(seeds[1], (FIELDS, BATCH_ROWS), 0, SAMP), jax.random.fold_in(seeds[1], 1), 0, SAMP - 1).astype(jnp.int32),
        "codebook": normal_values(seeds[2], (FIELDS, CENT, D_FIELD), 0.5, 3.0, ((0, 16),)),
        "w_in": normal_values(seeds[3], (FIELDS * D_FIELD, HID), (FIELDS * D_FIELD) ** -0.5, 0.125, ((0, 16),)),
        "w_out": normal_values(seeds[4], (HID,), HID ** -0.5, 0.09375, (), jnp.float32),
        "labels": jnp.clip(1.0 * jax.random.uniform(seeds[5], (SAMPLES,), jnp.float32) ** level_of(seeds[5], (SAMPLES,), ((0, 32),), -0.2, 0.2), 0.0, 1.0),
    }


def silu_slope(value):
    gate = jax.nn.sigmoid(value)
    return gate + value * gate * (1.0 - gate)


def pool_field(rows, ids):
    return jax.ops.segment_sum(rows.astype(jnp.float32), ids, SAMPLES)


def pick_rows(table_rows, ids):
    return table_rows[ids]


def reference(codes, row_bag, codebook, w_in, w_out, labels):
    table = codebook.reshape(FIELDS, CENT, SUB, SUBW)
    field_ids = jnp.arange(FIELDS, dtype=jnp.int32)[:, None, None]
    sub_ids = jnp.arange(SUB, dtype=jnp.int32)[None, None, :]
    decoded = table[field_ids, codes, sub_ids].reshape(FIELDS, BATCH_ROWS, D_FIELD)
    owner = (jnp.arange(BATCH_ROWS, dtype=jnp.int32) // ROWS_DEV) * SAMP
    bags = (row_bag + owner[None, :]).astype(jnp.int32)
    pooled = jax.vmap(pool_field)(decoded, bags).astype(jnp.bfloat16)
    weights = w_in.reshape(FIELDS, D_FIELD, HID)

    def add_field(total, pair):
        rows, block = pair
        return total + jnp.dot(rows, block, preferred_element_type=jnp.float32), None

    pre, _ = lax.scan(add_field, jnp.zeros((SAMPLES, HID), jnp.float32), (pooled, weights))
    act = jax.nn.silu(pre)
    logit = jnp.dot(act, w_out, precision=lax.Precision.HIGHEST)
    slope = jax.nn.sigmoid(logit) - labels
    grad_hidden = (slope[:, None] * w_out[None, :] * silu_slope(pre)).astype(jnp.bfloat16)
    grad_head = jnp.dot(slope, act, precision=lax.Precision.HIGHEST)

    def field_grads(pair):
        rows, block = pair
        grad_weight = lax.dot_general(rows, grad_hidden, (((0,), (0,)), ((), ())), preferred_element_type=jnp.float32)
        grad_pool = lax.dot_general(grad_hidden, block, (((1,), (1,)), ((), ())), preferred_element_type=jnp.float32)
        return grad_weight, grad_pool.astype(jnp.bfloat16)

    grad_weight, grad_pool = lax.map(field_grads, (pooled, weights))
    grad_weight = grad_weight.reshape(FIELDS * D_FIELD, HID)
    row_grads = jax.vmap(pick_rows)(grad_pool, bags).astype(jnp.float32).reshape(FIELDS, BATCH_ROWS, SUB, SUBW)

    def field_table(rows_grad, field_codes):
        def one_sub(sub_rows, sub_codes):
            return jax.ops.segment_sum(sub_rows, sub_codes, CENT)

        per_sub = jax.vmap(one_sub, in_axes=(1, 1))(rows_grad, field_codes)
        return jnp.transpose(per_sub, (1, 0, 2)).reshape(CENT, D_FIELD)

    grad_codebook = jax.vmap(field_table)(row_grads, codes)
    return grad_codebook, grad_weight, grad_head
```

```python
import functools

import jax
import jax.numpy as jnp
from jax import lax
from jax.experimental import pallas as pl
from jax.experimental.pallas import tpu as pltpu
from jax.sharding import PartitionSpec as P

D_FIELD = 128
SUB = 16
SUBW = 8
CENT = 256
EMB = 16
DENSE = 32
ZED = 16
SAMP = 256
WIDE = 256
HID = 4096
F32 = jnp.float32
BF16 = jnp.bfloat16
NT = (((1,), (1,)), ((), ()))
MESH = pl.DeviceIdType.MESH
BLOCK = 144


def pool_kernel(codes, bag, table, pooled, low, high, members):
    rows = codes.shape[1]

    def onehot(row):
        ids = lax.broadcasted_iota(jnp.int32, (CENT, rows), 0)
        return jnp.where(row == ids, 1.0, 0.0).astype(BF16)

    members[...] = onehot(bag[...])

    def step(m, carry):
        count = lax.dot_general(onehot(codes[pl.ds(m, 1), :]), members[...], NT, preferred_element_type=F32)
        upper = jnp.floor(count * (1.0 / 256.0))
        lower = count - upper * 256.0
        place = pl.ds(pl.multiple_of(m * CENT, CENT), CENT)
        low[place, :] = lower.astype(BF16)
        high[place, :] = upper.astype(BF16)
        part = table[pl.ds(pl.multiple_of(m * SUBW, SUBW), SUBW), :].astype(BF16)
        pooled[pl.ds(pl.multiple_of(m * SUBW, SUBW), SUBW), :] = jnp.dot(
            part, lower.astype(BF16), preferred_element_type=F32
        ) + 256.0 * jnp.dot(part, upper.astype(BF16), preferred_element_type=F32)
        return carry

    lax.fori_loop(0, SUB, step, 0)


def pool(codes, bag, table):
    vmem = pl.BlockSpec(memory_space=pltpu.VMEM)
    counts = jax.ShapeDtypeStruct((SUB * CENT, SAMP), BF16)
    return pl.pallas_call(
        pool_kernel,
        out_shape=(jax.ShapeDtypeStruct((D_FIELD, SAMP), F32), counts, counts),
        in_specs=[vmem] * 3,
        out_specs=(vmem,) * 3,
        scratch_shapes=[pltpu.VMEM((SAMP, codes.shape[1]), BF16)],
        compiler_params=pltpu.CompilerParams(vmem_limit_bytes=40 << 20),
        name="pool",
    )(codes, bag, table)


def step_kernel(
    pooled, low, high, w_in, w_out, labels, out,
    w_cols, w_turned, fields, fields32, turned, logits, heads, pool_out, pool_in,
    y_out, y_in, mine, near_out, near_in, acc, far_out, far_in, red, cols,
    tab, tab_y, tab_near, tab_far,
    local, w_s, w_r, f_s, f_r, sib_s, sib_r, lg_s, lg_r, hd_s, hd_r, gp_s, gp_r,
    y_s, y_r, n_s, n_r, fr_s, fr_r, a_s, a_r,
    ty_s, ty_r, tn_s, tn_r, tf_s, tf_r, of_s, of_r, on_s, on_r, oy_s, oy_r,
):
    e = lax.axis_index("emb")
    g = lax.axis_index("dense")
    y = g // ZED
    z = lax.rem(g, ZED)
    zq = z // 4
    zr = lax.rem(z, 4)
    sib = e + 1 - 2 * lax.rem(e, 2)
    other = 1 - y

    def emb_at(i):
        return lax.rem(e + i, EMB)

    def emb_from(i):
        return lax.rem(e + EMB - i, EMB)

    def z_at(off):
        return (e, y * ZED + lax.rem(z + off + ZED, ZED))

    def send(src, dst, ss, rs, to):
        return pltpu.make_async_remote_copy(
            src_ref=src, dst_ref=dst, send_sem=ss, recv_sem=rs, device_id=to, device_id_type=MESH
        )

    def loop(lo, hi, body):
        def step(i, carry):
            body(i)
            return carry

        lax.fori_loop(lo, hi, step, 0)

    y_mate = (e, other * ZED + z)
    barrier = pltpu.get_barrier_semaphore()
    loop(1, EMB, lambda i: pl.semaphore_signal(barrier, inc=1, device_id=(emb_at(i), g), device_id_type=MESH))
    for off in (1, -1, 2, -2, 4, -4, 8):
        pl.semaphore_signal(barrier, inc=1, device_id=z_at(off), device_id_type=MESH)
    pl.semaphore_signal(barrier, inc=1, device_id=y_mate, device_id_type=MESH)
    pl.semaphore_wait(barrier, EMB - 1 + 8)

    def w_copy(i):
        cols_of = pl.ds(pl.multiple_of(emb_at(i) * WIDE, WIDE), WIDE)
        return send(w_in.at[:, cols_of], w_cols.at[e], w_s.at[i], w_r.at[i], (emb_at(i), g))

    def f_copy(i):
        return send(fields.at[e], fields.at[e], f_s.at[i], f_r.at[i], (emb_at(2 * i), g))

    def sib_copy(i):
        f = lax.rem(e + 2 * EMB - 2 * i, EMB)
        return send(fields.at[f], fields.at[f], sib_s.at[i], sib_r.at[i], (sib, g))

    fields[e] = pooled[...].astype(BF16)
    loop(1, 8, lambda i: f_copy(i).start())
    sib_copy(0).start()
    loop(1, EMB, lambda i: w_copy(i).start())
    own_w = pltpu.make_async_copy(
        w_in.at[:, pl.ds(pl.multiple_of(e * WIDE, WIDE), WIDE)], w_cols.at[e], local.at[0]
    )
    own_w.start()

    def forward(i):
        f_copy(i).wait_recv()
        sib_copy(i).start()

    loop(1, 8, forward)
    loop(0, 8, lambda i: sib_copy(i).wait_recv())
    own_w.wait()
    loop(1, EMB, lambda i: w_copy(i).wait_recv())
    for f in range(EMB):
        w_turned[:, f * D_FIELD : (f + 1) * D_FIELD] = w_cols[f].T

    pre = jnp.dot(w_turned[...], fields[...].reshape(EMB * D_FIELD, SAMP), preferred_element_type=F32)
    gate = jax.nn.sigmoid(pre)
    act = pre * gate
    w_row = jnp.concatenate([w_out[pl.ds(2 * e, 1), :], w_out[pl.ds(2 * e + 1, 1), :]], axis=1)
    w_rows = jnp.broadcast_to(w_row, (8, WIDE))
    logits[e] = jnp.dot(w_rows, act, precision=lax.Precision.HIGHEST, preferred_element_type=F32)

    def lg_copy(i):
        return send(logits.at[e], logits.at[e], lg_s.at[i], lg_r.at[i], (emb_at(i), g))

    loop(1, EMB, lambda i: lg_copy(i).start())

    for f in range(EMB):
        fields32[:, f] = fields[f].astype(F32).reshape(16, 8, SAMP)
    for c in range(4):
        for a in range(4):
            turned[c, a * 128 : (a + 1) * 128] = fields32[a * 4 + c].reshape(128, SAMP).astype(BF16)
    slant = gate + pre * gate * (1.0 - gate)
    w_left = jnp.broadcast_to(w_row[:, :128], (128, 128)).T
    w_right = jnp.broadcast_to(w_row[:, 128:], (128, 128)).T
    w_tall = jnp.concatenate([w_left, w_right], axis=0)
    w_tall = jnp.concatenate([w_tall, w_tall], axis=1)

    loop(1, EMB, lambda i: lg_copy(i).wait_recv())
    logit = logits[0]
    for f in range(1, EMB):
        logit = logit + logits[f]
    slope = jax.nn.sigmoid(logit) - labels[...]
    grad = (slope[:1] * w_tall * slant).astype(BF16)
    halves = (grad[:128], grad[128:])

    head = lax.dot_general(slope, act, NT, precision=lax.Precision.HIGHEST, preferred_element_type=F32)
    heads[e] = jnp.concatenate([head[:1, :128], head[:1, 128:], jnp.zeros((6, 128), F32)], axis=0)

    def hd_copy(i):
        return send(heads.at[e], heads.at[e], hd_s.at[i], hd_r.at[i], (emb_at(i), g))

    loop(1, EMB, lambda i: hd_copy(i).start())

    def gp_copy(i):
        return send(pool_out.at[emb_at(i)], pool_in.at[e], gp_s.at[i], gp_r.at[i], (emb_at(i), g))

    def gp_part(i):
        f = emb_at(i)
        pool_out[f] = jnp.dot(w_cols[f], grad, preferred_element_type=F32)

    def gp_start(i):
        gp_part(i)
        gp_copy(i).start()

    loop(1, EMB, gp_start)
    gp_part(0)
    pool_in[e] = pool_out[e]

    def grad_half(c, half):
        rhs = jnp.where(half == 0, halves[0], halves[1])
        return lax.dot_general(turned[c], rhs, NT, preferred_element_type=F32)

    def y_copy(k, c):
        return send(y_out.at[c], y_in.at[c], y_s.at[k], y_r.at[k], y_mate)

    near = (2, 1, -1)
    order = [lax.rem(z + off + 4, 4) for off in near] + [zr]
    for k, c in enumerate(order):
        y_out[c] = grad_half(c, other).astype(BF16)
        y_copy(k, c).start()
    for k, c in enumerate(order):
        mine[c] = grad_half(c, y)

    def near_copy(k):
        return send(near_out.at[k], near_in.at[k], n_s.at[k], n_r.at[k], z_at(near[k]))

    for k in range(3):
        c = order[k]
        y_copy(k, c).wait_recv()
        near_out[k] = mine[c] + y_in[c].astype(F32)
        near_copy(k).start()
    y_copy(3, zr).wait_recv()
    acc[...] = (mine[zr] + y_in[zr].astype(F32)).reshape(4, 128, 128)

    loop(1, EMB, lambda i: gp_copy(i).wait_recv())
    total = pool_in[0]
    for f in range(1, EMB):
        total = total + pool_in[f]
    grad_pool = total.astype(BF16)
    parts = []
    for m in range(SUB):
        rows = grad_pool[m * SUBW : (m + 1) * SUBW]
        span = slice(m * CENT, (m + 1) * CENT)
        parts.append(
            lax.dot_general(rows, low[span, :], NT, preferred_element_type=F32)
            + 256.0 * lax.dot_general(rows, high[span, :], NT, preferred_element_type=F32)
        )
    table = jnp.concatenate(parts, axis=0).T
    loop(1, EMB, lambda i: hd_copy(i).wait_recv())
    for yy in range(2):
        for zz in range(ZED):
            gg = yy * ZED + zz
            tab[yy, zz % 4, zz // 4, :8] = table[gg * 8 : gg * 8 + 8]
            tab[yy, zz % 4, zz // 4, 8:] = jnp.concatenate(
                [heads[gg // 2, gg % 2 : gg % 2 + 1], jnp.zeros((7, 128), F32)], axis=0
            )
    ty_copy = send(tab.at[other], tab_y, ty_s, ty_r, y_mate)
    ty_copy.start()

    for k in range(3):
        near_copy(k).wait_recv()
        acc[...] = acc[...] + near_in[k].reshape(4, 128, 128)

    def far_copy(m):
        return send(far_out.at[m - 1], far_in.at[m - 1], fr_s.at[m - 1], fr_r.at[m - 1], z_at(4 * m))

    for m in range(1, 4):
        far_out[m - 1] = acc[lax.rem(zq + m, 4)]
        far_copy(m).start()

    ty_copy.wait_recv()
    tab[y] = tab[y] + tab_y[...]

    def tn_copy(k):
        return send(tab.at[y, order[k]], tab_near.at[k], tn_s.at[k], tn_r.at[k], z_at(near[k]))

    for k in range(3):
        tn_copy(k).start()

    whole = acc[zq]
    for m in range(1, 4):
        far_copy(m).wait_recv()
        whole = whole + far_in[m - 1]
    red[...] = whole.reshape(EMB, 8, 128)

    def a_copy(i):
        return send(red.at[emb_at(i)], cols.at[e], a_s.at[i], a_r.at[i], (emb_at(i), g))

    loop(1, EMB, lambda i: a_copy(i).start())
    cols[e] = red[e]

    for k in range(3):
        tn_copy(k).wait_recv()
    tab_sum = tab[y, zr] + tab_near[0] + tab_near[1] + tab_near[2]
    tab[y, zr] = tab_sum

    def tf_copy(m):
        return send(
            tab.at[y, zr, lax.rem(zq + m, 4)], tab_far.at[m - 1], tf_s.at[m - 1], tf_r.at[m - 1], z_at(4 * m)
        )

    for m in range(1, 4):
        tf_copy(m).start()
    for m in range(1, 4):
        tf_copy(m).wait_recv()
    tab_whole = tab[y, zr, zq] + tab_far[0] + tab_far[1] + tab_far[2]
    out[y, zr, zq, 128:] = tab_whole
    loop(1, EMB, lambda i: a_copy(i).wait_recv())
    out[y, zr, zq, :128] = cols[...].reshape(128, 128)

    def block(off, m):
        src = lax.rem(z + 2 * ZED - off - 4 * m, ZED)
        return out.at[y, lax.rem(src, 4), src // 4]

    def of_copy(m):
        return send(block(0, 0), block(0, 0), of_s.at[m - 1], of_r.at[m - 1], z_at(4 * m))

    def of_wait(m):
        send(block(0, m), block(0, m), of_s.at[m - 1], of_r.at[m - 1], z_at(4 * m)).wait_recv()

    ways = (1, -1, 2)

    def on_copy(k, m):
        return send(block(0, m), block(0, m), on_s.at[k, m], on_r.at[k, m], z_at(ways[k]))

    def on_wait(k, m):
        got = block(ways[k], m)
        send(got, got, on_s.at[k, m], on_r.at[k, m], z_at(ways[k])).wait_recv()

    def oy_copy(k, m):
        got = block(0 if k == 0 else ways[k - 1], m)
        return send(got, got, oy_s.at[k, m], oy_r.at[k, m], y_mate)

    def oy_wait(k, m):
        src = lax.rem(z + 2 * ZED - (0 if k == 0 else ways[k - 1]) - 4 * m, ZED)
        got = out.at[other, lax.rem(src, 4), src // 4]
        send(got, got, oy_s.at[k, m], oy_r.at[k, m], y_mate).wait_recv()

    for m in range(1, 4):
        of_copy(m).start()
    for m in range(4):
        if m:
            of_wait(m)
        for k in range(3):
            on_copy(k, m).start()
        oy_copy(0, m).start()
    for m in range(4):
        for k in range(3):
            on_wait(k, m)
            oy_copy(k + 1, m).start()
    for m in range(4):
        for k in range(4):
            oy_wait(k, m)

    loop(1, 8, lambda i: f_copy(i).wait_send())
    loop(0, 8, lambda i: sib_copy(i).wait_send())

    def sent(i):
        w_copy(i).wait_send()
        lg_copy(i).wait_send()
        hd_copy(i).wait_send()
        gp_copy(i).wait_send()
        a_copy(i).wait_send()

    loop(1, EMB, sent)
    for k, c in enumerate(order):
        y_copy(k, c).wait_send()
    ty_copy.wait_send()
    for k in range(3):
        near_copy(k).wait_send()
        tn_copy(k).wait_send()
    for m in range(1, 4):
        far_copy(m).wait_send()
        tf_copy(m).wait_send()
        of_copy(m).wait_send()
    for m in range(4):
        for k in range(3):
            on_copy(k, m).wait_send()
        for k in range(4):
            oy_copy(k, m).wait_send()


def train(pooled, low, high, w_in, w_out, labels):
    vmem = pl.BlockSpec(memory_space=pltpu.VMEM)
    V, D = pltpu.VMEM, pltpu.SemaphoreType.DMA
    scratch = [
        V((EMB, D_FIELD, WIDE), BF16),
        V((WIDE, EMB * D_FIELD), BF16),
        V((EMB, D_FIELD, SAMP), BF16),
        V((16, EMB, 8, SAMP), F32),
        V((4, 512, SAMP), BF16),
        V((EMB, 8, SAMP), F32),
        V((EMB, 8, 128), F32),
        V((EMB, D_FIELD, SAMP), F32),
        V((EMB, D_FIELD, SAMP), F32),
        V((4, 512, 128), BF16),
        V((4, 512, 128), BF16),
        V((4, 512, 128), F32),
        V((3, 512, 128), F32),
        V((3, 512, 128), F32),
        V((4, 128, 128), F32),
        V((3, 128, 128), F32),
        V((3, 128, 128), F32),
        V((EMB, 8, 128), F32),
        V((EMB, 8, 128), F32),
        V((2, 4, 4, 16, 128), F32),
        V((4, 4, 16, 128), F32),
        V((3, 4, 16, 128), F32),
        V((3, 16, 128), F32),
        D((1,)),
    ]
    sems = [(16,), (8,), (8,), (16,), (16,), (16,), (4,), (3,), (3,), (16,), (), (3,), (3,), (3,), (3, 4), (4, 4)]
    for shape in sems:
        scratch += [D(shape), D(shape)] if shape else [D, D]
    return pl.pallas_call(
        step_kernel,
        out_shape=jax.ShapeDtypeStruct((2, 4, 4, BLOCK, 128), F32),
        in_specs=[vmem, vmem, vmem, pl.BlockSpec(memory_space=pl.ANY), vmem, vmem],
        out_specs=vmem,
        scratch_shapes=scratch,
        compiler_params=pltpu.CompilerParams(
            collective_id=1, has_side_effects=True, vmem_limit_bytes=48 << 20
        ),
        name="train_step",
    )(pooled, low, high, w_in, w_out, labels)


def spread_kernel(gathered, weight, table, head):
    a = pl.program_id(0)
    for c in range(4):
        for yy in range(2):
            for f in range(EMB):
                spot = f * WIDE + yy * 128
                weight[c * 8 : c * 8 + 8, spot : spot + 128] = gathered[yy, c, 0, f * 8 : f * 8 + 8]
            tab = gathered[yy, c, 0, 128:]
            gg = yy * ZED + a * 4 + c
            table[pl.ds(pl.multiple_of(gg * 8, 8), 8), :] = tab[:8]
            head[pl.ds(gg, 1), :] = tab[8:9]


def spread(gathered):
    return pl.pallas_call(
        spread_kernel,
        grid=(4,),
        out_shape=(
            jax.ShapeDtypeStruct((D_FIELD, HID), F32),
            jax.ShapeDtypeStruct((CENT, D_FIELD), F32),
            jax.ShapeDtypeStruct((DENSE, 128), F32),
        ),
        in_specs=[pl.BlockSpec((2, 4, 1, BLOCK, 128), lambda i: (0, 0, i, 0, 0))],
        out_specs=(
            pl.BlockSpec((32, HID), lambda i: (i, 0)),
            pl.BlockSpec((CENT, D_FIELD), lambda i: (0, 0)),
            pl.BlockSpec((DENSE, 128), lambda i: (0, 0)),
        ),
        name="spread",
    )(gathered)


def body(codes, row_bag, codebook, w_in, w_out, labels):
    pooled, low, high = pool(codes[0].T, row_bag, codebook[0].T.astype(F32))
    gathered = train(pooled, low, high, w_in, w_out.reshape(32, 128), labels.reshape(1, SAMP))
    weight, table, head = spread(gathered)
    return table[None], weight, head.reshape(HID)


def solution(mesh):
    in_specs = (
        P("emb", "dense", None),
        P("emb", "dense"),
        P("emb", None, None),
        P("emb", None),
        P(),
        P("dense"),
    )
    out_specs = (P("emb", None, None), P("emb", None), P())
    return jax.shard_map(body, mesh=mesh, in_specs=in_specs, out_specs=out_specs, check_vma=False)
```

```python
import functools

import jax
import jax.numpy as jnp
from jax import lax
from jax.experimental import pallas as pl
from jax.experimental.pallas import tpu as pltpu
from jax.sharding import PartitionSpec as P

D_FIELD = 128
SUB = 16
SUBW = 8
CENT = 256
EMB = 16
DENSE = 32
ZED = 16
SAMP = 256
WIDE = 256
HID = 4096
F32 = jnp.float32
BF16 = jnp.bfloat16
F8 = jnp.float8_e4m3fn
I16 = jnp.int16
NT = (((1,), (1,)), ((), ()))
MESH = pl.DeviceIdType.MESH
BLOCK = 160
GROUP = 4


def encode(value):
    top = jnp.maximum(jnp.max(jnp.abs(value), axis=0, keepdims=True), 1e-30)
    power = jnp.ceil(jnp.log2(top) + 0.001)
    coded = jnp.floor(value * jnp.exp2(15.0 - power) + 0.5)
    return coded.astype(jnp.int32).astype(I16), power


def tile_of(power):
    return jnp.broadcast_to(power, (16, power.shape[1])).astype(jnp.int32).astype(I16)


def number(coded):
    return coded.astype(jnp.int32).astype(F32)


def decode(coded, power):
    return number(coded) * jnp.exp2(number(power)[:1] - 15.0)


def step_kernel(
    codes_hbm, bag_hbm, book_hbm, w_in, w_out_hbm, labels_hbm, out,
    codes, bag, book, w_out, labels, table_t, members, pooled, low, high,
    w_cols, w_turned, fields, fields32, turned, logits, heads,
    gp_own, gp_sib, gp_got, gp_out, gp_in,
    y_out, y_in, mine, near_out, near_in, acc, far_out, far_in, red, cols,
    tab, tab_y, tab_near, tab_far,
    local, w_s, w_r, f_s, f_r, sib_s, sib_r, lg_s, lg_r, hd_s, hd_r, gs_s, gs_r, gp_s, gp_r,
    y_s, y_r, n_s, n_r, fr_s, fr_r, a_s, a_r,
    ty_s, ty_r, tn_s, tn_r, tf_s, tf_r, of_s, of_r, on_s, on_r, oy_s, oy_r,
):
    e = lax.axis_index("emb")
    g = lax.axis_index("dense")
    y = g // ZED
    z = lax.rem(g, ZED)
    zq = z // 4
    zr = lax.rem(z, 4)
    sib = e + 1 - 2 * lax.rem(e, 2)
    other = 1 - y

    def emb_at(i):
        return lax.rem(e + i, EMB)

    def emb_from(i):
        return lax.rem(e + EMB - i, EMB)

    def z_at(off):
        return (e, y * ZED + lax.rem(z + off + ZED, ZED))

    def send(src, dst, ss, rs, to):
        return pltpu.make_async_remote_copy(
            src_ref=src, dst_ref=dst, send_sem=ss, recv_sem=rs, device_id=to, device_id_type=MESH
        )

    def loop(lo, hi, body):
        def step(i, carry):
            body(i)
            return carry

        lax.fori_loop(lo, hi, step, 0)

    y_mate = (e, other * ZED + z)
    loads = [
        pltpu.make_async_copy(src, dst, local.at[1 + i])
        for i, (src, dst) in enumerate(
            ((bag_hbm, bag), (codes_hbm, codes), (book_hbm, book), (w_out_hbm, w_out), (labels_hbm, labels))
        )
    ]
    for load in loads:
        load.start()
    sent = []
    barrier = pltpu.get_barrier_semaphore()
    loop(1, EMB, lambda i: pl.semaphore_signal(barrier, inc=1, device_id=(emb_at(i), g), device_id_type=MESH))
    for off in (1, -1, 2, -2, 4, -4, 8):
        pl.semaphore_signal(barrier, inc=1, device_id=z_at(off), device_id_type=MESH)
    pl.semaphore_signal(barrier, inc=1, device_id=y_mate, device_id_type=MESH)
    pl.semaphore_wait(barrier, EMB - 1 + 8)

    def w_copy(i):
        cols_of = pl.ds(pl.multiple_of(emb_at(i) * WIDE, WIDE), WIDE)
        return send(w_in.at[:, cols_of], w_cols.at[e], w_s.at[i], w_r.at[i], (emb_at(i), g))

    def rows_of(f, h):
        return fields.at[f, pl.ds(h * 64, 64)]

    def f_copy(i, h):
        return send(rows_of(e, h), rows_of(e, h), f_s.at[h, i], f_r.at[h, i], (emb_at(2 * i), g))

    def sib_copy(i, h):
        f = lax.rem(e + 2 * EMB - 2 * i, EMB)
        return send(rows_of(f, h), rows_of(f, h), sib_s.at[h, i], sib_r.at[h, i], (sib, g))

    loop(1, EMB, lambda i: w_copy(i).start())
    sent.append(lambda: loop(1, EMB, lambda i: w_copy(i).wait_send()))
    own_w = pltpu.make_async_copy(
        w_in.at[:, pl.ds(pl.multiple_of(e * WIDE, WIDE), WIDE)], w_cols.at[e], local.at[0]
    )
    own_w.start()

    def onehot(row):
        ids = lax.broadcasted_iota(jnp.int32, (CENT, row.shape[1]), 0)
        return jnp.where(row == ids, 1.0, 0.0).astype(F8)

    for load in loads:
        load.wait()
    members[...] = onehot(bag[...])
    table_t[...] = book[...].astype(F32).T

    def count_step(step):
        at = step * GROUP
        picks = jnp.concatenate([onehot(codes[pl.ds(at + j, 1), :]) for j in range(GROUP)], axis=0)
        count = lax.dot_general(picks, members[...], NT, preferred_element_type=F32)
        upper = jnp.floor(count * (1.0 / 256.0))
        lower = (count - upper * 256.0).astype(BF16)
        upper = upper.astype(BF16)
        place = pl.ds(pl.multiple_of(at * CENT, CENT * GROUP), CENT * GROUP)
        low[place, :] = lower
        high[place, :] = upper
        rows = pl.ds(pl.multiple_of(at * SUBW, SUBW * GROUP), SUBW * GROUP)
        part = table_t[rows, :].astype(BF16)
        for j in range(GROUP):
            mine_at = slice(j * SUBW, (j + 1) * SUBW)
            span = slice(j * CENT, (j + 1) * CENT)
            pooled[pl.ds(pl.multiple_of((at + j) * SUBW, SUBW), SUBW), :] = jnp.dot(
                part[mine_at], lower[span], preferred_element_type=F32
            ) + 256.0 * jnp.dot(part[mine_at], upper[span], preferred_element_type=F32)

    for h in range(2):
        loop(h * 2, h * 2 + 2, count_step)
        fields[e, h * 64 : h * 64 + 64] = pooled[h * 64 : h * 64 + 64].astype(BF16)
        loop(1, 8, lambda i: f_copy(i, h).start())
        sib_copy(0, h).start()
        sent.append(lambda h=h: loop(1, 8, lambda i: f_copy(i, h).wait_send()))
        sent.append(lambda h=h: loop(0, 8, lambda i: sib_copy(i, h).wait_send()))

    def forward(i, h):
        f_copy(i, h).wait_recv()
        sib_copy(i, h).start()

    for h in range(2):
        loop(1, 8, lambda i: forward(i, h))
    own_w.wait()
    loop(1, EMB, lambda i: w_copy(i).wait_recv())
    for h in range(2):
        loop(0, 8, lambda i: sib_copy(i, h).wait_recv())
    for f in range(EMB):
        w_turned[:, f * D_FIELD : (f + 1) * D_FIELD] = w_cols[f].T

    pre = jnp.dot(w_turned[...], fields[...].reshape(EMB * D_FIELD, SAMP), preferred_element_type=F32)
    gate = jax.nn.sigmoid(pre)
    act = pre * gate
    w_row = jnp.concatenate([w_out[pl.ds(2 * e, 1), :], w_out[pl.ds(2 * e + 1, 1), :]], axis=1)
    w_rows = jnp.broadcast_to(w_row, (8, WIDE))
    logits[e] = jnp.dot(w_rows, act, precision=lax.Precision.HIGHEST, preferred_element_type=F32)

    def lg_copy(i):
        return send(logits.at[e], logits.at[e], lg_s.at[i], lg_r.at[i], (emb_at(i), g))

    loop(1, EMB, lambda i: lg_copy(i).start())
    sent.append(lambda: loop(1, EMB, lambda i: lg_copy(i).wait_send()))

    for f in range(EMB):
        fields32[:, f] = fields[f].astype(F32).reshape(16, 8, SAMP)
    for c in range(4):
        for a in range(4):
            turned[c, a * 128 : (a + 1) * 128] = fields32[a * 4 + c].reshape(128, SAMP).astype(BF16)
    slant = gate + pre * gate * (1.0 - gate)
    w_left = jnp.broadcast_to(w_row[:, :128], (128, 128)).T
    w_right = jnp.broadcast_to(w_row[:, 128:], (128, 128)).T
    w_tall = jnp.concatenate([w_left, w_right], axis=0)
    w_tall = jnp.concatenate([w_tall, w_tall], axis=1)

    loop(1, EMB, lambda i: lg_copy(i).wait_recv())
    logit = logits[0]
    for f in range(1, EMB):
        logit = logit + logits[f]
    slope = jax.nn.sigmoid(logit) - labels[...]
    grad = (slope[:1] * w_tall * slant).astype(BF16)
    halves = (grad[:128], grad[128:])

    head = lax.dot_general(slope, act, NT, precision=lax.Precision.HIGHEST, preferred_element_type=F32)
    heads[e] = jnp.concatenate([head[:1, :128], head[:1, 128:], jnp.zeros((6, 128), F32)], axis=0)

    def hd_copy(i):
        return send(heads.at[e], heads.at[e], hd_s.at[i], hd_r.at[i], (emb_at(i), g))

    loop(1, EMB, lambda i: hd_copy(i).start())
    sent.append(lambda: loop(1, EMB, lambda i: hd_copy(i).wait_send()))

    def grad_half(c, half):
        rhs = jnp.where(half == 0, halves[0], halves[1])
        return lax.dot_general(turned[c], rhs, NT, preferred_element_type=F32)

    def y_copy(k, c):
        return send(y_out.at[c], y_in.at[c], y_s.at[k], y_r.at[k], y_mate)

    near = (2, 1, -1)
    order = [lax.rem(z + off + 4, 4) for off in near] + [zr]
    for k, c in enumerate(order):
        y_out[c] = grad_half(c, other).astype(BF16)
        y_copy(k, c).start()
        sent.append(lambda k=k, c=c: y_copy(k, c).wait_send())
    core = lax.rem(e, 2)

    def gs_copy(i):
        return send(gp_sib.at[i], gp_got.at[i], gs_s.at[i], gs_r.at[i], (sib, g))

    def gs_start(i):
        gp_sib[i] = jnp.dot(w_cols[2 * i + 1 - core], grad, preferred_element_type=F32)
        gs_copy(i).start()

    loop(0, 8, gs_start)
    sent.append(lambda: loop(0, 8, lambda i: gs_copy(i).wait_send()))

    def gp_part(i):
        gp_own[i] = jnp.dot(w_cols[2 * i + core], grad, preferred_element_type=F32)

    loop(0, 8, gp_part)
    chip = e // 2

    def gp_copy(i):
        return send(
            gp_out.at[lax.rem(chip + i, 8)], gp_in.at[chip], gp_s.at[i], gp_r.at[i], (emb_at(2 * i), g)
        )

    def gp_start(i):
        c = lax.rem(chip + i, 8)
        gs_copy(c).wait_recv()
        coded, power = encode(gp_own[c] + gp_got[c])
        gp_out[c, :D_FIELD] = coded
        gp_out[c, D_FIELD:] = tile_of(power)
        gp_copy(i).start()

    loop(1, 8, gp_start)
    sent.append(lambda: loop(1, 8, lambda i: gp_copy(i).wait_send()))
    gs_copy(chip).wait_recv()
    for k, c in enumerate(order):
        mine[c] = grad_half(c, y)

    def near_copy(k):
        return send(near_out.at[k], near_in.at[k], n_s.at[k], n_r.at[k], z_at(near[k]))

    for k in range(3):
        c = order[k]
        y_copy(k, c).wait_recv()
        coded, power = encode(mine[c] + y_in[c].astype(F32))
        near_out[k, :512] = coded
        near_out[k, 512:] = tile_of(power)
        near_copy(k).start()
        sent.append(lambda k=k: near_copy(k).wait_send())
    y_copy(3, zr).wait_recv()
    acc[...] = (mine[zr] + y_in[zr].astype(F32)).reshape(4, 128, 128)

    loop(1, 8, lambda i: gp_copy(i).wait_recv())
    total = gp_own[chip] + gp_got[chip]
    for i in range(1, 8):
        c = lax.rem(chip + 8 - i, 8)
        total = total + decode(gp_in[c, :D_FIELD], gp_in[c, D_FIELD:])
    grad_pool = total.astype(BF16)
    parts = []
    for m in range(SUB):
        rows = grad_pool[m * SUBW : (m + 1) * SUBW]
        span = slice(m * CENT, (m + 1) * CENT)
        parts.append(
            lax.dot_general(rows, low[span, :], NT, preferred_element_type=F32)
            + 256.0 * lax.dot_general(rows, high[span, :], NT, preferred_element_type=F32)
        )
    table = jnp.concatenate(parts, axis=0).T
    loop(1, EMB, lambda i: hd_copy(i).wait_recv())
    for yy in range(2):
        for zz in range(ZED):
            gg = yy * ZED + zz
            tab[yy, zz % 4, zz // 4, :8] = table[gg * 8 : gg * 8 + 8]
            tab[yy, zz % 4, zz // 4, 8:] = jnp.concatenate(
                [heads[gg // 2, gg % 2 : gg % 2 + 1], jnp.zeros((7, 128), F32)], axis=0
            )
    ty_copy = send(tab.at[other], tab_y, ty_s, ty_r, y_mate)
    ty_copy.start()
    sent.append(lambda: ty_copy.wait_send())

    for k in range(3):
        near_copy(k).wait_recv()
        acc[...] = acc[...] + decode(near_in[k, :512], near_in[k, 512:]).reshape(4, 128, 128)

    def far_copy(m):
        return send(far_out.at[m - 1], far_in.at[m - 1], fr_s.at[m - 1], fr_r.at[m - 1], z_at(4 * m))

    for m in range(1, 4):
        coded, power = encode(acc[lax.rem(zq + m, 4)])
        far_out[m - 1, :128] = coded
        far_out[m - 1, 128:] = tile_of(power)
        far_copy(m).start()
        sent.append(lambda m=m: far_copy(m).wait_send())

    ty_copy.wait_recv()
    tab[y] = tab[y] + tab_y[...]

    def tn_copy(k):
        return send(tab.at[y, order[k]], tab_near.at[k], tn_s.at[k], tn_r.at[k], z_at(near[k]))

    for k in range(3):
        tn_copy(k).start()
        sent.append(lambda k=k: tn_copy(k).wait_send())

    whole = acc[zq]
    for m in range(1, 4):
        far_copy(m).wait_recv()
        whole = whole + decode(far_in[m - 1, :128], far_in[m - 1, 128:])
    red[...] = whole.reshape(EMB, 8, 128)

    def a_copy(i):
        return send(red.at[emb_at(i)], cols.at[e], a_s.at[i], a_r.at[i], (emb_at(i), g))

    loop(1, EMB, lambda i: a_copy(i).start())
    sent.append(lambda: loop(1, EMB, lambda i: a_copy(i).wait_send()))
    cols[e] = red[e]

    for k in range(3):
        tn_copy(k).wait_recv()
    tab_sum = tab[y, zr] + tab_near[0] + tab_near[1] + tab_near[2]
    tab[y, zr] = tab_sum

    def tf_copy(m):
        return send(
            tab.at[y, zr, lax.rem(zq + m, 4)], tab_far.at[m - 1], tf_s.at[m - 1], tf_r.at[m - 1], z_at(4 * m)
        )

    for m in range(1, 4):
        tf_copy(m).start()
        sent.append(lambda m=m: tf_copy(m).wait_send())
    for m in range(1, 4):
        tf_copy(m).wait_recv()
    tab_whole = tab[y, zr, zq] + tab_far[0] + tab_far[1] + tab_far[2]
    tab_code, tab_power = encode(tab_whole[:8])
    head_code, head_power = encode(tab_whole[8:])
    loop(1, EMB, lambda i: a_copy(i).wait_recv())
    coded, power = encode(cols[...].reshape(128, 128))
    spots = lax.broadcasted_iota(jnp.int32, (16, 128), 0)
    powers = jnp.where(spots < 8, power, jnp.where(spots < 12, tab_power, head_power))
    out[y, zr, zq, :128] = coded
    out[y, zr, zq, 128:144] = jnp.concatenate([tab_code.astype(jnp.int32), head_code.astype(jnp.int32)], axis=0).astype(I16)
    out[y, zr, zq, 144:] = powers.astype(jnp.int32).astype(I16)

    def block(off, m):
        src = lax.rem(z + 2 * ZED - off - 4 * m, ZED)
        return out.at[y, lax.rem(src, 4), src // 4]

    def of_copy(m):
        return send(block(0, 0), block(0, 0), of_s.at[m - 1], of_r.at[m - 1], z_at(4 * m))

    def of_wait(m):
        send(block(0, m), block(0, m), of_s.at[m - 1], of_r.at[m - 1], z_at(4 * m)).wait_recv()

    ways = (1, -1, 2)

    def on_copy(k, m):
        return send(block(0, m), block(0, m), on_s.at[k, m], on_r.at[k, m], z_at(ways[k]))

    def on_wait(k, m):
        got = block(ways[k], m)
        send(got, got, on_s.at[k, m], on_r.at[k, m], z_at(ways[k])).wait_recv()

    def oy_copy(k, m):
        got = block(0 if k == 0 else ways[k - 1], m)
        return send(got, got, oy_s.at[k, m], oy_r.at[k, m], y_mate)

    def oy_wait(k, m):
        src = lax.rem(z + 2 * ZED - (0 if k == 0 else ways[k - 1]) - 4 * m, ZED)
        got = out.at[other, lax.rem(src, 4), src // 4]
        send(got, got, oy_s.at[k, m], oy_r.at[k, m], y_mate).wait_recv()

    for m in range(1, 4):
        of_copy(m).start()
        sent.append(lambda m=m: of_copy(m).wait_send())
    for m in range(4):
        if m:
            of_wait(m)
        for k in range(3):
            on_copy(k, m).start()
            sent.append(lambda k=k, m=m: on_copy(k, m).wait_send())
        oy_copy(0, m).start()
        sent.append(lambda m=m: oy_copy(0, m).wait_send())
    for m in range(4):
        for k in range(3):
            on_wait(k, m)
            oy_copy(k + 1, m).start()
            sent.append(lambda k=k, m=m: oy_copy(k + 1, m).wait_send())
    for m in range(4):
        for k in range(4):
            oy_wait(k, m)
    for wait in sent:
        wait()


def train(codes, bag, book, w_in, w_out, labels):
    hbm = pl.BlockSpec(memory_space=pl.ANY)
    V, D = pltpu.VMEM, pltpu.SemaphoreType.DMA
    rows = codes.shape[1]
    scratch = [
        V((SUB, rows), jnp.int32),
        V((1, rows), jnp.int32),
        V((CENT, D_FIELD), BF16),
        V((32, 128), F32),
        V((1, SAMP), F32),
        V((D_FIELD, CENT), F32),
        V((SAMP, rows), F8),
        V((D_FIELD, SAMP), F32),
        V((SUB * CENT, SAMP), BF16),
        V((SUB * CENT, SAMP), BF16),
        V((EMB, D_FIELD, WIDE), BF16),
        V((WIDE, EMB * D_FIELD), BF16),
        V((EMB, D_FIELD, SAMP), BF16),
        V((16, EMB, 8, SAMP), F32),
        V((4, 512, SAMP), BF16),
        V((EMB, 8, SAMP), F32),
        V((EMB, 8, 128), F32),
        V((8, D_FIELD, SAMP), F32),
        V((8, D_FIELD, SAMP), F32),
        V((8, D_FIELD, SAMP), F32),
        V((8, D_FIELD + 16, SAMP), I16),
        V((8, D_FIELD + 16, SAMP), I16),
        V((4, 512, 128), BF16),
        V((4, 512, 128), BF16),
        V((4, 512, 128), F32),
        V((3, 528, 128), I16),
        V((3, 528, 128), I16),
        V((4, 128, 128), F32),
        V((3, 144, 128), I16),
        V((3, 144, 128), I16),
        V((EMB, 8, 128), F32),
        V((EMB, 8, 128), F32),
        V((2, 4, 4, 16, 128), F32),
        V((4, 4, 16, 128), F32),
        V((3, 4, 16, 128), F32),
        V((3, 16, 128), F32),
        D((6,)),
    ]
    sems = [(16,), (2, 8), (2, 8), (16,), (16,), (8,), (8,), (4,), (3,), (3,), (16,), (), (3,), (3,), (3,), (3, 4), (4, 4)]
    for shape in sems:
        scratch += [D(shape), D(shape)] if shape else [D, D]
    return pl.pallas_call(
        step_kernel,
        out_shape=jax.ShapeDtypeStruct((2, 4, 4, BLOCK, 128), I16),
        in_specs=[hbm] * 6,
        out_specs=pl.BlockSpec(memory_space=pltpu.VMEM),
        scratch_shapes=scratch,
        compiler_params=pltpu.CompilerParams(
            collective_id=1, has_side_effects=True, vmem_limit_bytes=56 << 20
        ),
        name="train_step",
    )(codes, bag, book, w_in, w_out, labels)


def spread_kernel(gathered, weight, table, head):
    a = pl.program_id(0)
    for c in range(4):
        for yy in range(2):
            whole = decode(gathered[yy, c, 0, :128], gathered[yy, c, 0, 144:])
            for f in range(EMB):
                spot = f * WIDE + yy * 128
                weight[c * 8 : c * 8 + 8, spot : spot + 128] = whole[f * 8 : f * 8 + 8]
            powers = number(gathered[yy, c, 0, 144:])
            tab = number(gathered[yy, c, 0, 128:144])
            gg = yy * ZED + a * 4 + c
            table[pl.ds(pl.multiple_of(gg * 8, 8), 8), :] = tab[:8] * jnp.exp2(powers[8:9] - 15.0)
            head[pl.ds(gg, 1), :] = tab[8:9] * jnp.exp2(powers[12:13] - 15.0)


def spread(gathered):
    return pl.pallas_call(
        spread_kernel,
        grid=(4,),
        out_shape=(
            jax.ShapeDtypeStruct((D_FIELD, HID), F32),
            jax.ShapeDtypeStruct((CENT, D_FIELD), F32),
            jax.ShapeDtypeStruct((DENSE, 128), F32),
        ),
        in_specs=[pl.BlockSpec((2, 4, 1, BLOCK, 128), lambda i: (0, 0, i, 0, 0))],
        out_specs=(
            pl.BlockSpec((32, HID), lambda i: (i, 0)),
            pl.BlockSpec((CENT, D_FIELD), lambda i: (0, 0)),
            pl.BlockSpec((DENSE, 128), lambda i: (0, 0)),
        ),
        name="spread",
    )(gathered)


def body(codes, row_bag, codebook, w_in, w_out, labels):
    gathered = train(
        codes[0].T, row_bag, codebook[0], w_in, w_out.reshape(32, 128), labels.reshape(1, SAMP)
    )
    weight, table, head = spread(gathered)
    return table[None], weight, head.reshape(HID)


def solution(mesh):
    in_specs = (
        P("emb", "dense", None),
        P("emb", "dense"),
        P("emb", None, None),
        P("emb", None),
        P(),
        P("dense"),
    )
    out_specs = (P("emb", None, None), P("emb", None), P())
    return jax.shard_map(body, mesh=mesh, in_specs=in_specs, out_specs=out_specs, check_vma=False)
```

```python
import functools

import jax
import jax.numpy as jnp
from jax import lax
from jax.experimental import pallas as pl
from jax.experimental.pallas import tpu as pltpu
from jax.sharding import PartitionSpec as P

D_FIELD = 128
SUB = 16
SUBW = 8
CENT = 256
EMB = 16
DENSE = 32
ZED = 16
SAMP = 256
WIDE = 256
HID = 4096
F32 = jnp.float32
BF16 = jnp.bfloat16
F8 = jnp.float8_e4m3fn
I16 = jnp.int16
NT = (((1,), (1,)), ((), ()))
MESH = pl.DeviceIdType.MESH
BLOCK = 144
GROUP = 4


def encode(value):
    top = jnp.maximum(jnp.max(jnp.abs(value), axis=0, keepdims=True), 1e-30)
    power = jnp.ceil(jnp.log2(top) + 0.001)
    coded = jnp.floor(value * jnp.exp2(15.0 - power) + 0.5)
    return coded.astype(jnp.int32).astype(I16), power


def tile_of(power):
    return jnp.broadcast_to(power, (16, power.shape[1])).astype(jnp.int32).astype(I16)


def number(coded):
    return coded.astype(jnp.int32).astype(F32)


def decode(coded, power):
    return number(coded) * jnp.exp2(number(power)[:1] - 15.0)


def step_kernel(
    codes_hbm, bag_hbm, book_hbm, w_in, w_out_hbm, labels_hbm, out,
    codes, bag, book, w_out, labels, table_t, members, pooled, low, high,
    w_cols, w_turned, fields, fields32, turned, logits, heads,
    gp_own, gp_sib, gp_got, gp_out, gp_in,
    y_out, y_in, mine, near_out, near_in, acc, far_out, far_in, red, cols,
    table, tab, tab_y, tab_near, tab_far,
    local, w_s, w_r, wu_s, wu_r, wd_s, wd_r, f_s, f_r, sib_s, sib_r, lg_s, lg_r, hd_s, hd_r, gs_s, gs_r, gp_s, gp_r,
    y_s, y_r, n_s, n_r, fr_s, fr_r, a_s, a_r,
    ty_s, ty_r, tn_s, tn_r, tf_s, tf_r, of_s, of_r, on_s, on_r, oy_s, oy_r,
):
    e = lax.axis_index("emb")
    g = lax.axis_index("dense")
    y = g // ZED
    z = lax.rem(g, ZED)
    zq = z // 4
    zr = lax.rem(z, 4)
    sib = e + 1 - 2 * lax.rem(e, 2)
    other = 1 - y

    def emb_at(i):
        return lax.rem(e + i, EMB)

    def emb_from(i):
        return lax.rem(e + EMB - i, EMB)

    def z_at(off):
        return (e, y * ZED + lax.rem(z + off + ZED, ZED))

    def send(src, dst, ss, rs, to):
        return pltpu.make_async_remote_copy(
            src_ref=src, dst_ref=dst, send_sem=ss, recv_sem=rs, device_id=to, device_id_type=MESH
        )

    def loop(lo, hi, body):
        def step(i, carry):
            body(i)
            return carry

        lax.fori_loop(lo, hi, step, 0)

    y_mate = (e, other * ZED + z)
    loads = [
        pltpu.make_async_copy(src, dst, local.at[1 + i])
        for i, (src, dst) in enumerate(
            ((bag_hbm, bag), (codes_hbm, codes), (book_hbm, book), (w_out_hbm, w_out), (labels_hbm, labels))
        )
    ]
    for load in loads:
        load.start()
    sent = []
    barrier = pltpu.get_barrier_semaphore()
    loop(1, EMB, lambda i: pl.semaphore_signal(barrier, inc=1, device_id=(emb_at(i), g), device_id_type=MESH))
    for off in (1, -1, 2, -2, 4, -4, 8):
        pl.semaphore_signal(barrier, inc=1, device_id=z_at(off), device_id_type=MESH)
    pl.semaphore_signal(barrier, inc=1, device_id=y_mate, device_id_type=MESH)

    half = lax.rem(z, 2)
    own_lanes = pl.ds(pl.multiple_of(half * 128, 128), 128)
    far_lanes = pl.ds(pl.multiple_of((1 - half) * 128, 128), 128)

    def w_copy(i):
        cols_of = pl.ds(pl.multiple_of(emb_at(i) * WIDE + half * 128, 128), 128)
        return send(w_in.at[:, cols_of], w_cols.at[e, :, own_lanes], w_s.at[i], w_r.at[i], (emb_at(i), g))

    def up_copy(i, lanes):
        part = w_cols.at[emb_from(i), pl.ds(0, 64), lanes]
        return send(part, part, wu_s.at[i], wu_r.at[i], z_at(1))

    def down_copy(i, lanes):
        part = w_cols.at[emb_from(i), pl.ds(64, 64), lanes]
        return send(part, part, wd_s.at[i], wd_r.at[i], z_at(-1))

    def pass_on(i):
        w_copy(i).wait_recv()
        up_copy(i, own_lanes).start()
        down_copy(i, own_lanes).start()

    def rows_of(f, h):
        return fields.at[f, pl.ds(h * 64, 64)]

    def f_copy(i, h):
        return send(rows_of(e, h), rows_of(e, h), f_s.at[h, i], f_r.at[h, i], (emb_at(2 * i), g))

    def sib_copy(i, h):
        f = lax.rem(e + 2 * EMB - 2 * i, EMB)
        return send(rows_of(f, h), rows_of(f, h), sib_s.at[h, i], sib_r.at[h, i], (sib, g))

    def onehot(row):
        ids = lax.broadcasted_iota(jnp.int32, (CENT, row.shape[1]), 0)
        return jnp.where(row == ids, 1.0, 0.0).astype(F8)

    for load in loads:
        load.wait()
    members[...] = onehot(bag[...])
    table_t[...] = book[...].astype(F32).T

    def count_step(step):
        at = step * GROUP
        picks = jnp.concatenate([onehot(codes[pl.ds(at + j, 1), :]) for j in range(GROUP)], axis=0)
        count = lax.dot_general(picks, members[...], NT, preferred_element_type=F32)
        upper = jnp.floor(count * (1.0 / 256.0))
        lower = (count - upper * 256.0).astype(BF16)
        upper = upper.astype(BF16)
        place = pl.ds(pl.multiple_of(at * CENT, CENT * GROUP), CENT * GROUP)
        low[place, :] = lower
        high[place, :] = upper
        rows = pl.ds(pl.multiple_of(at * SUBW, SUBW * GROUP), SUBW * GROUP)
        part = table_t[rows, :].astype(BF16)
        for j in range(GROUP):
            mine_at = slice(j * SUBW, (j + 1) * SUBW)
            span = slice(j * CENT, (j + 1) * CENT)
            pooled[pl.ds(pl.multiple_of((at + j) * SUBW, SUBW), SUBW), :] = jnp.dot(
                part[mine_at], lower[span], preferred_element_type=F32
            ) + 256.0 * jnp.dot(part[mine_at], upper[span], preferred_element_type=F32)

    def send_half(h):
        rows = pl.ds(h * 64, 64)
        fields[e, rows] = pooled[rows].astype(BF16)
        loop(1, 8, lambda i: f_copy(i, h).start())
        sib_copy(0, h).start()
        sent.append(lambda: loop(1, 8, lambda i: f_copy(i, h).wait_send()))
        sent.append(lambda: loop(0, 8, lambda i: sib_copy(i, h).wait_send()))

    loop(0, 1, count_step)
    pl.semaphore_wait(barrier, EMB - 1 + 8)
    loop(1, EMB, lambda i: w_copy(i).start())
    sent.append(lambda: loop(1, EMB, lambda i: w_copy(i).wait_send()))
    own_w = pltpu.make_async_copy(
        w_in.at[:, pl.ds(pl.multiple_of(e * WIDE, WIDE), WIDE)], w_cols.at[e], local.at[0]
    )
    own_w.start()

    def later_step(step):
        count_step(step)

        @pl.when(step == 1)
        def _():
            send_half(0)

    loop(1, 4, later_step)
    send_half(1)
    loop(1, EMB, pass_on)
    sent.append(lambda: loop(1, EMB, lambda i: up_copy(i, own_lanes).wait_send()))
    sent.append(lambda: loop(1, EMB, lambda i: down_copy(i, own_lanes).wait_send()))

    def forward(i, h):
        f_copy(i, h).wait_recv()
        sib_copy(i, h).start()

    for h in range(2):
        loop(1, 8, lambda i: forward(i, h))

    def turn(f):
        w_turned[:, pl.ds(pl.multiple_of(f * D_FIELD, D_FIELD), D_FIELD)] = w_cols[f].T

    def take(i):
        up_copy(i, far_lanes).wait_recv()
        down_copy(i, far_lanes).wait_recv()
        turn(emb_from(i))

    own_w.wait()
    turn(e)
    loop(1, EMB, take)
    for h in range(2):
        loop(0, 8, lambda i: sib_copy(i, h).wait_recv())
    pre = jnp.dot(w_turned[...], fields[...].reshape(EMB * D_FIELD, SAMP), preferred_element_type=F32)
    gate = jax.nn.sigmoid(pre)
    act = pre * gate
    w_row = jnp.concatenate([w_out[pl.ds(2 * e, 1), :], w_out[pl.ds(2 * e + 1, 1), :]], axis=1)
    w_rows = jnp.broadcast_to(w_row, (8, WIDE))
    logits[e] = jnp.dot(w_rows, act, precision=lax.Precision.HIGHEST, preferred_element_type=F32)

    def lg_copy(i):
        return send(logits.at[e], logits.at[e], lg_s.at[i], lg_r.at[i], (emb_at(i), g))

    loop(1, EMB, lambda i: lg_copy(i).start())
    sent.append(lambda: loop(1, EMB, lambda i: lg_copy(i).wait_send()))

    for f in range(EMB):
        fields32[:, f] = fields[f].astype(F32).reshape(16, 8, SAMP)
    for c in range(4):
        for a in range(4):
            turned[c, a * 128 : (a + 1) * 128] = fields32[a * 4 + c].reshape(128, SAMP).astype(BF16)
    slant = gate + pre * gate * (1.0 - gate)
    w_left = jnp.broadcast_to(w_row[:, :128], (128, 128)).T
    w_right = jnp.broadcast_to(w_row[:, 128:], (128, 128)).T
    w_tall = jnp.concatenate([w_left, w_right], axis=0)
    w_tall = jnp.concatenate([w_tall, w_tall], axis=1)

    loop(1, EMB, lambda i: lg_copy(i).wait_recv())
    logit = logits[0]
    for f in range(1, EMB):
        logit = logit + logits[f]
    slope = jax.nn.sigmoid(logit) - labels[...]
    grad = (slope[:1] * w_tall * slant).astype(BF16)
    halves = (grad[:128], grad[128:])

    head = lax.dot_general(slope, act, NT, precision=lax.Precision.HIGHEST, preferred_element_type=F32)
    heads[e] = jnp.concatenate([head[:1, :128], head[:1, 128:], jnp.zeros((6, 128), F32)], axis=0)

    def hd_copy(i):
        return send(heads.at[e], heads.at[e], hd_s.at[i], hd_r.at[i], (emb_at(i), g))

    loop(1, EMB, lambda i: hd_copy(i).start())
    sent.append(lambda: loop(1, EMB, lambda i: hd_copy(i).wait_send()))

    def grad_half(c, half):
        rhs = jnp.where(half == 0, halves[0], halves[1])
        return lax.dot_general(turned[c], rhs, NT, preferred_element_type=F32)

    def y_copy(k, c):
        return send(y_out.at[c], y_in.at[c], y_s.at[k], y_r.at[k], y_mate)

    near = (2, 1, -1)
    order = [lax.rem(z + off + 4, 4) for off in near] + [zr]
    for k, c in enumerate(order):
        coded, power = encode(grad_half(c, other))
        y_out[c, :512] = coded
        y_out[c, 512:] = tile_of(power)
        y_copy(k, c).start()
        sent.append(lambda k=k, c=c: y_copy(k, c).wait_send())
    core = lax.rem(e, 2)

    def gs_copy(i):
        return send(gp_sib.at[i], gp_got.at[i], gs_s.at[i], gs_r.at[i], (sib, g))

    def gs_start(i):
        gp_sib[i] = jnp.dot(w_cols[2 * i + 1 - core], grad, preferred_element_type=F32)
        gs_copy(i).start()

    loop(0, 8, gs_start)
    sent.append(lambda: loop(0, 8, lambda i: gs_copy(i).wait_send()))

    def gp_part(i):
        gp_own[i] = jnp.dot(w_cols[2 * i + core], grad, preferred_element_type=F32)

    loop(0, 8, gp_part)
    chip = e // 2

    def gp_copy(i):
        return send(
            gp_out.at[lax.rem(chip + i, 8)], gp_in.at[chip], gp_s.at[i], gp_r.at[i], (emb_at(2 * i), g)
        )

    def gp_start(i):
        c = lax.rem(chip + i, 8)
        gs_copy(c).wait_recv()
        coded, power = encode(gp_own[c] + gp_got[c])
        gp_out[c, :D_FIELD] = coded
        gp_out[c, D_FIELD:] = tile_of(power)
        gp_copy(i).start()

    loop(1, 8, gp_start)
    sent.append(lambda: loop(1, 8, lambda i: gp_copy(i).wait_send()))
    gs_copy(chip).wait_recv()
    for k, c in enumerate(order):
        mine[c] = grad_half(c, y)

    def near_copy(k):
        return send(near_out.at[k], near_in.at[k], n_s.at[k], n_r.at[k], z_at(near[k]))

    for k in range(3):
        c = order[k]
        y_copy(k, c).wait_recv()
        coded, power = encode(mine[c] + decode(y_in[c, :512], y_in[c, 512:]))
        near_out[k, :512] = coded
        near_out[k, 512:] = tile_of(power)
        near_copy(k).start()
        sent.append(lambda k=k: near_copy(k).wait_send())
    y_copy(3, zr).wait_recv()
    acc[...] = (mine[zr] + decode(y_in[zr, :512], y_in[zr, 512:])).reshape(4, 128, 128)

    loop(1, 8, lambda i: gp_copy(i).wait_recv())
    total = gp_own[chip] + gp_got[chip]
    for i in range(1, 8):
        c = lax.rem(chip + 8 - i, 8)
        total = total + decode(gp_in[c, :D_FIELD], gp_in[c, D_FIELD:])
    grad_pool = total.astype(BF16)
    subs = lax.broadcasted_iota(jnp.int32, (CENT, D_FIELD), 1) // SUBW
    table[...] = jnp.zeros((CENT, D_FIELD), F32)

    def table_step(step):
        place = pl.ds(pl.multiple_of(step * GROUP * CENT, GROUP * CENT), GROUP * CENT)
        got = lax.dot_general(low[place, :], grad_pool, NT, preferred_element_type=F32)
        got = got + 256.0 * lax.dot_general(high[place, :], grad_pool, NT, preferred_element_type=F32)
        for j in range(GROUP):
            part = got[j * CENT : (j + 1) * CENT]
            table[...] = table[...] + jnp.where(subs == step * GROUP + j, part, 0.0)

    loop(0, SUB // GROUP, table_step)
    loop(1, EMB, lambda i: hd_copy(i).wait_recv())
    for yy in range(2):
        for zz in range(ZED):
            gg = yy * ZED + zz
            tab[yy, zz % 4, zz // 4, :8] = table[gg * 8 : gg * 8 + 8]
            tab[yy, zz % 4, zz // 4, 8:] = jnp.concatenate(
                [heads[gg // 2, gg % 2 : gg % 2 + 1], jnp.zeros((7, 128), F32)], axis=0
            )
    ty_copy = send(tab.at[other], tab_y, ty_s, ty_r, y_mate)
    ty_copy.start()
    sent.append(lambda: ty_copy.wait_send())

    for k in range(3):
        near_copy(k).wait_recv()
        acc[...] = acc[...] + decode(near_in[k, :512], near_in[k, 512:]).reshape(4, 128, 128)

    def far_copy(m):
        return send(far_out.at[m - 1], far_in.at[m - 1], fr_s.at[m - 1], fr_r.at[m - 1], z_at(4 * m))

    for m in range(1, 4):
        coded, power = encode(acc[lax.rem(zq + m, 4)])
        far_out[m - 1, :128] = coded
        far_out[m - 1, 128:] = tile_of(power)
        far_copy(m).start()
        sent.append(lambda m=m: far_copy(m).wait_send())

    ty_copy.wait_recv()
    tab[y] = tab[y] + tab_y[...]

    def tn_copy(k):
        return send(tab.at[y, order[k]], tab_near.at[k], tn_s.at[k], tn_r.at[k], z_at(near[k]))

    for k in range(3):
        tn_copy(k).start()
        sent.append(lambda k=k: tn_copy(k).wait_send())

    whole = acc[zq]
    for m in range(1, 4):
        far_copy(m).wait_recv()
        whole = whole + decode(far_in[m - 1, :128], far_in[m - 1, 128:])
    red[...] = whole.reshape(EMB, 8, 128)

    def a_copy(i):
        return send(red.at[emb_at(i)], cols.at[e], a_s.at[i], a_r.at[i], (emb_at(i), g))

    loop(1, EMB, lambda i: a_copy(i).start())
    sent.append(lambda: loop(1, EMB, lambda i: a_copy(i).wait_send()))
    cols[e] = red[e]

    for k in range(3):
        tn_copy(k).wait_recv()
    tab_sum = tab[y, zr] + tab_near[0] + tab_near[1] + tab_near[2]
    tab[y, zr] = tab_sum

    def tf_copy(m):
        return send(
            tab.at[y, zr, lax.rem(zq + m, 4)], tab_far.at[m - 1], tf_s.at[m - 1], tf_r.at[m - 1], z_at(4 * m)
        )

    for m in range(1, 4):
        tf_copy(m).start()
        sent.append(lambda m=m: tf_copy(m).wait_send())
    for m in range(1, 4):
        tf_copy(m).wait_recv()
    tab_whole = tab[y, zr, zq] + tab_far[0] + tab_far[1] + tab_far[2]
    tab_code, tab_power = encode(tab_whole[:8])
    head_code, head_power = encode(tab_whole[8:])
    loop(1, EMB, lambda i: a_copy(i).wait_recv())
    coded, power = encode(cols[...].reshape(128, 128))
    spots = lax.broadcasted_iota(jnp.int32, (16, 128), 0)
    tail = jnp.concatenate([number(tab_code), number(head_code)], axis=0)
    for at, row in ((9, power), (10, tab_power), (11, head_power)):
        tail = jnp.where(spots == at, row, tail)
    out[y, zr, zq, :128] = coded
    out[y, zr, zq, 128:] = tail.astype(jnp.int32).astype(I16)
    def block(off, m):
        src = lax.rem(z + 2 * ZED - off - 4 * m, ZED)
        return out.at[y, lax.rem(src, 4), src // 4]

    def of_copy(m):
        return send(block(0, 0), block(0, 0), of_s.at[m - 1], of_r.at[m - 1], z_at(4 * m))

    def of_wait(m):
        send(block(0, m), block(0, m), of_s.at[m - 1], of_r.at[m - 1], z_at(4 * m)).wait_recv()

    ways = (1, -1, 2)

    def on_copy(k, m):
        return send(block(0, m), block(0, m), on_s.at[k, m], on_r.at[k, m], z_at(ways[k]))

    def on_wait(k, m):
        got = block(ways[k], m)
        send(got, got, on_s.at[k, m], on_r.at[k, m], z_at(ways[k])).wait_recv()

    def oy_copy(k, m):
        got = block(0 if k == 0 else ways[k - 1], m)
        return send(got, got, oy_s.at[k, m], oy_r.at[k, m], y_mate)

    def oy_wait(k, m):
        src = lax.rem(z + 2 * ZED - (0 if k == 0 else ways[k - 1]) - 4 * m, ZED)
        got = out.at[other, lax.rem(src, 4), src // 4]
        send(got, got, oy_s.at[k, m], oy_r.at[k, m], y_mate).wait_recv()

    for m in range(1, 4):
        of_copy(m).start()
        sent.append(lambda m=m: of_copy(m).wait_send())
    for m in range(4):
        if m:
            of_wait(m)
        for k in range(3):
            on_copy(k, m).start()
            sent.append(lambda k=k, m=m: on_copy(k, m).wait_send())
        oy_copy(0, m).start()
        sent.append(lambda m=m: oy_copy(0, m).wait_send())
    for m in range(4):
        for k in range(3):
            on_wait(k, m)
            oy_copy(k + 1, m).start()
            sent.append(lambda k=k, m=m: oy_copy(k + 1, m).wait_send())
    for m in range(4):
        for k in range(4):
            oy_wait(k, m)
    for wait in sent:
        wait()


def train(codes, bag, book, w_in, w_out, labels):
    hbm = pl.BlockSpec(memory_space=pl.ANY)
    V, D = pltpu.VMEM, pltpu.SemaphoreType.DMA
    rows = codes.shape[1]
    scratch = [
        V((SUB, rows), jnp.int32),
        V((1, rows), jnp.int32),
        V((CENT, D_FIELD), BF16),
        V((32, 128), F32),
        V((1, SAMP), F32),
        V((D_FIELD, CENT), F32),
        V((SAMP, rows), F8),
        V((D_FIELD, SAMP), F32),
        V((SUB * CENT, SAMP), BF16),
        V((SUB * CENT, SAMP), BF16),
        V((EMB, D_FIELD, WIDE), BF16),
        V((WIDE, EMB * D_FIELD), BF16),
        V((EMB, D_FIELD, SAMP), BF16),
        V((16, EMB, 8, SAMP), F32),
        V((4, 512, SAMP), BF16),
        V((EMB, 8, SAMP), F32),
        V((EMB, 8, 128), F32),
        V((8, D_FIELD, SAMP), F32),
        V((8, D_FIELD, SAMP), F32),
        V((8, D_FIELD, SAMP), F32),
        V((8, D_FIELD + 16, SAMP), I16),
        V((8, D_FIELD + 16, SAMP), I16),
        V((4, 528, 128), I16),
        V((4, 528, 128), I16),
        V((4, 512, 128), F32),
        V((3, 528, 128), I16),
        V((3, 528, 128), I16),
        V((4, 128, 128), F32),
        V((3, 144, 128), I16),
        V((3, 144, 128), I16),
        V((EMB, 8, 128), F32),
        V((EMB, 8, 128), F32),
        V((CENT, D_FIELD), F32),
        V((2, 4, 4, 16, 128), F32),
        V((4, 4, 16, 128), F32),
        V((3, 4, 16, 128), F32),
        V((3, 16, 128), F32),
        D((6,)),
    ]
    sems = [(16,), (16,), (16,), (2, 8), (2, 8), (16,), (16,), (8,), (8,), (4,), (3,), (3,), (16,), (), (3,), (3,), (3,), (3, 4), (4, 4)]
    for shape in sems:
        scratch += [D(shape), D(shape)] if shape else [D, D]
    return pl.pallas_call(
        step_kernel,
        out_shape=jax.ShapeDtypeStruct((2, 4, 4, BLOCK, 128), I16),
        in_specs=[hbm] * 6,
        out_specs=pl.BlockSpec(memory_space=pltpu.VMEM),
        scratch_shapes=scratch,
        compiler_params=pltpu.CompilerParams(
            collective_id=1, has_side_effects=True, vmem_limit_bytes=56 << 20
        ),
        name="train_step",
    )(codes, bag, book, w_in, w_out, labels)


def spread_kernel(gathered, weight, table, head):
    a = pl.program_id(0)
    for c in range(4):
        for yy in range(2):
            tail = number(gathered[yy, c, 0, 128:])
            scales = jnp.exp2(tail[8:] - 15.0)
            whole = number(gathered[yy, c, 0, :128]) * scales[1:2]
            for f in range(EMB):
                spot = f * WIDE + yy * 128
                weight[c * 8 : c * 8 + 8, spot : spot + 128] = whole[f * 8 : f * 8 + 8]
            gg = yy * ZED + a * 4 + c
            table[pl.ds(pl.multiple_of(gg * 8, 8), 8), :] = tail[:8] * scales[2:3]
            head[pl.ds(gg, 1), :] = tail[8:9] * scales[3:4]


def spread(gathered):
    return pl.pallas_call(
        spread_kernel,
        grid=(4,),
        out_shape=(
            jax.ShapeDtypeStruct((D_FIELD, HID), F32),
            jax.ShapeDtypeStruct((CENT, D_FIELD), F32),
            jax.ShapeDtypeStruct((DENSE, 128), F32),
        ),
        in_specs=[pl.BlockSpec((2, 4, 1, BLOCK, 128), lambda i: (0, 0, i, 0, 0))],
        out_specs=(
            pl.BlockSpec((32, HID), lambda i: (i, 0)),
            pl.BlockSpec((CENT, D_FIELD), lambda i: (0, 0)),
            pl.BlockSpec((DENSE, 128), lambda i: (0, 0)),
        ),
        name="spread",
    )(gathered)


def body(codes, row_bag, codebook, w_in, w_out, labels):
    gathered = train(
        codes[0].T, row_bag, codebook[0], w_in, w_out.reshape(32, 128), labels.reshape(1, SAMP)
    )
    weight, table, head = spread(gathered)
    return table[None], weight, head.reshape(HID)


def solution(mesh):
    in_specs = (
        P("emb", "dense", None),
        P("emb", "dense"),
        P("emb", None, None),
        P("emb", None),
        P(),
        P("dense"),
    )
    out_specs = (P("emb", None, None), P("emb", None), P())
    return jax.shard_map(body, mesh=mesh, in_specs=in_specs, out_specs=out_specs, check_vma=False)
```

```python
import functools

import jax
import jax.numpy as jnp
from jax import lax
from jax.experimental import pallas as pl
from jax.experimental.pallas import tpu as pltpu
from jax.sharding import PartitionSpec as P

D_FIELD = 128
SUB = 16
SUBW = 8
CENT = 256
EMB = 16
DENSE = 32
ZED = 16
SAMP = 256
WIDE = 256
HID = 4096
F32 = jnp.float32
BF16 = jnp.bfloat16
F8 = jnp.float8_e4m3fn
I16 = jnp.int16
NT = (((1,), (1,)), ((), ()))
MESH = pl.DeviceIdType.MESH
BLOCK = 144
GROUP = 4


def encode(value):
    top = jnp.maximum(jnp.max(jnp.abs(value), axis=0, keepdims=True), 1e-30)
    power = jnp.ceil(jnp.log2(top) + 0.001)
    coded = jnp.floor(value * jnp.exp2(15.0 - power) + 0.5)
    return coded.astype(jnp.int32).astype(I16), power


def tile_of(power):
    return jnp.broadcast_to(power, (16, power.shape[1])).astype(jnp.int32).astype(I16)


def number(coded):
    return coded.astype(jnp.int32).astype(F32)


def decode(coded, power):
    return number(coded) * jnp.exp2(number(power)[:1] - 15.0)


def step_kernel(
    codes_hbm, bag_hbm, book_hbm, w_in, w_out_hbm, labels_hbm, out,
    codes, bag, book, w_out, labels, table_t, members, pooled, low, high,
    w_cols, w_turned, fields, fields32, turned, logits, heads,
    gp_own, gp_sib, gp_got, gp_out, gp_in,
    y_out, y_in, mine, near_out, near_in, acc, far_out, far_in, red, cols,
    table, tab, tab_y, tab_near, tab_far, tabs,
    local, w_s, w_r, wu_s, wu_r, wd_s, wd_r, f_s, f_r, sib_s, sib_r, lg_s, lg_r, hd_s, hd_r, gs_s, gs_r, gp_s, gp_r,
    y_s, y_r, n_s, n_r, fr_s, fr_r, a_s, a_r,
    ty_s, ty_r, tn_s, tn_r, tf_s, tf_r, tg_s, tg_r, on_s, on_r, oy_s, oy_r,
):
    e = lax.axis_index("emb")
    g = lax.axis_index("dense")
    y = g // ZED
    z = lax.rem(g, ZED)
    zq = z // 4
    zr = lax.rem(z, 4)
    sib = e + 1 - 2 * lax.rem(e, 2)
    other = 1 - y

    def emb_at(i):
        return lax.rem(e + i, EMB)

    def emb_from(i):
        return lax.rem(e + EMB - i, EMB)

    def z_at(off):
        return (e, y * ZED + lax.rem(z + off + ZED, ZED))

    def send(src, dst, ss, rs, to):
        return pltpu.make_async_remote_copy(
            src_ref=src, dst_ref=dst, send_sem=ss, recv_sem=rs, device_id=to, device_id_type=MESH
        )

    def loop(lo, hi, body):
        def step(i, carry):
            body(i)
            return carry

        lax.fori_loop(lo, hi, step, 0)

    y_mate = (e, other * ZED + z)
    loads = [
        pltpu.make_async_copy(src, dst, local.at[1 + i])
        for i, (src, dst) in enumerate(
            ((bag_hbm, bag), (codes_hbm, codes), (book_hbm, book), (w_out_hbm, w_out), (labels_hbm, labels))
        )
    ]
    for load in loads:
        load.start()
    sent = []
    barrier = pltpu.get_barrier_semaphore()
    loop(1, EMB, lambda i: pl.semaphore_signal(barrier, inc=1, device_id=(emb_at(i), g), device_id_type=MESH))
    for off in (1, -1, 2, -2, 4, -4, 8):
        pl.semaphore_signal(barrier, inc=1, device_id=z_at(off), device_id_type=MESH)
    pl.semaphore_signal(barrier, inc=1, device_id=y_mate, device_id_type=MESH)

    half = lax.rem(z, 2)
    own_lanes = pl.ds(pl.multiple_of(half * 128, 128), 128)
    far_lanes = pl.ds(pl.multiple_of((1 - half) * 128, 128), 128)

    def w_copy(i):
        cols_of = pl.ds(pl.multiple_of(emb_at(i) * WIDE + half * 128, 128), 128)
        return send(w_in.at[:, cols_of], w_cols.at[e, :, own_lanes], w_s.at[i], w_r.at[i], (emb_at(i), g))

    def up_copy(i, lanes):
        part = w_cols.at[emb_from(i), pl.ds(0, 64), lanes]
        return send(part, part, wu_s.at[i], wu_r.at[i], z_at(1))

    def down_copy(i, lanes):
        part = w_cols.at[emb_from(i), pl.ds(64, 64), lanes]
        return send(part, part, wd_s.at[i], wd_r.at[i], z_at(-1))

    def pass_on(i):
        w_copy(i).wait_recv()
        up_copy(i, own_lanes).start()
        down_copy(i, own_lanes).start()

    def rows_of(f, h):
        return fields.at[f, pl.ds(h * 64, 64)]

    def f_copy(i, h):
        return send(rows_of(e, h), rows_of(e, h), f_s.at[h, i], f_r.at[h, i], (emb_at(2 * i), g))

    def sib_copy(i, h):
        f = lax.rem(e + 2 * EMB - 2 * i, EMB)
        return send(rows_of(f, h), rows_of(f, h), sib_s.at[h, i], sib_r.at[h, i], (sib, g))

    def onehot(row):
        ids = lax.broadcasted_iota(jnp.int32, (CENT, row.shape[1]), 0).astype(F32).astype(BF16)
        same = row.astype(F32).astype(BF16) == ids
        return jnp.where(same, jnp.ones((), BF16), jnp.zeros((), BF16)).astype(F8)

    for load in loads:
        load.wait()
    members[...] = onehot(bag[...])
    table_t[...] = book[...].astype(F32).T

    def count_step(step):
        at = step * GROUP
        picks = jnp.concatenate([onehot(codes[pl.ds(at + j, 1), :]) for j in range(GROUP)], axis=0)
        count = lax.dot_general(picks, members[...], NT, preferred_element_type=F32)
        upper = jnp.floor(count * (1.0 / 256.0))
        lower = (count - upper * 256.0).astype(BF16)
        upper = upper.astype(BF16)
        place = pl.ds(pl.multiple_of(at * CENT, CENT * GROUP), CENT * GROUP)
        low[place, :] = lower
        high[place, :] = upper
        rows = pl.ds(pl.multiple_of(at * SUBW, SUBW * GROUP), SUBW * GROUP)
        part = table_t[rows, :].astype(BF16)
        for j in range(GROUP):
            mine_at = slice(j * SUBW, (j + 1) * SUBW)
            span = slice(j * CENT, (j + 1) * CENT)
            pooled[pl.ds(pl.multiple_of((at + j) * SUBW, SUBW), SUBW), :] = jnp.dot(
                part[mine_at], lower[span], preferred_element_type=F32
            ) + 256.0 * jnp.dot(part[mine_at], upper[span], preferred_element_type=F32)

    def send_half(h):
        rows = pl.ds(h * 64, 64)
        fields[e, rows] = pooled[rows].astype(BF16)
        loop(1, 8, lambda i: f_copy(i, h).start())
        sib_copy(0, h).start()
        sent.append(lambda: loop(1, 8, lambda i: f_copy(i, h).wait_send()))
        sent.append(lambda: loop(0, 8, lambda i: sib_copy(i, h).wait_send()))

    loop(0, 1, count_step)
    pl.semaphore_wait(barrier, EMB - 1 + 8)
    loop(1, EMB, lambda i: w_copy(i).start())
    sent.append(lambda: loop(1, EMB, lambda i: w_copy(i).wait_send()))
    own_w = pltpu.make_async_copy(
        w_in.at[:, pl.ds(pl.multiple_of(e * WIDE, WIDE), WIDE)], w_cols.at[e], local.at[0]
    )
    own_w.start()

    def later_step(step):
        count_step(step)

        @pl.when(step == 1)
        def _():
            send_half(0)

    loop(1, 4, later_step)
    send_half(1)
    loop(1, EMB, pass_on)
    sent.append(lambda: loop(1, EMB, lambda i: up_copy(i, own_lanes).wait_send()))
    sent.append(lambda: loop(1, EMB, lambda i: down_copy(i, own_lanes).wait_send()))

    def forward(i, h):
        f_copy(i, h).wait_recv()
        sib_copy(i, h).start()

    for h in range(2):
        loop(1, 8, lambda i: forward(i, h))

    def turn(f):
        w_turned[:, pl.ds(pl.multiple_of(f * D_FIELD, D_FIELD), D_FIELD)] = w_cols[f].T

    def take(i):
        up_copy(i, far_lanes).wait_recv()
        down_copy(i, far_lanes).wait_recv()
        turn(emb_from(i))

    own_w.wait()
    turn(e)
    loop(1, EMB, take)
    for h in range(2):
        loop(0, 8, lambda i: sib_copy(i, h).wait_recv())
    pre = jnp.dot(w_turned[...], fields[...].reshape(EMB * D_FIELD, SAMP), preferred_element_type=F32)
    gate = jax.nn.sigmoid(pre)
    act = pre * gate
    w_row = jnp.concatenate([w_out[pl.ds(2 * e, 1), :], w_out[pl.ds(2 * e + 1, 1), :]], axis=1)
    w_rows = jnp.broadcast_to(w_row, (8, WIDE))
    logits[e] = jnp.dot(w_rows, act, precision=lax.Precision.HIGHEST, preferred_element_type=F32)

    def lg_copy(i):
        return send(logits.at[e], logits.at[e], lg_s.at[i], lg_r.at[i], (emb_at(i), g))

    loop(1, EMB, lambda i: lg_copy(i).start())
    sent.append(lambda: loop(1, EMB, lambda i: lg_copy(i).wait_send()))

    for f in range(EMB):
        fields32[:, f] = fields[f].astype(F32).reshape(16, 8, SAMP)
    for c in range(4):
        for a in range(4):
            turned[c, a * 128 : (a + 1) * 128] = fields32[a * 4 + c].reshape(128, SAMP).astype(BF16)
    slant = gate + pre * gate * (1.0 - gate)
    w_left = jnp.broadcast_to(w_row[:, :128], (128, 128)).T
    w_right = jnp.broadcast_to(w_row[:, 128:], (128, 128)).T
    w_tall = jnp.concatenate([w_left, w_right], axis=0)
    w_tall = jnp.concatenate([w_tall, w_tall], axis=1)

    loop(1, EMB, lambda i: lg_copy(i).wait_recv())
    logit = logits[0]
    for f in range(1, EMB):
        logit = logit + logits[f]
    slope = jax.nn.sigmoid(logit) - labels[...]
    grad = (slope[:1] * w_tall * slant).astype(BF16)
    halves = (grad[:128], grad[128:])

    def grad_half(c, half):
        rhs = jnp.where(half == 0, halves[0], halves[1])
        return lax.dot_general(turned[c], rhs, NT, preferred_element_type=F32)

    def y_copy(k, c):
        return send(y_out.at[c], y_in.at[c], y_s.at[k], y_r.at[k], y_mate)

    near = (2, 1, -1)
    order = [lax.rem(z + off + 4, 4) for off in near] + [zr]
    for k, c in enumerate(order):
        coded, power = encode(grad_half(c, other))
        y_out[c, :512] = coded
        y_out[c, 512:] = tile_of(power)
        y_copy(k, c).start()
        sent.append(lambda k=k, c=c: y_copy(k, c).wait_send())
    head = lax.dot_general(slope, act, NT, precision=lax.Precision.HIGHEST, preferred_element_type=F32)
    heads[e] = jnp.concatenate([head[:1, :128], head[:1, 128:], jnp.zeros((6, 128), F32)], axis=0)

    def hd_copy(i):
        return send(heads.at[e], heads.at[e], hd_s.at[i], hd_r.at[i], (emb_at(i), g))

    loop(1, EMB, lambda i: hd_copy(i).start())
    sent.append(lambda: loop(1, EMB, lambda i: hd_copy(i).wait_send()))

    core = lax.rem(e, 2)

    def gs_copy(i):
        return send(gp_sib.at[i], gp_got.at[i], gs_s.at[i], gs_r.at[i], (sib, g))

    def gs_start(i):
        gp_sib[i] = jnp.dot(w_cols[2 * i + 1 - core], grad, preferred_element_type=F32)
        gs_copy(i).start()

    loop(0, 8, gs_start)
    sent.append(lambda: loop(0, 8, lambda i: gs_copy(i).wait_send()))

    def gp_part(i):
        gp_own[i] = jnp.dot(w_cols[2 * i + core], grad, preferred_element_type=F32)

    loop(0, 8, gp_part)
    chip = e // 2

    def gp_copy(i):
        return send(
            gp_out.at[lax.rem(chip + i, 8)], gp_in.at[chip], gp_s.at[i], gp_r.at[i], (emb_at(2 * i), g)
        )

    def gp_start(i):
        c = lax.rem(chip + i, 8)
        gs_copy(c).wait_recv()
        coded, power = encode(gp_own[c] + gp_got[c])
        gp_out[c, :D_FIELD] = coded
        gp_out[c, D_FIELD:] = tile_of(power)
        gp_copy(i).start()

    loop(1, 8, gp_start)
    sent.append(lambda: loop(1, 8, lambda i: gp_copy(i).wait_send()))
    gs_copy(chip).wait_recv()
    for k, c in enumerate(order):
        mine[c] = grad_half(c, y)

    def near_copy(k):
        return send(near_out.at[k], near_in.at[k], n_s.at[k], n_r.at[k], z_at(near[k]))

    for k in range(3):
        c = order[k]
        y_copy(k, c).wait_recv()
        coded, power = encode(mine[c] + decode(y_in[c, :512], y_in[c, 512:]))
        near_out[k, :512] = coded
        near_out[k, 512:] = tile_of(power)
        near_copy(k).start()
        sent.append(lambda k=k: near_copy(k).wait_send())
    y_copy(3, zr).wait_recv()
    acc[...] = (mine[zr] + decode(y_in[zr, :512], y_in[zr, 512:])).reshape(4, 128, 128)

    loop(1, 8, lambda i: gp_copy(i).wait_recv())
    total = gp_own[chip] + gp_got[chip]
    for i in range(1, 8):
        c = lax.rem(chip + 8 - i, 8)
        total = total + decode(gp_in[c, :D_FIELD], gp_in[c, D_FIELD:])
    grad_pool = total.astype(BF16)
    subs = lax.broadcasted_iota(jnp.int32, (CENT, D_FIELD), 1) // SUBW
    table[...] = jnp.zeros((CENT, D_FIELD), F32)

    def table_step(step):
        place = pl.ds(pl.multiple_of(step * GROUP * CENT, GROUP * CENT), GROUP * CENT)
        got = lax.dot_general(low[place, :], grad_pool, NT, preferred_element_type=F32)
        got = got + 256.0 * lax.dot_general(high[place, :], grad_pool, NT, preferred_element_type=F32)
        for j in range(GROUP):
            part = got[j * CENT : (j + 1) * CENT]
            table[...] = table[...] + jnp.where(subs == step * GROUP + j, part, 0.0)

    loop(0, SUB // GROUP, table_step)
    loop(1, EMB, lambda i: hd_copy(i).wait_recv())
    for yy in range(2):
        for zz in range(ZED):
            gg = yy * ZED + zz
            tab[yy, zz % 4, zz // 4, :8] = table[gg * 8 : gg * 8 + 8]
            tab[yy, zz % 4, zz // 4, 8:] = jnp.concatenate(
                [heads[gg // 2, gg % 2 : gg % 2 + 1], jnp.zeros((7, 128), F32)], axis=0
            )
    ty_copy = send(tab.at[other], tab_y, ty_s, ty_r, y_mate)
    ty_copy.start()
    sent.append(lambda: ty_copy.wait_send())

    for k in range(3):
        near_copy(k).wait_recv()
        acc[...] = acc[...] + decode(near_in[k, :512], near_in[k, 512:]).reshape(4, 128, 128)

    def far_copy(m):
        return send(far_out.at[m - 1], far_in.at[m - 1], fr_s.at[m - 1], fr_r.at[m - 1], z_at(4 * m))

    for m in range(1, 4):
        coded, power = encode(acc[lax.rem(zq + m, 4)])
        far_out[m - 1, :128] = coded
        far_out[m - 1, 128:] = tile_of(power)
        far_copy(m).start()
        sent.append(lambda m=m: far_copy(m).wait_send())

    ty_copy.wait_recv()
    tab[y] = tab[y] + tab_y[...]

    def tn_copy(k):
        return send(tab.at[y, order[k]], tab_near.at[k], tn_s.at[k], tn_r.at[k], z_at(near[k]))

    for k in range(3):
        tn_copy(k).start()
        sent.append(lambda k=k: tn_copy(k).wait_send())

    for k in range(3):
        tn_copy(k).wait_recv()
    tab_sum = tab[y, zr] + tab_near[0] + tab_near[1] + tab_near[2]
    tab[y, zr] = tab_sum

    def tf_copy(m):
        return send(
            tab.at[y, zr, lax.rem(zq + m, 4)], tab_far.at[m - 1], tf_s.at[m - 1], tf_r.at[m - 1], z_at(4 * m)
        )

    for m in range(1, 4):
        tf_copy(m).start()
        sent.append(lambda m=m: tf_copy(m).wait_send())
    whole = acc[zq]
    for m in range(1, 4):
        far_copy(m).wait_recv()
        whole = whole + decode(far_in[m - 1, :128], far_in[m - 1, 128:])
    red[...] = whole.reshape(EMB, 8, 128)

    def a_copy(m, i):
        to = (emb_at(i), y * ZED + lax.rem(z + 4 * m, ZED))
        return send(red.at[emb_at(i)], cols.at[m, e], a_s.at[m, i], a_r.at[m, i], to)

    for m in (2, 1, 3, 0):
        first = 1 if m == 0 else 0
        loop(first, EMB, lambda i: a_copy(m, i).start())
        sent.append(lambda m=m, first=first: loop(first, EMB, lambda i: a_copy(m, i).wait_send()))
    cols[0, e] = red[e]

    for m in range(1, 4):
        tf_copy(m).wait_recv()
    tabs[0] = tab[y, zr, zq] + tab_far[0] + tab_far[1] + tab_far[2]

    def tg_copy(m):
        return send(tabs.at[0], tabs.at[m], tg_s.at[m - 1], tg_r.at[m - 1], z_at(4 * m))

    for m in range(1, 4):
        tg_copy(m).start()
        sent.append(lambda m=m: tg_copy(m).wait_send())

    def block(off, m):
        src = lax.rem(z + 2 * ZED - off - 4 * m, ZED)
        return out.at[y, lax.rem(src, 4), src // 4]

    def pack(m):
        tab_code, tab_power = encode(tabs[m, :8])
        head_code, head_power = encode(tabs[m, 8:])
        coded, power = encode(cols[m].reshape(128, 128))
        spots = lax.broadcasted_iota(jnp.int32, (16, 128), 0)
        tail = jnp.concatenate([number(tab_code), number(head_code)], axis=0)
        for at, row in ((9, power), (10, tab_power), (11, head_power)):
            tail = jnp.where(spots == at, row, tail)
        here = block(0, m)
        here[:128] = coded
        here[128:] = tail.astype(jnp.int32).astype(I16)

    ways = (1, -1, 2)

    def on_copy(k, m):
        got = block(1 if k == 2 else 0, m)
        return send(got, got, on_s.at[k, m], on_r.at[k, m], z_at(-1 if k == 1 else 1))

    def on_wait(k, m):
        got = block(ways[k], m)
        send(got, got, on_s.at[k, m], on_r.at[k, m], z_at(1)).wait_recv()

    def oy_copy(k, m):
        got = block(0 if k == 0 else ways[k - 1], m)
        return send(got, got, oy_s.at[k, m], oy_r.at[k, m], y_mate)

    def oy_wait(k, m):
        src = lax.rem(z + 2 * ZED - (0 if k == 0 else ways[k - 1]) - 4 * m, ZED)
        got = out.at[other, lax.rem(src, 4), src // 4]
        send(got, got, oy_s.at[k, m], oy_r.at[k, m], y_mate).wait_recv()

    def put(copy):
        copy.start()
        sent.append(copy.wait_send)

    turns = (0, 1, 3, 2)
    for m in turns:
        loop(1 if m == 0 else 0, EMB, lambda i: a_copy(m, i).wait_recv())
        if m:
            tg_copy(m).wait_recv()
        pack(m)
        put(on_copy(0, m))
        put(on_copy(1, m))
        put(oy_copy(0, m))
    for m in turns:
        on_wait(0, m)
        put(on_copy(2, m))
        put(oy_copy(1, m))
        on_wait(1, m)
        put(oy_copy(2, m))
    for m in turns:
        on_wait(2, m)
        put(oy_copy(3, m))
    for m in range(4):
        for k in range(4):
            oy_wait(k, m)
    for wait in sent:
        wait()


def train(codes, bag, book, w_in, w_out, labels):
    hbm = pl.BlockSpec(memory_space=pl.ANY)
    V, D = pltpu.VMEM, pltpu.SemaphoreType.DMA
    rows = codes.shape[1]
    scratch = [
        V((SUB, rows), jnp.int32),
        V((1, rows), jnp.int32),
        V((CENT, D_FIELD), BF16),
        V((32, 128), F32),
        V((1, SAMP), F32),
        V((D_FIELD, CENT), F32),
        V((SAMP, rows), F8),
        V((D_FIELD, SAMP), F32),
        V((SUB * CENT, SAMP), BF16),
        V((SUB * CENT, SAMP), BF16),
        V((EMB, D_FIELD, WIDE), BF16),
        V((WIDE, EMB * D_FIELD), BF16),
        V((EMB, D_FIELD, SAMP), BF16),
        V((16, EMB, 8, SAMP), F32),
        V((4, 512, SAMP), BF16),
        V((EMB, 8, SAMP), F32),
        V((EMB, 8, 128), F32),
        V((8, D_FIELD, SAMP), F32),
        V((8, D_FIELD, SAMP), F32),
        V((8, D_FIELD, SAMP), F32),
        V((8, D_FIELD + 16, SAMP), I16),
        V((8, D_FIELD + 16, SAMP), I16),
        V((4, 528, 128), I16),
        V((4, 528, 128), I16),
        V((4, 512, 128), F32),
        V((3, 528, 128), I16),
        V((3, 528, 128), I16),
        V((4, 128, 128), F32),
        V((3, 144, 128), I16),
        V((3, 144, 128), I16),
        V((EMB, 8, 128), F32),
        V((4, EMB, 8, 128), F32),
        V((CENT, D_FIELD), F32),
        V((2, 4, 4, 16, 128), F32),
        V((4, 4, 16, 128), F32),
        V((3, 4, 16, 128), F32),
        V((3, 16, 128), F32),
        V((4, 16, 128), F32),
        D((6,)),
    ]
    sems = [(16,), (16,), (16,), (2, 8), (2, 8), (16,), (16,), (8,), (8,), (4,), (3,), (3,), (4, 16), (), (3,), (3,), (3,), (3, 4), (4, 4)]
    for shape in sems:
        scratch += [D(shape), D(shape)] if shape else [D, D]
    return pl.pallas_call(
        step_kernel,
        out_shape=jax.ShapeDtypeStruct((2, 4, 4, BLOCK, 128), I16),
        in_specs=[hbm] * 6,
        out_specs=pl.BlockSpec(memory_space=pltpu.VMEM),
        scratch_shapes=scratch,
        compiler_params=pltpu.CompilerParams(
            collective_id=1, has_side_effects=True, vmem_limit_bytes=56 << 20
        ),
        name="train_step",
    )(codes, bag, book, w_in, w_out, labels)


def spread_kernel(gathered, weight, table, head):
    a = pl.program_id(0)
    for c in range(4):
        for yy in range(2):
            tail = number(gathered[yy, c, 0, 128:])
            scales = jnp.exp2(tail[8:] - 15.0)
            whole = number(gathered[yy, c, 0, :128]) * scales[1:2]
            for f in range(EMB):
                spot = f * WIDE + yy * 128
                weight[c * 8 : c * 8 + 8, spot : spot + 128] = whole[f * 8 : f * 8 + 8]
            gg = yy * ZED + a * 4 + c
            table[pl.ds(pl.multiple_of(gg * 8, 8), 8), :] = tail[:8] * scales[2:3]
            head[pl.ds(gg, 1), :] = tail[8:9] * scales[3:4]


def spread(gathered):
    return pl.pallas_call(
        spread_kernel,
        grid=(4,),
        out_shape=(
            jax.ShapeDtypeStruct((D_FIELD, HID), F32),
            jax.ShapeDtypeStruct((CENT, D_FIELD), F32),
            jax.ShapeDtypeStruct((DENSE, 128), F32),
        ),
        in_specs=[pl.BlockSpec((2, 4, 1, BLOCK, 128), lambda i: (0, 0, i, 0, 0))],
        out_specs=(
            pl.BlockSpec((32, HID), lambda i: (i, 0)),
            pl.BlockSpec((CENT, D_FIELD), lambda i: (0, 0)),
            pl.BlockSpec((DENSE, 128), lambda i: (0, 0)),
        ),
        name="spread",
    )(gathered)


def body(codes, row_bag, codebook, w_in, w_out, labels):
    gathered = train(
        codes[0].T, row_bag, codebook[0], w_in, w_out.reshape(32, 128), labels.reshape(1, SAMP)
    )
    weight, table, head = spread(gathered)
    return table[None], weight, head.reshape(HID)


def solution(mesh):
    in_specs = (
        P("emb", "dense", None),
        P("emb", "dense"),
        P("emb", None, None),
        P("emb", None),
        P(),
        P("dense"),
    )
    out_specs = (P("emb", None, None), P("emb", None), P())
    return jax.shard_map(body, mesh=mesh, in_specs=in_specs, out_specs=out_specs, check_vma=False)
```

```python
import functools

import jax
import jax.numpy as jnp
from jax import lax
from jax.experimental import pallas as pl
from jax.experimental.pallas import tpu as pltpu
from jax.sharding import PartitionSpec as P

D_FIELD = 128
SUB = 16
SUBW = 8
CENT = 256
EMB = 16
DENSE = 32
ZED = 16
SAMP = 256
WIDE = 256
HID = 4096
F32 = jnp.float32
BF16 = jnp.bfloat16
F8 = jnp.float8_e4m3fn
I16 = jnp.int16
NT = (((1,), (1,)), ((), ()))
MESH = pl.DeviceIdType.MESH
BLOCK = 144
GROUP = 4


def encode(value):
    top = jnp.maximum(jnp.max(jnp.abs(value), axis=0, keepdims=True), 1e-30)
    power = jnp.ceil(jnp.log2(top) + 0.001)
    coded = jnp.floor(value * jnp.exp2(15.0 - power) + 0.5)
    return coded.astype(jnp.int32).astype(I16), power


def tile_of(power):
    return jnp.broadcast_to(power, (16, power.shape[1])).astype(jnp.int32).astype(I16)


def number(coded):
    return coded.astype(jnp.int32).astype(F32)


def decode(coded, power):
    return number(coded) * jnp.exp2(number(power)[:1] - 15.0)


def step_kernel(
    codes_hbm, bag_hbm, book_hbm, w_in, w_out_hbm, labels_hbm, out,
    codes, bag, book, w_out, labels, table_t, members, pooled, low, high,
    w_cols, w_turned, fields, fields32, turned, logits, heads,
    gp_own, gp_sib, gp_got, gp_out, gp_in, gq_out, gq_in, gp_sum,
    y_out, y_in, mine, near_out, near_in, acc, far_out, far_in, red, cols,
    table, tab, tab_y, tab_near, tab_far,
    local, w_s, w_r, wu_s, wu_r, wd_s, wd_r, f_s, f_r, sib_s, sib_r, lg_s, lg_r, hd_s, hd_r, gs_s, gs_r, gp_s, gp_r, gq_s, gq_r,
    y_s, y_r, n_s, n_r, fr_s, fr_r, a_s, a_r,
    ty_s, ty_r, tn_s, tn_r, tf_s, tf_r, of_s, of_r, on_s, on_r, oy_s, oy_r,
):
    e = lax.axis_index("emb")
    g = lax.axis_index("dense")
    y = g // ZED
    z = lax.rem(g, ZED)
    zq = z // 4
    zr = lax.rem(z, 4)
    sib = e + 1 - 2 * lax.rem(e, 2)
    other = 1 - y

    def emb_at(i):
        return lax.rem(e + i, EMB)

    def emb_from(i):
        return lax.rem(e + EMB - i, EMB)

    def z_at(off):
        return (e, y * ZED + lax.rem(z + off + ZED, ZED))

    def send(src, dst, ss, rs, to):
        return pltpu.make_async_remote_copy(
            src_ref=src, dst_ref=dst, send_sem=ss, recv_sem=rs, device_id=to, device_id_type=MESH
        )

    def loop(lo, hi, body):
        def step(i, carry):
            body(i)
            return carry

        lax.fori_loop(lo, hi, step, 0)

    y_mate = (e, other * ZED + z)
    loads = [
        pltpu.make_async_copy(src, dst, local.at[1 + i])
        for i, (src, dst) in enumerate(
            ((bag_hbm, bag), (codes_hbm, codes), (book_hbm, book), (w_out_hbm, w_out), (labels_hbm, labels))
        )
    ]
    for load in loads:
        load.start()
    sent = []
    barrier = pltpu.get_barrier_semaphore()
    loop(1, EMB, lambda i: pl.semaphore_signal(barrier, inc=1, device_id=(emb_at(i), g), device_id_type=MESH))
    for off in (1, -1, 2, -2, 4, -4, 8):
        pl.semaphore_signal(barrier, inc=1, device_id=z_at(off), device_id_type=MESH)
    pl.semaphore_signal(barrier, inc=1, device_id=y_mate, device_id_type=MESH)

    half = lax.rem(z, 2)
    own_lanes = pl.ds(pl.multiple_of(half * 128, 128), 128)
    far_lanes = pl.ds(pl.multiple_of((1 - half) * 128, 128), 128)

    def w_copy(i):
        cols_of = pl.ds(pl.multiple_of(emb_at(i) * WIDE + half * 128, 128), 128)
        return send(w_in.at[:, cols_of], w_cols.at[e, :, own_lanes], w_s.at[i], w_r.at[i], (emb_at(i), g))

    def up_copy(i, lanes):
        part = w_cols.at[emb_from(i), pl.ds(0, 64), lanes]
        return send(part, part, wu_s.at[i], wu_r.at[i], z_at(1))

    def down_copy(i, lanes):
        part = w_cols.at[emb_from(i), pl.ds(64, 64), lanes]
        return send(part, part, wd_s.at[i], wd_r.at[i], z_at(-1))

    def pass_on(i):
        w_copy(i).wait_recv()
        up_copy(i, own_lanes).start()
        down_copy(i, own_lanes).start()

    def rows_of(f, h):
        return fields.at[f, pl.ds(h * 64, 64)]

    def f_copy(i, h):
        return send(rows_of(e, h), rows_of(e, h), f_s.at[h, i], f_r.at[h, i], (emb_at(2 * i), g))

    def sib_copy(i, h):
        f = lax.rem(e + 2 * EMB - 2 * i, EMB)
        return send(rows_of(f, h), rows_of(f, h), sib_s.at[h, i], sib_r.at[h, i], (sib, g))

    def onehot(row):
        ids = lax.broadcasted_iota(jnp.int32, (CENT, row.shape[1]), 0).astype(F32).astype(BF16)
        same = row.astype(F32).astype(BF16) == ids
        return jnp.where(same, jnp.ones((), BF16), jnp.zeros((), BF16)).astype(F8)

    for load in loads:
        load.wait()
    members[...] = onehot(bag[...])
    table_t[...] = book[...].astype(F32).T

    def count_step(step):
        at = step * GROUP
        picks = jnp.concatenate([onehot(codes[pl.ds(at + j, 1), :]) for j in range(GROUP)], axis=0)
        count = lax.dot_general(picks, members[...], NT, preferred_element_type=F32)
        upper = jnp.floor(count * (1.0 / 256.0))
        lower = (count - upper * 256.0).astype(BF16)
        upper = upper.astype(BF16)
        place = pl.ds(pl.multiple_of(at * CENT, CENT * GROUP), CENT * GROUP)
        low[place, :] = lower
        high[place, :] = upper
        rows = pl.ds(pl.multiple_of(at * SUBW, SUBW * GROUP), SUBW * GROUP)
        part = table_t[rows, :].astype(BF16)
        for j in range(GROUP):
            mine_at = slice(j * SUBW, (j + 1) * SUBW)
            span = slice(j * CENT, (j + 1) * CENT)
            pooled[pl.ds(pl.multiple_of((at + j) * SUBW, SUBW), SUBW), :] = jnp.dot(
                part[mine_at], lower[span], preferred_element_type=F32
            ) + 256.0 * jnp.dot(part[mine_at], upper[span], preferred_element_type=F32)

    def send_half(h):
        rows = pl.ds(h * 64, 64)
        fields[e, rows] = pooled[rows].astype(BF16)
        loop(1, 8, lambda i: f_copy(i, h).start())
        sib_copy(0, h).start()
        sent.append(lambda: loop(1, 8, lambda i: f_copy(i, h).wait_send()))
        sent.append(lambda: loop(0, 8, lambda i: sib_copy(i, h).wait_send()))

    loop(0, 1, count_step)
    pl.semaphore_wait(barrier, EMB - 1 + 8)
    loop(1, EMB, lambda i: w_copy(i).start())
    sent.append(lambda: loop(1, EMB, lambda i: w_copy(i).wait_send()))
    own_w = pltpu.make_async_copy(
        w_in.at[:, pl.ds(pl.multiple_of(e * WIDE, WIDE), WIDE)], w_cols.at[e], local.at[0]
    )
    own_w.start()

    def later_step(step):
        count_step(step)

        @pl.when(step == 1)
        def _():
            send_half(0)

    loop(1, 4, later_step)
    send_half(1)
    loop(1, EMB, pass_on)
    sent.append(lambda: loop(1, EMB, lambda i: up_copy(i, own_lanes).wait_send()))
    sent.append(lambda: loop(1, EMB, lambda i: down_copy(i, own_lanes).wait_send()))

    def forward(i, h):
        f_copy(i, h).wait_recv()
        sib_copy(i, h).start()

    for h in range(2):
        loop(1, 8, lambda i: forward(i, h))

    def turn(f):
        w_turned[:, pl.ds(pl.multiple_of(f * D_FIELD, D_FIELD), D_FIELD)] = w_cols[f].T

    def take(i):
        up_copy(i, far_lanes).wait_recv()
        down_copy(i, far_lanes).wait_recv()
        turn(emb_from(i))

    own_w.wait()
    turn(e)
    loop(1, EMB, take)
    for h in range(2):
        loop(0, 8, lambda i: sib_copy(i, h).wait_recv())
    pre = jnp.dot(w_turned[...], fields[...].reshape(EMB * D_FIELD, SAMP), preferred_element_type=F32)
    gate = jax.nn.sigmoid(pre)
    act = pre * gate
    w_row = jnp.concatenate([w_out[pl.ds(2 * e, 1), :], w_out[pl.ds(2 * e + 1, 1), :]], axis=1)
    w_rows = jnp.broadcast_to(w_row, (8, WIDE))
    logits[e] = jnp.dot(w_rows, act, precision=lax.Precision.HIGHEST, preferred_element_type=F32)

    def lg_copy(i):
        return send(logits.at[e], logits.at[e], lg_s.at[i], lg_r.at[i], (emb_at(i), g))

    loop(1, EMB, lambda i: lg_copy(i).start())
    sent.append(lambda: loop(1, EMB, lambda i: lg_copy(i).wait_send()))

    for f in range(EMB):
        fields32[:, f] = fields[f].astype(F32).reshape(16, 8, SAMP)
    for c in range(4):
        for a in range(4):
            turned[c, a * 128 : (a + 1) * 128] = fields32[a * 4 + c].reshape(128, SAMP).astype(BF16)
    slant = gate + pre * gate * (1.0 - gate)
    w_left = jnp.broadcast_to(w_row[:, :128], (128, 128)).T
    w_right = jnp.broadcast_to(w_row[:, 128:], (128, 128)).T
    w_tall = jnp.concatenate([w_left, w_right], axis=0)
    w_tall = jnp.concatenate([w_tall, w_tall], axis=1)

    loop(1, EMB, lambda i: lg_copy(i).wait_recv())
    logit = logits[0]
    for f in range(1, EMB):
        logit = logit + logits[f]
    slope = jax.nn.sigmoid(logit) - labels[...]
    grad = (slope[:1] * w_tall * slant).astype(BF16)
    halves = (grad[:128], grad[128:])

    def grad_half(c, half):
        rhs = jnp.where(half == 0, halves[0], halves[1])
        return lax.dot_general(turned[c], rhs, NT, preferred_element_type=F32)

    def y_copy(k, c):
        return send(y_out.at[c], y_in.at[c], y_s.at[k], y_r.at[k], y_mate)

    near = (2, 1, -1)
    order = [lax.rem(z + off + 4, 4) for off in near] + [zr]
    for k, c in enumerate(order):
        coded, power = encode(grad_half(c, other))
        y_out[c, :512] = coded
        y_out[c, 512:] = tile_of(power)
        y_copy(k, c).start()
        sent.append(lambda k=k, c=c: y_copy(k, c).wait_send())
    head = lax.dot_general(slope, act, NT, precision=lax.Precision.HIGHEST, preferred_element_type=F32)
    heads[e] = jnp.concatenate([head[:1, :128], head[:1, 128:], jnp.zeros((6, 128), F32)], axis=0)

    def hd_copy(i):
        return send(heads.at[e], heads.at[e], hd_s.at[i], hd_r.at[i], (emb_at(i), g))

    loop(1, EMB, lambda i: hd_copy(i).start())
    sent.append(lambda: loop(1, EMB, lambda i: hd_copy(i).wait_send()))

    core = lax.rem(e, 2)

    def gs_copy(i):
        return send(gp_sib.at[i], gp_got.at[i], gs_s.at[i], gs_r.at[i], (sib, g))

    def gs_start(i):
        gp_sib[i] = jnp.dot(w_cols[2 * i + 1 - core], grad, preferred_element_type=F32)
        gs_copy(i).start()

    loop(0, 8, gs_start)
    sent.append(lambda: loop(0, 8, lambda i: gs_copy(i).wait_send()))

    def gp_part(i):
        gp_own[i] = jnp.dot(w_cols[2 * i + core], grad, preferred_element_type=F32)

    loop(0, 8, gp_part)
    chip = e // 2
    y_high = chip // 4
    col = lax.rem(chip, 4)

    def gp_copy(i):
        to = (y_high * 8 + 2 * lax.rem(col + i, 4) + core, g)
        return send(gp_out.at[i - 1], gp_in.at[i - 1], gp_s.at[i - 1], gp_r.at[i - 1], to)

    def gp_start(i):
        for h in range(2):
            c = h * 4 + lax.rem(col + i, 4)
            gs_copy(c).wait_recv()
            coded, power = encode(gp_own[c] + gp_got[c])
            gp_out[i - 1, h, :D_FIELD] = coded
            gp_out[i - 1, h, D_FIELD:] = tile_of(power)
        gp_copy(i).start()

    loop(1, 4, gp_start)
    sent.append(lambda: loop(1, 4, lambda i: gp_copy(i).wait_send()))
    for h in range(2):
        gs_copy(h * 4 + col).wait_recv()
    for k, c in enumerate(order):
        mine[c] = grad_half(c, y)

    def near_copy(k):
        return send(near_out.at[k], near_in.at[k], n_s.at[k], n_r.at[k], z_at(near[k]))

    for k in range(3):
        c = order[k]
        y_copy(k, c).wait_recv()
        coded, power = encode(mine[c] + decode(y_in[c, :512], y_in[c, 512:]))
        near_out[k, :512] = coded
        near_out[k, 512:] = tile_of(power)
        near_copy(k).start()
        sent.append(lambda k=k: near_copy(k).wait_send())
    y_copy(3, zr).wait_recv()
    acc[...] = (mine[zr] + decode(y_in[zr, :512], y_in[zr, 512:])).reshape(4, 128, 128)

    loop(1, 4, lambda i: gp_copy(i).wait_recv())

    def row_sum(h):
        total = gp_own[h * 4 + col] + gp_got[h * 4 + col]
        for i in range(3):
            total = total + decode(gp_in[i, h, :D_FIELD], gp_in[i, h, D_FIELD:])
        return total

    coded, power = encode(row_sum(1 - y_high))
    gq_out[:D_FIELD] = coded
    gq_out[D_FIELD:] = tile_of(power)
    gq_copy = send(gq_out, gq_in, gq_s, gq_r, (emb_at(8), g))
    gq_copy.start()
    sent.append(lambda: gq_copy.wait_send())
    gp_sum[...] = row_sum(y_high)

    for k in range(3):
        near_copy(k).wait_recv()
        acc[...] = acc[...] + decode(near_in[k, :512], near_in[k, 512:]).reshape(4, 128, 128)

    def far_copy(m):
        return send(far_out.at[m - 1], far_in.at[m - 1], fr_s.at[m - 1], fr_r.at[m - 1], z_at(4 * m))

    for m in (2, 1, 3):
        coded, power = encode(acc[lax.rem(zq + m, 4)])
        far_out[m - 1, :128] = coded
        far_out[m - 1, 128:] = tile_of(power)
        far_copy(m).start()
        sent.append(lambda m=m: far_copy(m).wait_send())

    gq_copy.wait_recv()
    grad_pool = (gp_sum[...] + decode(gq_in[:D_FIELD], gq_in[D_FIELD:])).astype(BF16)
    subs = lax.broadcasted_iota(jnp.int32, (CENT, D_FIELD), 1) // SUBW
    table[...] = jnp.zeros((CENT, D_FIELD), F32)

    def table_step(step):
        place = pl.ds(pl.multiple_of(step * GROUP * CENT, GROUP * CENT), GROUP * CENT)
        got = lax.dot_general(low[place, :], grad_pool, NT, preferred_element_type=F32)
        got = got + 256.0 * lax.dot_general(high[place, :], grad_pool, NT, preferred_element_type=F32)
        for j in range(GROUP):
            part = got[j * CENT : (j + 1) * CENT]
            table[...] = table[...] + jnp.where(subs == step * GROUP + j, part, 0.0)

    loop(0, SUB // GROUP, table_step)
    loop(1, EMB, lambda i: hd_copy(i).wait_recv())
    for yy in range(2):
        for zz in range(ZED):
            gg = yy * ZED + zz
            tab[yy, zz % 4, zz // 4, :8] = table[gg * 8 : gg * 8 + 8]
            tab[yy, zz % 4, zz // 4, 8:] = jnp.concatenate(
                [heads[gg // 2, gg % 2 : gg % 2 + 1], jnp.zeros((7, 128), F32)], axis=0
            )
    ty_copy = send(tab.at[other], tab_y, ty_s, ty_r, y_mate)
    ty_copy.start()
    sent.append(lambda: ty_copy.wait_send())
    ty_copy.wait_recv()
    tab[y] = tab[y] + tab_y[...]

    def tn_copy(k):
        return send(tab.at[y, order[k]], tab_near.at[k], tn_s.at[k], tn_r.at[k], z_at(near[k]))

    for k in range(3):
        tn_copy(k).start()
        sent.append(lambda k=k: tn_copy(k).wait_send())
    for k in range(3):
        tn_copy(k).wait_recv()
    tab[y, zr] = tab[y, zr] + tab_near[0] + tab_near[1] + tab_near[2]

    def tf_copy(m):
        return send(
            tab.at[y, zr, lax.rem(zq + m, 4)], tab_far.at[m - 1], tf_s.at[m - 1], tf_r.at[m - 1], z_at(4 * m)
        )

    for m in range(1, 4):
        tf_copy(m).start()
        sent.append(lambda m=m: tf_copy(m).wait_send())

    whole = acc[zq]
    for m in range(1, 4):
        far_copy(m).wait_recv()
        whole = whole + decode(far_in[m - 1, :128], far_in[m - 1, 128:])
    red[...] = whole.reshape(EMB, 8, 128)

    def a_copy(i):
        return send(red.at[emb_at(i)], cols.at[e], a_s.at[i], a_r.at[i], (emb_at(i), g))

    loop(1, EMB, lambda i: a_copy(i).start())
    sent.append(lambda: loop(1, EMB, lambda i: a_copy(i).wait_send()))
    cols[e] = red[e]

    for m in range(1, 4):
        tf_copy(m).wait_recv()
    tab_whole = tab[y, zr, zq] + tab_far[0] + tab_far[1] + tab_far[2]
    tab_code, tab_power = encode(tab_whole[:8])
    head_code, head_power = encode(tab_whole[8:])
    loop(1, EMB, lambda i: a_copy(i).wait_recv())
    coded, power = encode(cols[...].reshape(128, 128))
    spots = lax.broadcasted_iota(jnp.int32, (16, 128), 0)
    tail = jnp.concatenate([number(tab_code), number(head_code)], axis=0)
    for at, row in ((9, power), (10, tab_power), (11, head_power)):
        tail = jnp.where(spots == at, row, tail)
    out[y, zr, zq, :128] = coded
    out[y, zr, zq, 128:] = tail.astype(jnp.int32).astype(I16)
    def block(off, m):
        src = lax.rem(z + 2 * ZED - off - 4 * m, ZED)
        return out.at[y, lax.rem(src, 4), src // 4]

    def of_copy(m):
        return send(block(0, 0), block(0, 0), of_s.at[m - 1], of_r.at[m - 1], z_at(4 * m))

    def of_wait(m):
        send(block(0, m), block(0, m), of_s.at[m - 1], of_r.at[m - 1], z_at(4 * m)).wait_recv()

    ways = (1, -1, 2)

    def on_copy(k, m):
        got = block(1 if k == 2 else 0, m)
        return send(got, got, on_s.at[k, m], on_r.at[k, m], z_at(-1 if k == 1 else 1))

    def on_wait(k, m):
        got = block(ways[k], m)
        send(got, got, on_s.at[k, m], on_r.at[k, m], z_at(1)).wait_recv()

    def oy_copy(k, m):
        got = block(0 if k == 0 else ways[k - 1], m)
        return send(got, got, oy_s.at[k, m], oy_r.at[k, m], y_mate)

    def oy_wait(k, m):
        src = lax.rem(z + 2 * ZED - (0 if k == 0 else ways[k - 1]) - 4 * m, ZED)
        got = out.at[other, lax.rem(src, 4), src // 4]
        send(got, got, oy_s.at[k, m], oy_r.at[k, m], y_mate).wait_recv()

    def put(copy):
        copy.start()
        sent.append(copy.wait_send)

    turns = (0, 1, 3, 2)
    for m in (2, 1, 3):
        put(of_copy(m))
    for m in turns:
        if m:
            of_wait(m)
        put(on_copy(0, m))
        put(on_copy(1, m))
        put(oy_copy(0, m))
    for m in turns:
        on_wait(0, m)
        put(on_copy(2, m))
        put(oy_copy(1, m))
        on_wait(1, m)
        put(oy_copy(2, m))
    for m in turns:
        on_wait(2, m)
        put(oy_copy(3, m))
    for m in range(4):
        for k in range(4):
            oy_wait(k, m)
    for wait in sent:
        wait()


def train(codes, bag, book, w_in, w_out, labels):
    hbm = pl.BlockSpec(memory_space=pl.ANY)
    V, D = pltpu.VMEM, pltpu.SemaphoreType.DMA
    rows = codes.shape[1]
    scratch = [
        V((SUB, rows), jnp.int32),
        V((1, rows), jnp.int32),
        V((CENT, D_FIELD), BF16),
        V((32, 128), F32),
        V((1, SAMP), F32),
        V((D_FIELD, CENT), F32),
        V((SAMP, rows), F8),
        V((D_FIELD, SAMP), F32),
        V((SUB * CENT, SAMP), BF16),
        V((SUB * CENT, SAMP), BF16),
        V((EMB, D_FIELD, WIDE), BF16),
        V((WIDE, EMB * D_FIELD), BF16),
        V((EMB, D_FIELD, SAMP), BF16),
        V((16, EMB, 8, SAMP), F32),
        V((4, 512, SAMP), BF16),
        V((EMB, 8, SAMP), F32),
        V((EMB, 8, 128), F32),
        V((8, D_FIELD, SAMP), F32),
        V((8, D_FIELD, SAMP), F32),
        V((8, D_FIELD, SAMP), F32),
        V((3, 2, D_FIELD + 16, SAMP), I16),
        V((3, 2, D_FIELD + 16, SAMP), I16),
        V((D_FIELD + 16, SAMP), I16),
        V((D_FIELD + 16, SAMP), I16),
        V((D_FIELD, SAMP), F32),
        V((4, 528, 128), I16),
        V((4, 528, 128), I16),
        V((4, 512, 128), F32),
        V((3, 528, 128), I16),
        V((3, 528, 128), I16),
        V((4, 128, 128), F32),
        V((3, 144, 128), I16),
        V((3, 144, 128), I16),
        V((EMB, 8, 128), F32),
        V((EMB, 8, 128), F32),
        V((CENT, D_FIELD), F32),
        V((2, 4, 4, 16, 128), F32),
        V((4, 4, 16, 128), F32),
        V((3, 4, 16, 128), F32),
        V((3, 16, 128), F32),
        D((6,)),
    ]
    sems = [(16,), (16,), (16,), (2, 8), (2, 8), (16,), (16,), (8,), (3,), (), (4,), (3,), (3,), (16,), (), (3,), (3,), (3,), (3, 4), (4, 4)]
    for shape in sems:
        scratch += [D(shape), D(shape)] if shape else [D, D]
    return pl.pallas_call(
        step_kernel,
        out_shape=jax.ShapeDtypeStruct((2, 4, 4, BLOCK, 128), I16),
        in_specs=[hbm] * 6,
        out_specs=pl.BlockSpec(memory_space=pltpu.VMEM),
        scratch_shapes=scratch,
        compiler_params=pltpu.CompilerParams(
            collective_id=1, has_side_effects=True, vmem_limit_bytes=56 << 20
        ),
        name="train_step",
    )(codes, bag, book, w_in, w_out, labels)


def spread_kernel(gathered, weight, table, head):
    a = pl.program_id(0)
    for c in range(4):
        for yy in range(2):
            tail = number(gathered[yy, c, 0, 128:])
            scales = jnp.exp2(tail[8:] - 15.0)
            whole = number(gathered[yy, c, 0, :128]) * scales[1:2]
            for f in range(EMB):
                spot = f * WIDE + yy * 128
                weight[c * 8 : c * 8 + 8, spot : spot + 128] = whole[f * 8 : f * 8 + 8]
            gg = yy * ZED + a * 4 + c
            table[pl.ds(pl.multiple_of(gg * 8, 8), 8), :] = tail[:8] * scales[2:3]
            head[pl.ds(gg, 1), :] = tail[8:9] * scales[3:4]


def spread(gathered):
    return pl.pallas_call(
        spread_kernel,
        grid=(4,),
        out_shape=(
            jax.ShapeDtypeStruct((D_FIELD, HID), F32),
            jax.ShapeDtypeStruct((CENT, D_FIELD), F32),
            jax.ShapeDtypeStruct((DENSE, 128), F32),
        ),
        in_specs=[pl.BlockSpec((2, 4, 1, BLOCK, 128), lambda i: (0, 0, i, 0, 0))],
        out_specs=(
            pl.BlockSpec((32, HID), lambda i: (i, 0)),
            pl.BlockSpec((CENT, D_FIELD), lambda i: (0, 0)),
            pl.BlockSpec((DENSE, 128), lambda i: (0, 0)),
        ),
        name="spread",
    )(gathered)


def body(codes, row_bag, codebook, w_in, w_out, labels):
    gathered = train(
        codes[0].T, row_bag, codebook[0], w_in, w_out.reshape(32, 128), labels.reshape(1, SAMP)
    )
    weight, table, head = spread(gathered)
    return table[None], weight, head.reshape(HID)


def solution(mesh):
    in_specs = (
        P("emb", "dense", None),
        P("emb", "dense"),
        P("emb", None, None),
        P("emb", None),
        P(),
        P("dense"),
    )
    out_specs = (P("emb", None, None), P("emb", None), P())
    return jax.shard_map(body, mesh=mesh, in_specs=in_specs, out_specs=out_specs, check_vma=False)
```

```python
import functools

import jax
import jax.numpy as jnp
from jax import lax
from jax.experimental import pallas as pl
from jax.experimental.pallas import tpu as pltpu
from jax.sharding import PartitionSpec as P

D_FIELD = 128
SUB = 16
SUBW = 8
CENT = 256
EMB = 16
DENSE = 32
ZED = 16
SAMP = 256
WIDE = 256
HID = 4096
F32 = jnp.float32
BF16 = jnp.bfloat16
F8 = jnp.float8_e4m3fn
I16 = jnp.int16
NT = (((1,), (1,)), ((), ()))
MESH = pl.DeviceIdType.MESH
BLOCK = 144
GROUP = 4


def encode(value):
    top = jnp.maximum(jnp.max(jnp.abs(value), axis=0, keepdims=True), 1e-30)
    power = jnp.ceil(jnp.log2(top) + 0.001)
    coded = jnp.floor(value * jnp.exp2(15.0 - power) + 0.5)
    return coded.astype(jnp.int32).astype(I16), power


def tile_of(power):
    return jnp.broadcast_to(power, (16, power.shape[1])).astype(jnp.int32).astype(I16)


def number(coded):
    return coded.astype(jnp.int32).astype(F32)


def decode(coded, power):
    return number(coded) * jnp.exp2(number(power)[:1] - 15.0)


def step_kernel(
    codes_hbm, bag_hbm, book_hbm, w_in, w_out_hbm, labels_hbm, out_hbm, out,
    codes, bag, book, w_out, labels, table_t, members, pooled, low, high,
    w_cols, w_turned, fields, fields32, turned, logits, heads,
    gp_own, gp_sib, gp_got, gp_out, gp_in, gq_out, gq_in, gp_sum,
    y_out, y_in, mine, near_out, near_in, acc, far_out, far_in, red, cols,
    table, tab, tab_y, tab_near, tab_far,
    local, w_s, w_r, wu_s, wu_r, wd_s, wd_r, f_s, f_r, sib_s, sib_r, lg_s, lg_r, hd_s, hd_r, gs_s, gs_r, gp_s, gp_r, gq_s, gq_r,
    y_s, y_r, n_s, n_r, fr_s, fr_r, a_s, a_r,
    ty_s, ty_r, tn_s, tn_r, tf_s, tf_r, of_s, of_r, on_s, on_r, oy_s, oy_r, kept,
):
    e = lax.axis_index("emb")
    g = lax.axis_index("dense")
    y = g // ZED
    z = lax.rem(g, ZED)
    zq = z // 4
    zr = lax.rem(z, 4)
    sib = e + 1 - 2 * lax.rem(e, 2)
    other = 1 - y

    def emb_at(i):
        return lax.rem(e + i, EMB)

    def emb_from(i):
        return lax.rem(e + EMB - i, EMB)

    def z_at(off):
        return (e, y * ZED + lax.rem(z + off + ZED, ZED))

    def send(src, dst, ss, rs, to):
        return pltpu.make_async_remote_copy(
            src_ref=src, dst_ref=dst, send_sem=ss, recv_sem=rs, device_id=to, device_id_type=MESH
        )

    def loop(lo, hi, body):
        def step(i, carry):
            body(i)
            return carry

        lax.fori_loop(lo, hi, step, 0)

    y_mate = (e, other * ZED + z)
    loads = [
        pltpu.make_async_copy(src, dst, local.at[1 + i])
        for i, (src, dst) in enumerate(
            ((bag_hbm, bag), (codes_hbm, codes), (book_hbm, book), (w_out_hbm, w_out), (labels_hbm, labels))
        )
    ]
    for load in loads:
        load.start()
    sent = []
    barrier = pltpu.get_barrier_semaphore()
    loop(1, EMB, lambda i: pl.semaphore_signal(barrier, inc=1, device_id=(emb_at(i), g), device_id_type=MESH))
    for off in (1, -1, 2, -2, 4, -4, 8):
        pl.semaphore_signal(barrier, inc=1, device_id=z_at(off), device_id_type=MESH)
    pl.semaphore_signal(barrier, inc=1, device_id=y_mate, device_id_type=MESH)

    half = lax.rem(z, 2)
    own_lanes = pl.ds(pl.multiple_of(half * 128, 128), 128)
    far_lanes = pl.ds(pl.multiple_of((1 - half) * 128, 128), 128)

    def w_copy(i):
        cols_of = pl.ds(pl.multiple_of(emb_at(i) * WIDE + half * 128, 128), 128)
        return send(w_in.at[:, cols_of], w_cols.at[e, :, own_lanes], w_s.at[i], w_r.at[i], (emb_at(i), g))

    def up_copy(i, lanes):
        part = w_cols.at[emb_from(i), pl.ds(0, 64), lanes]
        return send(part, part, wu_s.at[i], wu_r.at[i], z_at(1))

    def down_copy(i, lanes):
        part = w_cols.at[emb_from(i), pl.ds(64, 64), lanes]
        return send(part, part, wd_s.at[i], wd_r.at[i], z_at(-1))

    def pass_on(i):
        w_copy(i).wait_recv()
        up_copy(i, own_lanes).start()
        down_copy(i, own_lanes).start()

    pl.semaphore_wait(barrier, EMB - 1 + 8)
    loop(1, EMB, lambda i: w_copy(i).start())
    sent.append(lambda: loop(1, EMB, lambda i: w_copy(i).wait_send()))
    own_w = pltpu.make_async_copy(
        w_in.at[:, pl.ds(pl.multiple_of(e * WIDE, WIDE), WIDE)], w_cols.at[e], local.at[0]
    )
    own_w.start()

    def rows_of(f, h):
        return fields.at[f, pl.ds(h * 64, 64)]

    def f_copy(i, h):
        return send(rows_of(e, h), rows_of(e, h), f_s.at[h, i], f_r.at[h, i], (emb_at(2 * i), g))

    def sib_copy(i, h):
        f = lax.rem(e + 2 * EMB - 2 * i, EMB)
        return send(rows_of(f, h), rows_of(f, h), sib_s.at[h, i], sib_r.at[h, i], (sib, g))

    def onehot(row):
        ids = lax.broadcasted_iota(jnp.int32, (CENT, row.shape[1]), 0).astype(F32).astype(BF16)
        same = row.astype(F32).astype(BF16) == ids
        return jnp.where(same, jnp.ones((), BF16), jnp.zeros((), BF16)).astype(F8)

    for load in loads:
        load.wait()
    members[...] = onehot(bag[...])
    table_t[...] = book[...].astype(F32).T

    def count_step(step):
        at = step * GROUP
        picks = jnp.concatenate([onehot(codes[pl.ds(at + j, 1), :]) for j in range(GROUP)], axis=0)
        count = lax.dot_general(picks, members[...], NT, preferred_element_type=F32)
        upper = jnp.floor(count * (1.0 / 256.0))
        lower = (count - upper * 256.0).astype(BF16)
        upper = upper.astype(BF16)
        place = pl.ds(pl.multiple_of(at * CENT, CENT * GROUP), CENT * GROUP)
        low[place, :] = lower
        high[place, :] = upper
        rows = pl.ds(pl.multiple_of(at * SUBW, SUBW * GROUP), SUBW * GROUP)
        part = table_t[rows, :].astype(BF16)
        for j in range(GROUP):
            mine_at = slice(j * SUBW, (j + 1) * SUBW)
            span = slice(j * CENT, (j + 1) * CENT)
            pooled[pl.ds(pl.multiple_of((at + j) * SUBW, SUBW), SUBW), :] = jnp.dot(
                part[mine_at], lower[span], preferred_element_type=F32
            ) + 256.0 * jnp.dot(part[mine_at], upper[span], preferred_element_type=F32)

    def send_half(h):
        rows = pl.ds(h * 64, 64)
        fields[e, rows] = pooled[rows].astype(BF16)
        loop(1, 8, lambda i: f_copy(i, h).start())
        sib_copy(0, h).start()
        sent.append(lambda: loop(1, 8, lambda i: f_copy(i, h).wait_send()))
        sent.append(lambda: loop(0, 8, lambda i: sib_copy(i, h).wait_send()))

    loop(0, 1, count_step)

    def later_step(step):
        count_step(step)

        @pl.when(step == 1)
        def _():
            send_half(0)

    loop(1, 4, later_step)
    send_half(1)
    loop(1, EMB, pass_on)
    sent.append(lambda: loop(1, EMB, lambda i: up_copy(i, own_lanes).wait_send()))
    sent.append(lambda: loop(1, EMB, lambda i: down_copy(i, own_lanes).wait_send()))

    def forward(i, h):
        f_copy(i, h).wait_recv()
        sib_copy(i, h).start()

    for h in range(2):
        loop(1, 8, lambda i: forward(i, h))

    def turn(f):
        w_turned[:, pl.ds(pl.multiple_of(f * D_FIELD, D_FIELD), D_FIELD)] = w_cols[f].T

    def take(i):
        up_copy(i, far_lanes).wait_recv()
        down_copy(i, far_lanes).wait_recv()
        turn(emb_from(i))

    own_w.wait()
    turn(e)
    loop(1, EMB, take)
    for h in range(2):
        loop(0, 8, lambda i: sib_copy(i, h).wait_recv())
    pre = jnp.dot(w_turned[...], fields[...].reshape(EMB * D_FIELD, SAMP), preferred_element_type=F32)
    gate = jax.nn.sigmoid(pre)
    act = pre * gate
    w_row = jnp.concatenate([w_out[pl.ds(2 * e, 1), :], w_out[pl.ds(2 * e + 1, 1), :]], axis=1)
    w_rows = jnp.broadcast_to(w_row, (8, WIDE))
    logits[e] = jnp.dot(w_rows, act, precision=lax.Precision.HIGHEST, preferred_element_type=F32)

    def lg_copy(i):
        return send(logits.at[e], logits.at[e], lg_s.at[i], lg_r.at[i], (emb_at(i), g))

    loop(1, EMB, lambda i: lg_copy(i).start())
    sent.append(lambda: loop(1, EMB, lambda i: lg_copy(i).wait_send()))

    for f in range(EMB):
        fields32[:, f] = fields[f].astype(F32).reshape(16, 8, SAMP)
    for c in range(4):
        for a in range(4):
            turned[c, a * 128 : (a + 1) * 128] = fields32[a * 4 + c].reshape(128, SAMP).astype(BF16)
    slant = gate + pre * gate * (1.0 - gate)
    w_left = jnp.broadcast_to(w_row[:, :128], (128, 128)).T
    w_right = jnp.broadcast_to(w_row[:, 128:], (128, 128)).T
    w_tall = jnp.concatenate([w_left, w_right], axis=0)
    w_tall = jnp.concatenate([w_tall, w_tall], axis=1)

    loop(1, EMB, lambda i: lg_copy(i).wait_recv())
    logit = logits[0]
    for f in range(1, EMB):
        logit = logit + logits[f]
    slope = jax.nn.sigmoid(logit) - labels[...]
    grad = (slope[:1] * w_tall * slant).astype(BF16)
    halves = (grad[:128], grad[128:])

    def grad_half(c, half):
        rhs = jnp.where(half == 0, halves[0], halves[1])
        return lax.dot_general(turned[c], rhs, NT, preferred_element_type=F32)

    def y_copy(k, c):
        return send(y_out.at[c], y_in.at[c], y_s.at[k], y_r.at[k], y_mate)

    near = (2, 1, -1)
    order = [lax.rem(z + off + 4, 4) for off in near] + [zr]
    for k, c in enumerate(order):
        coded, power = encode(grad_half(c, other))
        y_out[c, :512] = coded
        y_out[c, 512:] = tile_of(power)
        y_copy(k, c).start()
        sent.append(lambda k=k, c=c: y_copy(k, c).wait_send())
    head = lax.dot_general(slope, act, NT, precision=lax.Precision.HIGHEST, preferred_element_type=F32)
    heads[e] = jnp.concatenate([head[:1, :128], head[:1, 128:], jnp.zeros((6, 128), F32)], axis=0)

    def hd_copy(i):
        return send(heads.at[e], heads.at[e], hd_s.at[i], hd_r.at[i], (emb_at(i), g))

    loop(1, EMB, lambda i: hd_copy(i).start())
    sent.append(lambda: loop(1, EMB, lambda i: hd_copy(i).wait_send()))

    core = lax.rem(e, 2)

    def gs_copy(i):
        return send(gp_sib.at[i], gp_got.at[i], gs_s.at[i], gs_r.at[i], (sib, g))

    def gs_start(i):
        gp_sib[i] = jnp.dot(w_cols[2 * i + 1 - core], grad, preferred_element_type=F32)
        gs_copy(i).start()

    loop(0, 8, gs_start)
    sent.append(lambda: loop(0, 8, lambda i: gs_copy(i).wait_send()))

    def gp_part(i):
        gp_own[i] = jnp.dot(w_cols[2 * i + core], grad, preferred_element_type=F32)

    loop(0, 8, gp_part)
    chip = e // 2
    y_high = chip // 4
    col = lax.rem(chip, 4)

    def gp_copy(i):
        to = (y_high * 8 + 2 * lax.rem(col + i, 4) + core, g)
        return send(gp_out.at[i - 1], gp_in.at[i - 1], gp_s.at[i - 1], gp_r.at[i - 1], to)

    def gp_start(i):
        for h in range(2):
            c = h * 4 + lax.rem(col + i, 4)
            gs_copy(c).wait_recv()
            coded, power = encode(gp_own[c] + gp_got[c])
            gp_out[i - 1, h, :D_FIELD] = coded
            gp_out[i - 1, h, D_FIELD:] = tile_of(power)
        gp_copy(i).start()

    loop(1, 4, gp_start)
    sent.append(lambda: loop(1, 4, lambda i: gp_copy(i).wait_send()))
    for h in range(2):
        gs_copy(h * 4 + col).wait_recv()
    for k, c in enumerate(order):
        mine[c] = grad_half(c, y)

    def near_copy(k):
        return send(near_out.at[k], near_in.at[k], n_s.at[k], n_r.at[k], z_at(near[k]))

    for k in range(3):
        c = order[k]
        y_copy(k, c).wait_recv()
        coded, power = encode(mine[c] + decode(y_in[c, :512], y_in[c, 512:]))
        near_out[k, :512] = coded
        near_out[k, 512:] = tile_of(power)
        near_copy(k).start()
        sent.append(lambda k=k: near_copy(k).wait_send())
    y_copy(3, zr).wait_recv()
    acc[...] = (mine[zr] + decode(y_in[zr, :512], y_in[zr, 512:])).reshape(4, 128, 128)

    loop(1, 4, lambda i: gp_copy(i).wait_recv())

    def row_sum(h):
        total = gp_own[h * 4 + col] + gp_got[h * 4 + col]
        for i in range(3):
            total = total + decode(gp_in[i, h, :D_FIELD], gp_in[i, h, D_FIELD:])
        return total

    coded, power = encode(row_sum(1 - y_high))
    gq_out[:D_FIELD] = coded
    gq_out[D_FIELD:] = tile_of(power)
    gq_copy = send(gq_out, gq_in, gq_s, gq_r, (emb_at(8), g))
    gq_copy.start()
    sent.append(lambda: gq_copy.wait_send())
    gp_sum[...] = row_sum(y_high)

    for k in range(3):
        near_copy(k).wait_recv()
        acc[...] = acc[...] + decode(near_in[k, :512], near_in[k, 512:]).reshape(4, 128, 128)

    def far_copy(m):
        return send(far_out.at[m - 1], far_in.at[m - 1], fr_s.at[m - 1], fr_r.at[m - 1], z_at(4 * m))

    for m in (2, 1, 3):
        coded, power = encode(acc[lax.rem(zq + m, 4)])
        far_out[m - 1, :128] = coded
        far_out[m - 1, 128:] = tile_of(power)
        far_copy(m).start()
        sent.append(lambda m=m: far_copy(m).wait_send())

    gq_copy.wait_recv()
    grad_pool = (gp_sum[...] + decode(gq_in[:D_FIELD], gq_in[D_FIELD:])).astype(BF16)
    subs = lax.broadcasted_iota(jnp.int32, (CENT, D_FIELD), 1) // SUBW
    table[...] = jnp.zeros((CENT, D_FIELD), F32)

    def table_step(step):
        place = pl.ds(pl.multiple_of(step * GROUP * CENT, GROUP * CENT), GROUP * CENT)
        got = lax.dot_general(low[place, :], grad_pool, NT, preferred_element_type=F32)
        got = got + 256.0 * lax.dot_general(high[place, :], grad_pool, NT, preferred_element_type=F32)
        for j in range(GROUP):
            part = got[j * CENT : (j + 1) * CENT]
            table[...] = table[...] + jnp.where(subs == step * GROUP + j, part, 0.0)

    loop(0, SUB // GROUP, table_step)
    loop(1, EMB, lambda i: hd_copy(i).wait_recv())
    for yy in range(2):
        for zz in range(ZED):
            gg = yy * ZED + zz
            tab[yy, zz % 4, zz // 4, :8] = table[gg * 8 : gg * 8 + 8]
            tab[yy, zz % 4, zz // 4, 8:] = jnp.concatenate(
                [heads[gg // 2, gg % 2 : gg % 2 + 1], jnp.zeros((7, 128), F32)], axis=0
            )
    ty_copy = send(tab.at[other], tab_y, ty_s, ty_r, y_mate)
    ty_copy.start()
    sent.append(lambda: ty_copy.wait_send())
    ty_copy.wait_recv()
    tab[y] = tab[y] + tab_y[...]

    def tn_copy(k):
        return send(tab.at[y, order[k]], tab_near.at[k], tn_s.at[k], tn_r.at[k], z_at(near[k]))

    for k in range(3):
        tn_copy(k).start()
        sent.append(lambda k=k: tn_copy(k).wait_send())
    for k in range(3):
        tn_copy(k).wait_recv()
    tab[y, zr] = tab[y, zr] + tab_near[0] + tab_near[1] + tab_near[2]

    def tf_copy(m):
        return send(
            tab.at[y, zr, lax.rem(zq + m, 4)], tab_far.at[m - 1], tf_s.at[m - 1], tf_r.at[m - 1], z_at(4 * m)
        )

    for m in range(1, 4):
        tf_copy(m).start()
        sent.append(lambda m=m: tf_copy(m).wait_send())

    whole = acc[zq]
    for m in range(1, 4):
        far_copy(m).wait_recv()
        whole = whole + decode(far_in[m - 1, :128], far_in[m - 1, 128:])
    red[...] = whole.reshape(EMB, 8, 128)

    def a_copy(i):
        return send(red.at[emb_at(i)], cols.at[e], a_s.at[i], a_r.at[i], (emb_at(i), g))

    loop(1, EMB, lambda i: a_copy(i).start())
    sent.append(lambda: loop(1, EMB, lambda i: a_copy(i).wait_send()))
    cols[e] = red[e]

    for m in range(1, 4):
        tf_copy(m).wait_recv()
    tab_whole = tab[y, zr, zq] + tab_far[0] + tab_far[1] + tab_far[2]
    tab_code, tab_power = encode(tab_whole[:8])
    head_code, head_power = encode(tab_whole[8:])
    loop(1, EMB, lambda i: a_copy(i).wait_recv())
    coded, power = encode(cols[...].reshape(128, 128))
    spots = lax.broadcasted_iota(jnp.int32, (16, 128), 0)
    tail = jnp.concatenate([number(tab_code), number(head_code)], axis=0)
    for at, row in ((9, power), (10, tab_power), (11, head_power)):
        tail = jnp.where(spots == at, row, tail)
    out[y, zr, zq, :128] = coded
    out[y, zr, zq, 128:] = tail.astype(jnp.int32).astype(I16)
    def block(off, m):
        src = lax.rem(z + 2 * ZED - off - 4 * m, ZED)
        return out.at[y, lax.rem(src, 4), src // 4]

    def of_copy(m):
        return send(block(0, 0), block(0, 0), of_s.at[m - 1], of_r.at[m - 1], z_at(4 * m))

    def of_wait(m):
        send(block(0, m), block(0, m), of_s.at[m - 1], of_r.at[m - 1], z_at(4 * m)).wait_recv()

    ways = (1, -1, 2)

    def on_copy(k, m):
        got = block(1 if k == 2 else 0, m)
        return send(got, got, on_s.at[k, m], on_r.at[k, m], z_at(-1 if k == 1 else 1))

    def on_wait(k, m):
        got = block(ways[k], m)
        send(got, got, on_s.at[k, m], on_r.at[k, m], z_at(1)).wait_recv()

    def oy_copy(k, m):
        got = block(0 if k == 0 else ways[k - 1], m)
        return send(got, got, oy_s.at[k, m], oy_r.at[k, m], y_mate)

    def oy_wait(k, m):
        src = lax.rem(z + 2 * ZED - (0 if k == 0 else ways[k - 1]) - 4 * m, ZED)
        got = out.at[other, lax.rem(src, 4), src // 4]
        send(got, got, oy_s.at[k, m], oy_r.at[k, m], y_mate).wait_recv()

    def put(copy):
        copy.start()
        sent.append(copy.wait_send)

    turns = (0, 1, 3, 2)
    for m in (2, 1, 3):
        put(of_copy(m))
    for m in turns:
        if m:
            of_wait(m)
        put(on_copy(0, m))
        put(on_copy(1, m))
        put(oy_copy(0, m))
    for m in turns:
        on_wait(0, m)
        put(on_copy(2, m))
        put(oy_copy(1, m))
        on_wait(1, m)
        put(oy_copy(2, m))
    for m in turns:
        on_wait(2, m)
        put(oy_copy(3, m))
    def keep_all(yy, c, n):
        pltpu.make_async_copy(out.at[yy, c], out_hbm.at[yy, c], kept.at[n, 0]).start()
        sent.append(lambda: pltpu.make_async_copy(out.at[yy, c], out_hbm.at[yy, c], kept.at[n, 0]).wait())

    for c in range(4):
        keep_all(y, c, c)
    for k in range(4):
        for m in range(4):
            oy_wait(k, m)
        off = 0 if k == 0 else ways[k - 1]
        keep_all(other, lax.rem(z + ZED - off, 4), 4 + k)
    for wait in sent:
        wait()


def train(codes, bag, book, w_in, w_out, labels):
    hbm = pl.BlockSpec(memory_space=pl.ANY)
    V, D = pltpu.VMEM, pltpu.SemaphoreType.DMA
    rows = codes.shape[1]
    scratch = [
        V((2, 4, 4, BLOCK, 128), I16),
        V((SUB, rows), jnp.int32),
        V((1, rows), jnp.int32),
        V((CENT, D_FIELD), BF16),
        V((32, 128), F32),
        V((1, SAMP), F32),
        V((D_FIELD, CENT), F32),
        V((SAMP, rows), F8),
        V((D_FIELD, SAMP), F32),
        V((SUB * CENT, SAMP), BF16),
        V((SUB * CENT, SAMP), BF16),
        V((EMB, D_FIELD, WIDE), BF16),
        V((WIDE, EMB * D_FIELD), BF16),
        V((EMB, D_FIELD, SAMP), BF16),
        V((16, EMB, 8, SAMP), F32),
        V((4, 512, SAMP), BF16),
        V((EMB, 8, SAMP), F32),
        V((EMB, 8, 128), F32),
        V((8, D_FIELD, SAMP), F32),
        V((8, D_FIELD, SAMP), F32),
        V((8, D_FIELD, SAMP), F32),
        V((3, 2, D_FIELD + 16, SAMP), I16),
        V((3, 2, D_FIELD + 16, SAMP), I16),
        V((D_FIELD + 16, SAMP), I16),
        V((D_FIELD + 16, SAMP), I16),
        V((D_FIELD, SAMP), F32),
        V((4, 528, 128), I16),
        V((4, 528, 128), I16),
        V((4, 512, 128), F32),
        V((3, 528, 128), I16),
        V((3, 528, 128), I16),
        V((4, 128, 128), F32),
        V((3, 144, 128), I16),
        V((3, 144, 128), I16),
        V((EMB, 8, 128), F32),
        V((EMB, 8, 128), F32),
        V((CENT, D_FIELD), F32),
        V((2, 4, 4, 16, 128), F32),
        V((4, 4, 16, 128), F32),
        V((3, 4, 16, 128), F32),
        V((3, 16, 128), F32),
        D((6,)),
    ]
    sems = [(16,), (16,), (16,), (2, 8), (2, 8), (16,), (16,), (8,), (3,), (), (4,), (3,), (3,), (16,), (), (3,), (3,), (3,), (3, 4), (4, 4)]
    for shape in sems:
        scratch += [D(shape), D(shape)] if shape else [D, D]
    scratch += [D((8, 1))]
    return pl.pallas_call(
        step_kernel,
        out_shape=jax.ShapeDtypeStruct((2, 4, 4, BLOCK, 128), I16),
        in_specs=[hbm] * 6,
        out_specs=hbm,
        scratch_shapes=scratch,
        compiler_params=pltpu.CompilerParams(
            collective_id=1, has_side_effects=True, vmem_limit_bytes=56 << 20
        ),
        name="train_step",
    )(codes, bag, book, w_in, w_out, labels)


def spread_kernel(gathered, weight, table, head, parts, rows, load_s, store_s):
    def load(a):
        return pltpu.make_async_copy(gathered.at[:, :, a], parts.at[a], load_s.at[a])

    def store(a):
        return pltpu.make_async_copy(rows.at[a], weight.at[pl.ds(a * 32, 32)], store_s.at[a])

    for a in range(4):
        load(a).start()
    for a in range(4):
        load(a).wait()
        for c in range(4):
            for yy in range(2):
                tail = number(parts[a, yy, c, 128:])
                scales = jnp.exp2(tail[8:] - 15.0)
                whole = number(parts[a, yy, c, :128]) * scales[1:2]
                for f in range(EMB):
                    spot = f * WIDE + yy * 128
                    rows[a, c * 8 : c * 8 + 8, spot : spot + 128] = whole[f * 8 : f * 8 + 8]
                gg = yy * ZED + a * 4 + c
                table[gg * 8 : gg * 8 + 8, :] = tail[:8] * scales[2:3]
                head[gg : gg + 1, :] = tail[8:9] * scales[3:4]
        store(a).start()
    for a in range(4):
        store(a).wait()


def spread(gathered):
    hbm = pl.BlockSpec(memory_space=pl.ANY)
    vmem = pl.BlockSpec(memory_space=pltpu.VMEM)
    return pl.pallas_call(
        spread_kernel,
        out_shape=(
            jax.ShapeDtypeStruct((D_FIELD, HID), F32),
            jax.ShapeDtypeStruct((CENT, D_FIELD), F32),
            jax.ShapeDtypeStruct((DENSE, 128), F32),
        ),
        in_specs=[hbm],
        out_specs=(hbm, vmem, vmem),
        scratch_shapes=[
            pltpu.VMEM((4, 2, 4, BLOCK, 128), I16),
            pltpu.VMEM((4, 32, HID), F32),
            pltpu.SemaphoreType.DMA((4,)),
            pltpu.SemaphoreType.DMA((4,)),
        ],
        compiler_params=pltpu.CompilerParams(vmem_limit_bytes=60 << 20),
        name="spread",
    )(gathered)


def body(codes, row_bag, codebook, w_in, w_out, labels):
    gathered = train(
        codes[0].T, row_bag, codebook[0], w_in, w_out.reshape(32, 128), labels.reshape(1, SAMP)
    )
    weight, table, head = spread(gathered)
    return table[None], weight, head.reshape(HID)


def solution(mesh):
    in_specs = (
        P("emb", "dense", None),
        P("emb", "dense"),
        P("emb", None, None),
        P("emb", None),
        P(),
        P("dense"),
    )
    out_specs = (P("emb", None, None), P("emb", None), P())
    return jax.shard_map(body, mesh=mesh, in_specs=in_specs, out_specs=out_specs, check_vma=False)
```

```python
import functools

import jax
import jax.numpy as jnp
from jax import lax
from jax.experimental import pallas as pl
from jax.experimental.pallas import tpu as pltpu
from jax.sharding import PartitionSpec as P

D_FIELD = 128
SUB = 16
SUBW = 8
CENT = 256
EMB = 16
DENSE = 32
ZED = 16
SAMP = 256
WIDE = 256
HID = 4096
F32 = jnp.float32
BF16 = jnp.bfloat16
F8 = jnp.float8_e4m3fn
I16 = jnp.int16
NT = (((1,), (1,)), ((), ()))
MESH = pl.DeviceIdType.MESH
BLOCK = 144
GROUP = 4


def encode(value):
    top = jnp.maximum(jnp.max(jnp.abs(value), axis=0, keepdims=True), 1e-30)
    power = jnp.ceil(jnp.log2(top) + 0.001)
    coded = jnp.floor(value * jnp.exp2(15.0 - power) + 0.5)
    return coded.astype(jnp.int32).astype(I16), power


def tile_of(power):
    return jnp.broadcast_to(power, (16, power.shape[1])).astype(jnp.int32).astype(I16)


def number(coded):
    return coded.astype(jnp.int32).astype(F32)


def decode(coded, power):
    return number(coded) * jnp.exp2(number(power)[:1] - 15.0)


def step_kernel(
    codes_hbm, bag_hbm, book_hbm, w_in, w_out_hbm, labels_hbm, out_hbm, out,
    codes, bag, book, w_out, labels, table_t, members, pooled, low, high,
    w_cols, w_turned, fields, fields32, turned, logits, heads,
    gp_own, gp_sib, gp_got, gp_out, gp_in, gq_out, gq_in, gp_sum,
    y_out, y_in, mine, near_out, near_in, two_out, two_in, acc, far_out, far_in, red, cols,
    table, tab, tab_y, tab_near, tab_far,
    local, w_s, w_r, wu_s, wu_r, wd_s, wd_r, f_s, f_r, sib_s, sib_r, lg_s, lg_r, hd_s, hd_r, gs_s, gs_r, gp_s, gp_r, gq_s, gq_r,
    y_s, y_r, n_s, n_r, two_s, two_r, fr_s, fr_r, a_s, a_r,
    ty_s, ty_r, tn_s, tn_r, tf_s, tf_r, of_s, of_r, on_s, on_r, oy_s, oy_r, kept,
):
    e = lax.axis_index("emb")
    g = lax.axis_index("dense")
    y = g // ZED
    z = lax.rem(g, ZED)
    zq = z // 4
    zr = lax.rem(z, 4)
    sib = e + 1 - 2 * lax.rem(e, 2)
    other = 1 - y

    def emb_at(i):
        return lax.rem(e + i, EMB)

    def emb_from(i):
        return lax.rem(e + EMB - i, EMB)

    def z_at(off):
        return (e, y * ZED + lax.rem(z + off + ZED, ZED))

    def send(src, dst, ss, rs, to):
        return pltpu.make_async_remote_copy(
            src_ref=src, dst_ref=dst, send_sem=ss, recv_sem=rs, device_id=to, device_id_type=MESH
        )

    def loop(lo, hi, body):
        def step(i, carry):
            body(i)
            return carry

        lax.fori_loop(lo, hi, step, 0)

    y_mate = (e, other * ZED + z)
    loads = [
        pltpu.make_async_copy(src, dst, local.at[1 + i])
        for i, (src, dst) in enumerate(
            ((bag_hbm, bag), (codes_hbm, codes), (book_hbm, book), (w_out_hbm, w_out), (labels_hbm, labels))
        )
    ]
    for load in loads:
        load.start()
    sent = []
    barrier = pltpu.get_barrier_semaphore()
    loop(1, EMB, lambda i: pl.semaphore_signal(barrier, inc=1, device_id=(emb_at(i), g), device_id_type=MESH))
    for off in (1, -1, 2, -2, 4, -4, 8):
        pl.semaphore_signal(barrier, inc=1, device_id=z_at(off), device_id_type=MESH)
    pl.semaphore_signal(barrier, inc=1, device_id=y_mate, device_id_type=MESH)

    half = lax.rem(z, 2)
    own_lanes = pl.ds(pl.multiple_of(half * 128, 128), 128)
    far_lanes = pl.ds(pl.multiple_of((1 - half) * 128, 128), 128)

    def w_copy(i):
        cols_of = pl.ds(pl.multiple_of(emb_at(i) * WIDE + half * 128, 128), 128)
        return send(w_in.at[:, cols_of], w_cols.at[e, :, own_lanes], w_s.at[i], w_r.at[i], (emb_at(i), g))

    def up_copy(i, lanes):
        part = w_cols.at[emb_from(i), pl.ds(0, 64), lanes]
        return send(part, part, wu_s.at[i], wu_r.at[i], z_at(1))

    def down_copy(i, lanes):
        part = w_cols.at[emb_from(i), pl.ds(64, 64), lanes]
        return send(part, part, wd_s.at[i], wd_r.at[i], z_at(-1))

    def pass_on(i):
        w_copy(i).wait_recv()
        up_copy(i, own_lanes).start()
        down_copy(i, own_lanes).start()

    pl.semaphore_wait(barrier, EMB - 1 + 8)
    loop(1, EMB, lambda i: w_copy(i).start())
    sent.append(lambda: loop(1, EMB, lambda i: w_copy(i).wait_send()))
    own_w = pltpu.make_async_copy(
        w_in.at[:, pl.ds(pl.multiple_of(e * WIDE, WIDE), WIDE)], w_cols.at[e], local.at[0]
    )
    own_w.start()

    def rows_of(f, h):
        return fields.at[f, pl.ds(h * 64, 64)]

    def f_copy(i, h):
        return send(rows_of(e, h), rows_of(e, h), f_s.at[h, i], f_r.at[h, i], (emb_at(2 * i), g))

    def sib_copy(i, h):
        f = lax.rem(e + 2 * EMB - 2 * i, EMB)
        return send(rows_of(f, h), rows_of(f, h), sib_s.at[h, i], sib_r.at[h, i], (sib, g))

    def onehot(row):
        ids = lax.broadcasted_iota(jnp.int32, (CENT, row.shape[1]), 0).astype(F32).astype(BF16)
        same = row.astype(F32).astype(BF16) == ids
        return jnp.where(same, jnp.ones((), BF16), jnp.zeros((), BF16)).astype(F8)

    for load in loads:
        load.wait()
    members[...] = onehot(bag[...])
    table_t[...] = book[...].astype(F32).T

    def count_step(step):
        at = step * GROUP
        picks = jnp.concatenate([onehot(codes[pl.ds(at + j, 1), :]) for j in range(GROUP)], axis=0)
        count = lax.dot_general(picks, members[...], NT, preferred_element_type=F32)
        upper = jnp.floor(count * (1.0 / 256.0))
        lower = (count - upper * 256.0).astype(BF16)
        upper = upper.astype(BF16)
        place = pl.ds(pl.multiple_of(at * CENT, CENT * GROUP), CENT * GROUP)
        low[place, :] = lower
        high[place, :] = upper
        rows = pl.ds(pl.multiple_of(at * SUBW, SUBW * GROUP), SUBW * GROUP)
        part = table_t[rows, :].astype(BF16)
        for j in range(GROUP):
            mine_at = slice(j * SUBW, (j + 1) * SUBW)
            span = slice(j * CENT, (j + 1) * CENT)
            pooled[pl.ds(pl.multiple_of((at + j) * SUBW, SUBW), SUBW), :] = jnp.dot(
                part[mine_at], lower[span], preferred_element_type=F32
            ) + 256.0 * jnp.dot(part[mine_at], upper[span], preferred_element_type=F32)

    def send_half(h):
        rows = pl.ds(h * 64, 64)
        fields[e, rows] = pooled[rows].astype(BF16)
        loop(1, 8, lambda i: f_copy(i, h).start())
        sib_copy(0, h).start()
        sent.append(lambda: loop(1, 8, lambda i: f_copy(i, h).wait_send()))
        sent.append(lambda: loop(0, 8, lambda i: sib_copy(i, h).wait_send()))

    loop(0, 1, count_step)

    def later_step(step):
        count_step(step)

        @pl.when(step == 1)
        def _():
            send_half(0)

    loop(1, 4, later_step)
    send_half(1)
    loop(1, EMB, pass_on)
    sent.append(lambda: loop(1, EMB, lambda i: up_copy(i, own_lanes).wait_send()))
    sent.append(lambda: loop(1, EMB, lambda i: down_copy(i, own_lanes).wait_send()))

    def forward(i, h):
        f_copy(i, h).wait_recv()
        sib_copy(i, h).start()

    for h in range(2):
        loop(1, 8, lambda i: forward(i, h))

    def turn(f):
        w_turned[:, pl.ds(pl.multiple_of(f * D_FIELD, D_FIELD), D_FIELD)] = w_cols[f].T

    def take(i):
        up_copy(i, far_lanes).wait_recv()
        down_copy(i, far_lanes).wait_recv()
        turn(emb_from(i))

    own_w.wait()
    turn(e)
    loop(1, EMB, take)
    for h in range(2):
        loop(0, 8, lambda i: sib_copy(i, h).wait_recv())
    pre = jnp.dot(w_turned[...], fields[...].reshape(EMB * D_FIELD, SAMP), preferred_element_type=F32)
    gate = jax.nn.sigmoid(pre)
    act = pre * gate
    w_row = jnp.concatenate([w_out[pl.ds(2 * e, 1), :], w_out[pl.ds(2 * e + 1, 1), :]], axis=1)
    w_rows = jnp.broadcast_to(w_row, (8, WIDE))
    logits[e] = jnp.dot(w_rows, act, precision=lax.Precision.HIGHEST, preferred_element_type=F32)

    def lg_copy(i):
        return send(logits.at[e], logits.at[e], lg_s.at[i], lg_r.at[i], (emb_at(i), g))

    loop(1, EMB, lambda i: lg_copy(i).start())
    sent.append(lambda: loop(1, EMB, lambda i: lg_copy(i).wait_send()))

    for f in range(EMB):
        fields32[:, f] = fields[f].astype(F32).reshape(16, 8, SAMP)
    for c in range(4):
        for a in range(4):
            turned[c, a * 128 : (a + 1) * 128] = fields32[a * 4 + c].reshape(128, SAMP).astype(BF16)
    slant = gate + pre * gate * (1.0 - gate)
    w_left = jnp.broadcast_to(w_row[:, :128], (128, 128)).T
    w_right = jnp.broadcast_to(w_row[:, 128:], (128, 128)).T
    w_tall = jnp.concatenate([w_left, w_right], axis=0)
    w_tall = jnp.concatenate([w_tall, w_tall], axis=1)

    loop(1, EMB, lambda i: lg_copy(i).wait_recv())
    logit = logits[0]
    for f in range(1, EMB):
        logit = logit + logits[f]
    slope = jax.nn.sigmoid(logit) - labels[...]
    grad = (slope[:1] * w_tall * slant).astype(BF16)
    halves = (grad[:128], grad[128:])

    def grad_half(c, half):
        rhs = jnp.where(half == 0, halves[0], halves[1])
        return lax.dot_general(turned[c], rhs, NT, preferred_element_type=F32)

    def y_copy(k, c):
        return send(y_out.at[c], y_in.at[c], y_s.at[k], y_r.at[k], y_mate)

    near = (2, 1, -1)
    order = [lax.rem(z + off + 4, 4) for off in near] + [zr]
    for k, c in enumerate(order):
        coded, power = encode(grad_half(c, other))
        y_out[c, :512] = coded
        y_out[c, 512:] = tile_of(power)
        y_copy(k, c).start()
        sent.append(lambda k=k, c=c: y_copy(k, c).wait_send())
    head = lax.dot_general(slope, act, NT, precision=lax.Precision.HIGHEST, preferred_element_type=F32)
    heads[e] = jnp.concatenate([head[:1, :128], head[:1, 128:], jnp.zeros((6, 128), F32)], axis=0)

    def hd_copy(i):
        return send(heads.at[e], heads.at[e], hd_s.at[i], hd_r.at[i], (emb_at(i), g))

    loop(1, EMB, lambda i: hd_copy(i).start())
    sent.append(lambda: loop(1, EMB, lambda i: hd_copy(i).wait_send()))

    core = lax.rem(e, 2)

    def gs_copy(i):
        return send(gp_sib.at[i], gp_got.at[i], gs_s.at[i], gs_r.at[i], (sib, g))

    def gs_start(i):
        gp_sib[i] = jnp.dot(w_cols[2 * i + 1 - core], grad, preferred_element_type=F32)
        gs_copy(i).start()

    loop(0, 8, gs_start)
    sent.append(lambda: loop(0, 8, lambda i: gs_copy(i).wait_send()))

    def gp_part(i):
        gp_own[i] = jnp.dot(w_cols[2 * i + core], grad, preferred_element_type=F32)

    loop(0, 8, gp_part)
    chip = e // 2
    y_high = chip // 4
    col = lax.rem(chip, 4)

    def gp_copy(i):
        to = (y_high * 8 + 2 * lax.rem(col + i, 4) + core, g)
        return send(gp_out.at[i - 1], gp_in.at[i - 1], gp_s.at[i - 1], gp_r.at[i - 1], to)

    def gp_start(i):
        for h in range(2):
            c = h * 4 + lax.rem(col + i, 4)
            gs_copy(c).wait_recv()
            coded, power = encode(gp_own[c] + gp_got[c])
            gp_out[i - 1, h, :D_FIELD] = coded
            gp_out[i - 1, h, D_FIELD:] = tile_of(power)
        gp_copy(i).start()

    loop(1, 4, gp_start)
    sent.append(lambda: loop(1, 4, lambda i: gp_copy(i).wait_send()))
    for h in range(2):
        gs_copy(h * 4 + col).wait_recv()
    for k, c in enumerate(order):
        mine[c] = grad_half(c, y)

    def near_copy(k):
        return send(near_out.at[k - 1], near_in.at[k - 1], n_s.at[k - 1], n_r.at[k - 1], z_at(near[k]))

    def two_copy(h):
        return send(two_out.at[h], two_in.at[h], two_s.at[h], two_r.at[h], z_at(2 - 4 * h))

    for k in range(3):
        c = order[k]
        y_copy(k, c).wait_recv()
        pair = mine[c] + decode(y_in[c, :512], y_in[c, 512:])
        if k == 0:
            for h in range(2):
                coded, power = encode(pair[h * 256 : h * 256 + 256])
                two_out[h, :256] = coded
                two_out[h, 256:] = tile_of(power)
                two_copy(h).start()
                sent.append(lambda h=h: two_copy(h).wait_send())
        else:
            coded, power = encode(pair)
            near_out[k - 1, :512] = coded
            near_out[k - 1, 512:] = tile_of(power)
            near_copy(k).start()
            sent.append(lambda k=k: near_copy(k).wait_send())
    y_copy(3, zr).wait_recv()
    acc[...] = (mine[zr] + decode(y_in[zr, :512], y_in[zr, 512:])).reshape(4, 128, 128)

    loop(1, 4, lambda i: gp_copy(i).wait_recv())

    def row_sum(h):
        total = gp_own[h * 4 + col] + gp_got[h * 4 + col]
        for i in range(3):
            total = total + decode(gp_in[i, h, :D_FIELD], gp_in[i, h, D_FIELD:])
        return total

    coded, power = encode(row_sum(1 - y_high))
    gq_out[:D_FIELD] = coded
    gq_out[D_FIELD:] = tile_of(power)
    gq_copy = send(gq_out, gq_in, gq_s, gq_r, (emb_at(8), g))
    gq_copy.start()
    sent.append(lambda: gq_copy.wait_send())
    gp_sum[...] = row_sum(y_high)

    for h in range(2):
        two_copy(h).wait_recv()
        two = slice(h * 2, h * 2 + 2)
        acc[two] = acc[two] + decode(two_in[h, :256], two_in[h, 256:]).reshape(2, 128, 128)
    for k in (1, 2):
        near_copy(k).wait_recv()
        acc[...] = acc[...] + decode(near_in[k - 1, :512], near_in[k - 1, 512:]).reshape(4, 128, 128)

    def far_copy(m):
        return send(far_out.at[m - 1], far_in.at[m - 1], fr_s.at[m - 1], fr_r.at[m - 1], z_at(4 * m))

    for m in (2, 1, 3):
        coded, power = encode(acc[lax.rem(zq + m, 4)])
        far_out[m - 1, :128] = coded
        far_out[m - 1, 128:] = tile_of(power)
        far_copy(m).start()
        sent.append(lambda m=m: far_copy(m).wait_send())

    gq_copy.wait_recv()
    grad_pool = (gp_sum[...] + decode(gq_in[:D_FIELD], gq_in[D_FIELD:])).astype(BF16)
    subs = lax.broadcasted_iota(jnp.int32, (CENT, D_FIELD), 1) // SUBW
    table[...] = jnp.zeros((CENT, D_FIELD), F32)

    def table_step(step):
        place = pl.ds(pl.multiple_of(step * GROUP * CENT, GROUP * CENT), GROUP * CENT)
        got = lax.dot_general(low[place, :], grad_pool, NT, preferred_element_type=F32)
        got = got + 256.0 * lax.dot_general(high[place, :], grad_pool, NT, preferred_element_type=F32)
        for j in range(GROUP):
            part = got[j * CENT : (j + 1) * CENT]
            table[...] = table[...] + jnp.where(subs == step * GROUP + j, part, 0.0)

    loop(0, SUB // GROUP, table_step)
    loop(1, EMB, lambda i: hd_copy(i).wait_recv())
    for yy in range(2):
        for zz in range(ZED):
            gg = yy * ZED + zz
            tab[yy, zz % 4, zz // 4, :8] = table[gg * 8 : gg * 8 + 8]
            tab[yy, zz % 4, zz // 4, 8:] = jnp.concatenate(
                [heads[gg // 2, gg % 2 : gg % 2 + 1], jnp.zeros((7, 128), F32)], axis=0
            )
    ty_copy = send(tab.at[other], tab_y, ty_s, ty_r, y_mate)
    ty_copy.start()
    sent.append(lambda: ty_copy.wait_send())
    ty_copy.wait_recv()
    tab[y] = tab[y] + tab_y[...]

    def tn_copy(k):
        return send(tab.at[y, order[k]], tab_near.at[k], tn_s.at[k], tn_r.at[k], z_at(near[k]))

    for k in range(3):
        tn_copy(k).start()
        sent.append(lambda k=k: tn_copy(k).wait_send())
    for k in range(3):
        tn_copy(k).wait_recv()
    tab[y, zr] = tab[y, zr] + tab_near[0] + tab_near[1] + tab_near[2]

    def tf_copy(m):
        return send(
            tab.at[y, zr, lax.rem(zq + m, 4)], tab_far.at[m - 1], tf_s.at[m - 1], tf_r.at[m - 1], z_at(4 * m)
        )

    for m in range(1, 4):
        tf_copy(m).start()
        sent.append(lambda m=m: tf_copy(m).wait_send())

    whole = acc[zq]
    for m in range(1, 4):
        far_copy(m).wait_recv()
        whole = whole + decode(far_in[m - 1, :128], far_in[m - 1, 128:])
    red[...] = whole.reshape(EMB, 8, 128)

    def a_copy(i):
        return send(red.at[emb_at(i)], cols.at[e], a_s.at[i], a_r.at[i], (emb_at(i), g))

    loop(1, EMB, lambda i: a_copy(i).start())
    sent.append(lambda: loop(1, EMB, lambda i: a_copy(i).wait_send()))
    cols[e] = red[e]

    for m in range(1, 4):
        tf_copy(m).wait_recv()
    tab_whole = tab[y, zr, zq] + tab_far[0] + tab_far[1] + tab_far[2]
    tab_code, tab_power = encode(tab_whole[:8])
    head_code, head_power = encode(tab_whole[8:])
    loop(1, EMB, lambda i: a_copy(i).wait_recv())
    coded, power = encode(cols[...].reshape(128, 128))
    spots = lax.broadcasted_iota(jnp.int32, (16, 128), 0)
    tail = jnp.concatenate([number(tab_code), number(head_code)], axis=0)
    for at, row in ((9, power), (10, tab_power), (11, head_power)):
        tail = jnp.where(spots == at, row, tail)
    out[y, zr, zq, :128] = coded
    out[y, zr, zq, 128:] = tail.astype(jnp.int32).astype(I16)
    def block(off, m):
        src = lax.rem(z + 2 * ZED - off - 4 * m, ZED)
        return out.at[y, lax.rem(src, 4), src // 4]

    def of_copy(m):
        return send(block(0, 0), block(0, 0), of_s.at[m - 1], of_r.at[m - 1], z_at(4 * m))

    def of_wait(m):
        send(block(0, m), block(0, m), of_s.at[m - 1], of_r.at[m - 1], z_at(4 * m)).wait_recv()

    ways = (1, -1, 2)

    def on_copy(k, m):
        return send(block(0, m), block(0, m), on_s.at[k, m], on_r.at[k, m], z_at(ways[k]))

    def on_wait(k, m):
        got = block(ways[k], m)
        send(got, got, on_s.at[k, m], on_r.at[k, m], z_at(ways[k])).wait_recv()

    chain = ((1, 0), (1, 1), (-1, 0), (-1, 3))

    def ch_copy(i):
        way, m = chain[i]
        return send(block(way, m), block(way, m), on_s.at[2, i], on_r.at[2, i], z_at(way))

    def ch_block(i):
        way, m = chain[i]
        return block(2 * way, m)

    def ch_wait(i):
        send(ch_block(i), ch_block(i), on_s.at[2, i], on_r.at[2, i], z_at(chain[i][0])).wait_recv()

    def oy_copy(k, m):
        got = ch_block(m) if k == 3 else block(0 if k == 0 else ways[k - 1], m)
        return send(got, got, oy_s.at[k, m], oy_r.at[k, m], y_mate)

    def oy_wait(k, m):
        off, at = (2 * chain[m][0], chain[m][1]) if k == 3 else (0 if k == 0 else ways[k - 1], m)
        src = lax.rem(z + 2 * ZED - off - 4 * at, ZED)
        got = out.at[other, lax.rem(src, 4), src // 4]
        send(got, got, oy_s.at[k, m], oy_r.at[k, m], y_mate).wait_recv()

    def put(copy):
        copy.start()
        sent.append(copy.wait_send)

    turns = (0, 1, 3, 2)
    for m in (2, 1, 3):
        put(of_copy(m))
    for m in turns:
        if m:
            of_wait(m)
        put(on_copy(0, m))
        put(on_copy(1, m))
        put(oy_copy(0, m))
    for m in turns:
        on_wait(0, m)
        if (1, m) in chain:
            put(ch_copy(chain.index((1, m))))
        put(oy_copy(1, m))
        on_wait(1, m)
        if (-1, m) in chain:
            put(ch_copy(chain.index((-1, m))))
        put(oy_copy(2, m))
    for i in (0, 2, 1, 3):
        ch_wait(i)
        put(oy_copy(3, i))
    def keep_all(yy, c, n):
        pltpu.make_async_copy(out.at[yy, c], out_hbm.at[yy, c], kept.at[n, 0]).start()
        sent.append(lambda: pltpu.make_async_copy(out.at[yy, c], out_hbm.at[yy, c], kept.at[n, 0]).wait())

    for c in range(4):
        keep_all(y, c, c)
    for k in range(4):
        for m in range(4):
            oy_wait(k, m)
        off = 0 if k == 0 else ways[k - 1]
        keep_all(other, lax.rem(z + ZED - off, 4), 4 + k)
    for wait in sent:
        wait()


def train(codes, bag, book, w_in, w_out, labels):
    hbm = pl.BlockSpec(memory_space=pl.ANY)
    V, D = pltpu.VMEM, pltpu.SemaphoreType.DMA
    rows = codes.shape[1]
    scratch = [
        V((2, 4, 4, BLOCK, 128), I16),
        V((SUB, rows), jnp.int32),
        V((1, rows), jnp.int32),
        V((CENT, D_FIELD), BF16),
        V((32, 128), F32),
        V((1, SAMP), F32),
        V((D_FIELD, CENT), F32),
        V((SAMP, rows), F8),
        V((D_FIELD, SAMP), F32),
        V((SUB * CENT, SAMP), BF16),
        V((SUB * CENT, SAMP), BF16),
        V((EMB, D_FIELD, WIDE), BF16),
        V((WIDE, EMB * D_FIELD), BF16),
        V((EMB, D_FIELD, SAMP), BF16),
        V((16, EMB, 8, SAMP), F32),
        V((4, 512, SAMP), BF16),
        V((EMB, 8, SAMP), F32),
        V((EMB, 8, 128), F32),
        V((8, D_FIELD, SAMP), F32),
        V((8, D_FIELD, SAMP), F32),
        V((8, D_FIELD, SAMP), F32),
        V((3, 2, D_FIELD + 16, SAMP), I16),
        V((3, 2, D_FIELD + 16, SAMP), I16),
        V((D_FIELD + 16, SAMP), I16),
        V((D_FIELD + 16, SAMP), I16),
        V((D_FIELD, SAMP), F32),
        V((4, 528, 128), I16),
        V((4, 528, 128), I16),
        V((4, 512, 128), F32),
        V((2, 528, 128), I16),
        V((2, 528, 128), I16),
        V((2, 272, 128), I16),
        V((2, 272, 128), I16),
        V((4, 128, 128), F32),
        V((3, 144, 128), I16),
        V((3, 144, 128), I16),
        V((EMB, 8, 128), F32),
        V((EMB, 8, 128), F32),
        V((CENT, D_FIELD), F32),
        V((2, 4, 4, 16, 128), F32),
        V((4, 4, 16, 128), F32),
        V((3, 4, 16, 128), F32),
        V((3, 16, 128), F32),
        D((6,)),
    ]
    sems = [(16,), (16,), (16,), (2, 8), (2, 8), (16,), (16,), (8,), (3,), (), (4,), (2,), (2,), (3,), (16,), (), (3,), (3,), (3,), (3, 4), (4, 4)]
    for shape in sems:
        scratch += [D(shape), D(shape)] if shape else [D, D]
    scratch += [D((8, 1))]
    return pl.pallas_call(
        step_kernel,
        out_shape=jax.ShapeDtypeStruct((2, 4, 4, BLOCK, 128), I16),
        in_specs=[hbm] * 6,
        out_specs=hbm,
        scratch_shapes=scratch,
        compiler_params=pltpu.CompilerParams(
            collective_id=1, has_side_effects=True, vmem_limit_bytes=56 << 20
        ),
        name="train_step",
    )(codes, bag, book, w_in, w_out, labels)


def spread_kernel(gathered, weight, table, head, parts, rows, load_s, store_s):
    def load(a):
        return pltpu.make_async_copy(gathered.at[:, :, a], parts.at[a], load_s.at[a])

    def store(a):
        return pltpu.make_async_copy(rows.at[a], weight.at[pl.ds(a * 32, 32)], store_s.at[a])

    for a in range(4):
        load(a).start()
    for a in range(4):
        load(a).wait()
        for c in range(4):
            for yy in range(2):
                tail = number(parts[a, yy, c, 128:])
                scales = jnp.exp2(tail[8:] - 15.0)
                whole = number(parts[a, yy, c, :128]) * scales[1:2]
                for f in range(EMB):
                    spot = f * WIDE + yy * 128
                    rows[a, c * 8 : c * 8 + 8, spot : spot + 128] = whole[f * 8 : f * 8 + 8]
                gg = yy * ZED + a * 4 + c
                table[gg * 8 : gg * 8 + 8, :] = tail[:8] * scales[2:3]
                head[gg : gg + 1, :] = tail[8:9] * scales[3:4]
        store(a).start()
    for a in range(4):
        store(a).wait()


def spread(gathered):
    hbm = pl.BlockSpec(memory_space=pl.ANY)
    vmem = pl.BlockSpec(memory_space=pltpu.VMEM)
    return pl.pallas_call(
        spread_kernel,
        out_shape=(
            jax.ShapeDtypeStruct((D_FIELD, HID), F32),
            jax.ShapeDtypeStruct((CENT, D_FIELD), F32),
            jax.ShapeDtypeStruct((DENSE, 128), F32),
        ),
        in_specs=[hbm],
        out_specs=(hbm, vmem, vmem),
        scratch_shapes=[
            pltpu.VMEM((4, 2, 4, BLOCK, 128), I16),
            pltpu.VMEM((4, 32, HID), F32),
            pltpu.SemaphoreType.DMA((4,)),
            pltpu.SemaphoreType.DMA((4,)),
        ],
        compiler_params=pltpu.CompilerParams(vmem_limit_bytes=60 << 20),
        name="spread",
    )(gathered)


def body(codes, row_bag, codebook, w_in, w_out, labels):
    gathered = train(
        codes[0].T, row_bag, codebook[0], w_in, w_out.reshape(32, 128), labels.reshape(1, SAMP)
    )
    weight, table, head = spread(gathered)
    return table[None], weight, head.reshape(HID)


def solution(mesh):
    in_specs = (
        P("emb", "dense", None),
        P("emb", "dense"),
        P("emb", None, None),
        P("emb", None),
        P(),
        P("dense"),
    )
    out_specs = (P("emb", None, None), P("emb", None), P())
    return jax.shard_map(body, mesh=mesh, in_specs=in_specs, out_specs=out_specs, check_vma=False)
```

```python
import functools

import jax
import jax.numpy as jnp
from jax import lax
from jax.experimental import pallas as pl
from jax.experimental.pallas import tpu as pltpu
from jax.sharding import PartitionSpec as P

D_FIELD = 128
SUB = 16
SUBW = 8
CENT = 256
EMB = 16
DENSE = 32
ZED = 16
SAMP = 256
WIDE = 256
HID = 4096
F32 = jnp.float32
BF16 = jnp.bfloat16
F8 = jnp.float8_e4m3fn
I16 = jnp.int16
NT = (((1,), (1,)), ((), ()))
MESH = pl.DeviceIdType.MESH
BLOCK = 144
GROUP = 4


def encode(value):
    top = jnp.maximum(jnp.max(jnp.abs(value), axis=0, keepdims=True), 1e-30)
    power = jnp.ceil(jnp.log2(top) + 0.001)
    coded = jnp.floor(value * jnp.exp2(15.0 - power) + 0.5)
    return coded.astype(jnp.int32).astype(I16), power


def tile_of(power):
    return jnp.broadcast_to(power, (16, power.shape[1])).astype(jnp.int32).astype(I16)


def number(coded):
    return coded.astype(jnp.int32).astype(F32)


def decode(coded, power):
    return number(coded) * jnp.exp2(number(power)[:1] - 15.0)


def step_kernel(
    codes_hbm, bag_hbm, book_hbm, w_in, w_out_hbm, labels_hbm, out_hbm, out,
    codes, bag, book, w_out, labels, table_t, members, pooled, low, high,
    w_cols, w_turned, fields, fields32, turned, logits, heads,
    gp_own, gp_sib, gp_got, gp_out, gp_in, gq_out, gq_in, gp_sum,
    y_out, y_in, mine, near_out, near_in, acc, far_out, far_in, red, cols,
    table, tab, tab_y, tab_near, tab_far,
    local, w_s, w_r, wu_s, wu_r, wd_s, wd_r, f_s, f_r, sib_s, sib_r, lg_s, lg_r, hd_s, hd_r, gs_s, gs_r, gp_s, gp_r, gq_s, gq_r,
    y_s, y_r, n_s, n_r, fr_s, fr_r, a_s, a_r,
    ty_s, ty_r, tn_s, tn_r, tf_s, tf_r, of_s, of_r, on_s, on_r, oy_s, oy_r, kept,
):
    e = lax.axis_index("emb")
    g = lax.axis_index("dense")
    y = g // ZED
    z = lax.rem(g, ZED)
    zq = z // 4
    zr = lax.rem(z, 4)
    sib = e + 1 - 2 * lax.rem(e, 2)
    other = 1 - y

    def emb_at(i):
        return lax.rem(e + i, EMB)

    def emb_from(i):
        return lax.rem(e + EMB - i, EMB)

    def z_at(off):
        return (e, y * ZED + lax.rem(z + off + ZED, ZED))

    def send(src, dst, ss, rs, to):
        return pltpu.make_async_remote_copy(
            src_ref=src, dst_ref=dst, send_sem=ss, recv_sem=rs, device_id=to, device_id_type=MESH
        )

    def loop(lo, hi, body):
        def step(i, carry):
            body(i)
            return carry

        lax.fori_loop(lo, hi, step, 0)

    y_mate = (e, other * ZED + z)
    loads = [
        pltpu.make_async_copy(src, dst, local.at[1 + i])
        for i, (src, dst) in enumerate(
            ((bag_hbm, bag), (codes_hbm, codes), (book_hbm, book), (w_out_hbm, w_out), (labels_hbm, labels))
        )
    ]
    for load in loads:
        load.start()
    sent = []
    barrier = pltpu.get_barrier_semaphore()
    loop(1, EMB, lambda i: pl.semaphore_signal(barrier, inc=1, device_id=(emb_at(i), g), device_id_type=MESH))
    for off in (1, -1, 2, -2, 4, -4, 8):
        pl.semaphore_signal(barrier, inc=1, device_id=z_at(off), device_id_type=MESH)
    pl.semaphore_signal(barrier, inc=1, device_id=y_mate, device_id_type=MESH)

    half = lax.rem(z, 2)
    own_lanes = pl.ds(pl.multiple_of(half * 128, 128), 128)
    far_lanes = pl.ds(pl.multiple_of((1 - half) * 128, 128), 128)

    def w_copy(i):
        cols_of = pl.ds(pl.multiple_of(emb_at(i) * WIDE + half * 128, 128), 128)
        return send(w_in.at[:, cols_of], w_cols.at[e, :, own_lanes], w_s.at[i], w_r.at[i], (emb_at(i), g))

    def up_copy(i, lanes):
        part = w_cols.at[emb_from(i), pl.ds(0, 64), lanes]
        return send(part, part, wu_s.at[i], wu_r.at[i], z_at(1))

    def down_copy(i, lanes):
        part = w_cols.at[emb_from(i), pl.ds(64, 64), lanes]
        return send(part, part, wd_s.at[i], wd_r.at[i], z_at(-1))

    def pass_on(i):
        w_copy(i).wait_recv()
        up_copy(i, own_lanes).start()
        down_copy(i, own_lanes).start()

    pl.semaphore_wait(barrier, EMB - 1 + 8)
    loop(1, EMB, lambda i: w_copy(i).start())
    sent.append(lambda: loop(1, EMB, lambda i: w_copy(i).wait_send()))
    own_w = pltpu.make_async_copy(
        w_in.at[:, pl.ds(pl.multiple_of(e * WIDE, WIDE), WIDE)], w_cols.at[e], local.at[0]
    )
    own_w.start()

    def rows_of(f, h):
        return fields.at[f, pl.ds(h * 64, 64)]

    def f_copy(i, h):
        return send(rows_of(e, h), rows_of(e, h), f_s.at[h, i], f_r.at[h, i], (emb_at(2 * i), g))

    def sib_copy(i, h):
        f = lax.rem(e + 2 * EMB - 2 * i, EMB)
        return send(rows_of(f, h), rows_of(f, h), sib_s.at[h, i], sib_r.at[h, i], (sib, g))

    def onehot(row):
        ids = lax.broadcasted_iota(jnp.int32, (CENT, row.shape[1]), 0).astype(F32).astype(BF16)
        same = row.astype(F32).astype(BF16) == ids
        return jnp.where(same, jnp.ones((), BF16), jnp.zeros((), BF16)).astype(F8)

    for load in loads:
        load.wait()
    members[...] = onehot(bag[...])
    table_t[...] = book[...].astype(F32).T

    def count_step(step):
        at = step * GROUP
        picks = jnp.concatenate([onehot(codes[pl.ds(at + j, 1), :]) for j in range(GROUP)], axis=0)
        count = lax.dot_general(picks, members[...], NT, preferred_element_type=F32)
        upper = jnp.floor(count * (1.0 / 256.0))
        lower = (count - upper * 256.0).astype(BF16)
        upper = upper.astype(BF16)
        place = pl.ds(pl.multiple_of(at * CENT, CENT * GROUP), CENT * GROUP)
        low[place, :] = lower
        high[place, :] = upper
        rows = pl.ds(pl.multiple_of(at * SUBW, SUBW * GROUP), SUBW * GROUP)
        part = table_t[rows, :].astype(BF16)
        for j in range(GROUP):
            mine_at = slice(j * SUBW, (j + 1) * SUBW)
            span = slice(j * CENT, (j + 1) * CENT)
            pooled[pl.ds(pl.multiple_of((at + j) * SUBW, SUBW), SUBW), :] = jnp.dot(
                part[mine_at], lower[span], preferred_element_type=F32
            ) + 256.0 * jnp.dot(part[mine_at], upper[span], preferred_element_type=F32)

    def send_half(h):
        rows = pl.ds(h * 64, 64)
        fields[e, rows] = pooled[rows].astype(BF16)
        loop(1, 8, lambda i: f_copy(i, h).start())
        sib_copy(0, h).start()
        sent.append(lambda: loop(1, 8, lambda i: f_copy(i, h).wait_send()))
        sent.append(lambda: loop(0, 8, lambda i: sib_copy(i, h).wait_send()))

    loop(0, 1, count_step)

    def later_step(step):
        count_step(step)

        @pl.when(step == 1)
        def _():
            send_half(0)

    loop(1, 4, later_step)
    send_half(1)
    loop(1, EMB, pass_on)
    sent.append(lambda: loop(1, EMB, lambda i: up_copy(i, own_lanes).wait_send()))
    sent.append(lambda: loop(1, EMB, lambda i: down_copy(i, own_lanes).wait_send()))

    def forward(i, h):
        f_copy(i, h).wait_recv()
        sib_copy(i, h).start()

    for h in range(2):
        loop(1, 8, lambda i: forward(i, h))

    def turn(f):
        w_turned[:, pl.ds(pl.multiple_of(f * D_FIELD, D_FIELD), D_FIELD)] = w_cols[f].T

    def take(i):
        up_copy(i, far_lanes).wait_recv()
        down_copy(i, far_lanes).wait_recv()
        turn(emb_from(i))

    own_w.wait()
    turn(e)
    loop(1, EMB, take)
    for h in range(2):
        loop(0, 8, lambda i: sib_copy(i, h).wait_recv())
    pre = jnp.dot(w_turned[...], fields[...].reshape(EMB * D_FIELD, SAMP), preferred_element_type=F32)
    gate = jax.nn.sigmoid(pre)
    act = pre * gate
    w_row = jnp.concatenate([w_out[pl.ds(2 * e, 1), :], w_out[pl.ds(2 * e + 1, 1), :]], axis=1)
    w_rows = jnp.broadcast_to(w_row, (8, WIDE))
    logits[e] = jnp.dot(w_rows, act, precision=lax.Precision.HIGHEST, preferred_element_type=F32)

    def lg_copy(i):
        return send(logits.at[e], logits.at[e], lg_s.at[i], lg_r.at[i], (emb_at(i), g))

    loop(1, EMB, lambda i: lg_copy(i).start())
    sent.append(lambda: loop(1, EMB, lambda i: lg_copy(i).wait_send()))

    for f in range(EMB):
        fields32[:, f] = fields[f].astype(F32).reshape(16, 8, SAMP)
    for c in range(4):
        for a in range(4):
            turned[c, a * 128 : (a + 1) * 128] = fields32[a * 4 + c].reshape(128, SAMP).astype(BF16)
    slant = gate + pre * gate * (1.0 - gate)
    w_left = jnp.broadcast_to(w_row[:, :128], (128, 128)).T
    w_right = jnp.broadcast_to(w_row[:, 128:], (128, 128)).T
    w_tall = jnp.concatenate([w_left, w_right], axis=0)
    w_tall = jnp.concatenate([w_tall, w_tall], axis=1)

    loop(1, EMB, lambda i: lg_copy(i).wait_recv())
    logit = logits[0]
    for f in range(1, EMB):
        logit = logit + logits[f]
    slope = jax.nn.sigmoid(logit) - labels[...]
    grad = (slope[:1] * w_tall * slant).astype(BF16)
    halves = (grad[:128], grad[128:])

    def grad_half(c, half):
        rhs = jnp.where(half == 0, halves[0], halves[1])
        return lax.dot_general(turned[c], rhs, NT, preferred_element_type=F32)

    def y_copy(k, c):
        return send(y_out.at[c], y_in.at[c], y_s.at[k], y_r.at[k], y_mate)

    near = (2, 1, -1)
    order = [lax.rem(z + off + 4, 4) for off in near] + [zr]
    for k, c in enumerate(order):
        coded, power = encode(grad_half(c, other))
        y_out[c, :512] = coded
        y_out[c, 512:] = tile_of(power)
        y_copy(k, c).start()
        sent.append(lambda k=k, c=c: y_copy(k, c).wait_send())
    core = lax.rem(e, 2)

    def gs_copy(i):
        return send(gp_sib.at[i], gp_got.at[i], gs_s.at[i], gs_r.at[i], (sib, g))

    def gs_start(i):
        gp_sib[i] = jnp.dot(w_cols[2 * i + 1 - core], grad, preferred_element_type=F32)
        gs_copy(i).start()

    loop(0, 8, gs_start)
    sent.append(lambda: loop(0, 8, lambda i: gs_copy(i).wait_send()))

    def gp_part(i):
        gp_own[i] = jnp.dot(w_cols[2 * i + core], grad, preferred_element_type=F32)

    loop(0, 8, gp_part)
    chip = e // 2
    y_high = chip // 4
    col = lax.rem(chip, 4)

    def gp_copy(i):
        to = (y_high * 8 + 2 * lax.rem(col + i, 4) + core, g)
        return send(gp_out.at[i - 1], gp_in.at[i - 1], gp_s.at[i - 1], gp_r.at[i - 1], to)

    def gp_start(i):
        for h in range(2):
            c = h * 4 + lax.rem(col + i, 4)
            gs_copy(c).wait_recv()
            coded, power = encode(gp_own[c] + gp_got[c])
            gp_out[i - 1, h, :D_FIELD] = coded
            gp_out[i - 1, h, D_FIELD:] = tile_of(power)
        gp_copy(i).start()

    loop(1, 4, gp_start)
    sent.append(lambda: loop(1, 4, lambda i: gp_copy(i).wait_send()))
    for h in range(2):
        gs_copy(h * 4 + col).wait_recv()
    head = lax.dot_general(slope, act, NT, precision=lax.Precision.HIGHEST, preferred_element_type=F32)
    heads[e] = jnp.concatenate([head[:1, :128], head[:1, 128:], jnp.zeros((6, 128), F32)], axis=0)

    def hd_copy(i):
        return send(heads.at[e], heads.at[e], hd_s.at[i], hd_r.at[i], (emb_at(i), g))

    loop(1, EMB, lambda i: hd_copy(i).start())
    sent.append(lambda: loop(1, EMB, lambda i: hd_copy(i).wait_send()))

    for k, c in enumerate(order):
        mine[c] = grad_half(c, y)

    def near_copy(k):
        return send(near_out.at[k], near_in.at[k], n_s.at[k], n_r.at[k], z_at(near[k]))

    for k in range(3):
        c = order[k]
        y_copy(k, c).wait_recv()
        coded, power = encode(mine[c] + decode(y_in[c, :512], y_in[c, 512:]))
        near_out[k, :512] = coded
        near_out[k, 512:] = tile_of(power)
        near_copy(k).start()
        sent.append(lambda k=k: near_copy(k).wait_send())
    y_copy(3, zr).wait_recv()
    acc[...] = (mine[zr] + decode(y_in[zr, :512], y_in[zr, 512:])).reshape(4, 128, 128)

    loop(1, 4, lambda i: gp_copy(i).wait_recv())

    def row_sum(h):
        total = gp_own[h * 4 + col] + gp_got[h * 4 + col]
        for i in range(3):
            total = total + decode(gp_in[i, h, :D_FIELD], gp_in[i, h, D_FIELD:])
        return total

    coded, power = encode(row_sum(1 - y_high))
    gq_out[:D_FIELD] = coded
    gq_out[D_FIELD:] = tile_of(power)
    gq_copy = send(gq_out, gq_in, gq_s, gq_r, (emb_at(8), g))
    gq_copy.start()
    sent.append(lambda: gq_copy.wait_send())
    gp_sum[...] = row_sum(y_high)

    for k in range(3):
        near_copy(k).wait_recv()
        acc[...] = acc[...] + decode(near_in[k, :512], near_in[k, 512:]).reshape(4, 128, 128)

    def far_copy(m):
        return send(far_out.at[m - 1], far_in.at[m - 1], fr_s.at[m - 1], fr_r.at[m - 1], z_at(4 * m))

    for m in (2, 1, 3):
        coded, power = encode(acc[lax.rem(zq + m, 4)])
        far_out[m - 1, :128] = coded
        far_out[m - 1, 128:] = tile_of(power)
        far_copy(m).start()
        sent.append(lambda m=m: far_copy(m).wait_send())

    gq_copy.wait_recv()
    grad_pool = (gp_sum[...] + decode(gq_in[:D_FIELD], gq_in[D_FIELD:])).astype(BF16)
    subs = lax.broadcasted_iota(jnp.int32, (CENT, D_FIELD), 1) // SUBW
    table[...] = jnp.zeros((CENT, D_FIELD), F32)

    def table_step(step):
        place = pl.ds(pl.multiple_of(step * GROUP * CENT, GROUP * CENT), GROUP * CENT)
        got = lax.dot_general(low[place, :], grad_pool, NT, preferred_element_type=F32)
        got = got + 256.0 * lax.dot_general(high[place, :], grad_pool, NT, preferred_element_type=F32)
        for j in range(GROUP):
            part = got[j * CENT : (j + 1) * CENT]
            table[...] = table[...] + jnp.where(subs == step * GROUP + j, part, 0.0)

    loop(0, SUB // GROUP, table_step)
    loop(1, EMB, lambda i: hd_copy(i).wait_recv())
    for yy in range(2):
        for zz in range(ZED):
            gg = yy * ZED + zz
            tab[yy, zz % 4, zz // 4, :8] = table[gg * 8 : gg * 8 + 8]
            tab[yy, zz % 4, zz // 4, 8:] = jnp.concatenate(
                [heads[gg // 2, gg % 2 : gg % 2 + 1], jnp.zeros((7, 128), F32)], axis=0
            )
    ty_copy = send(tab.at[other], tab_y, ty_s, ty_r, y_mate)
    ty_copy.start()
    sent.append(lambda: ty_copy.wait_send())
    ty_copy.wait_recv()
    tab[y] = tab[y] + tab_y[...]

    def tn_copy(k):
        return send(tab.at[y, order[k]], tab_near.at[k], tn_s.at[k], tn_r.at[k], z_at(near[k]))

    for k in range(3):
        tn_copy(k).start()
        sent.append(lambda k=k: tn_copy(k).wait_send())
    for k in range(3):
        tn_copy(k).wait_recv()
    tab[y, zr] = tab[y, zr] + tab_near[0] + tab_near[1] + tab_near[2]

    def tf_copy(m):
        return send(
            tab.at[y, zr, lax.rem(zq + m, 4)], tab_far.at[m - 1], tf_s.at[m - 1], tf_r.at[m - 1], z_at(4 * m)
        )

    for m in range(1, 4):
        tf_copy(m).start()
        sent.append(lambda m=m: tf_copy(m).wait_send())

    whole = acc[zq]
    for m in range(1, 4):
        far_copy(m).wait_recv()
        whole = whole + decode(far_in[m - 1, :128], far_in[m - 1, 128:])
    red[...] = whole.reshape(EMB, 8, 128)

    def a_copy(i):
        return send(red.at[emb_at(i)], cols.at[e], a_s.at[i], a_r.at[i], (emb_at(i), g))

    loop(1, EMB, lambda i: a_copy(i).start())
    sent.append(lambda: loop(1, EMB, lambda i: a_copy(i).wait_send()))
    cols[e] = red[e]

    for m in range(1, 4):
        tf_copy(m).wait_recv()
    tab_whole = tab[y, zr, zq] + tab_far[0] + tab_far[1] + tab_far[2]
    tab_code, tab_power = encode(tab_whole[:8])
    head_code, head_power = encode(tab_whole[8:])
    loop(1, EMB, lambda i: a_copy(i).wait_recv())
    coded, power = encode(cols[...].reshape(128, 128))
    spots = lax.broadcasted_iota(jnp.int32, (16, 128), 0)
    tail = jnp.concatenate([number(tab_code), number(head_code)], axis=0)
    for at, row in ((9, power), (10, tab_power), (11, head_power)):
        tail = jnp.where(spots == at, row, tail)
    out[y, zr, zq, :128] = coded
    out[y, zr, zq, 128:] = tail.astype(jnp.int32).astype(I16)
    def block(off, m):
        src = lax.rem(z + 2 * ZED - off - 4 * m, ZED)
        return out.at[y, lax.rem(src, 4), src // 4]

    def of_copy(m):
        return send(block(0, 0), block(0, 0), of_s.at[m - 1], of_r.at[m - 1], z_at(4 * m))

    def of_wait(m):
        send(block(0, m), block(0, m), of_s.at[m - 1], of_r.at[m - 1], z_at(4 * m)).wait_recv()

    ways = (1, -1, 2)

    def on_copy(k, m):
        got = block(1 if k == 2 else 0, m)
        return send(got, got, on_s.at[k, m], on_r.at[k, m], z_at(-1 if k == 1 else 1))

    def on_wait(k, m):
        got = block(ways[k], m)
        send(got, got, on_s.at[k, m], on_r.at[k, m], z_at(1)).wait_recv()

    def oy_copy(k, m):
        got = block(0 if k == 0 else ways[k - 1], m)
        return send(got, got, oy_s.at[k, m], oy_r.at[k, m], y_mate)

    def oy_wait(k, m):
        src = lax.rem(z + 2 * ZED - (0 if k == 0 else ways[k - 1]) - 4 * m, ZED)
        got = out.at[other, lax.rem(src, 4), src // 4]
        send(got, got, oy_s.at[k, m], oy_r.at[k, m], y_mate).wait_recv()

    def put(copy):
        copy.start()
        sent.append(copy.wait_send)

    turns = (0, 1, 3, 2)
    for m in (2, 1, 3):
        put(of_copy(m))
    for m in turns:
        if m:
            of_wait(m)
        put(on_copy(0, m))
        put(on_copy(1, m))
        put(oy_copy(0, m))
    for m in turns:
        on_wait(0, m)
        put(on_copy(2, m))
        put(oy_copy(1, m))
        on_wait(1, m)
        put(oy_copy(2, m))
    for m in turns:
        on_wait(2, m)
        put(oy_copy(3, m))
    def keep_all(yy, c, n):
        pltpu.make_async_copy(out.at[yy, c], out_hbm.at[yy, c], kept.at[n, 0]).start()
        sent.append(lambda: pltpu.make_async_copy(out.at[yy, c], out_hbm.at[yy, c], kept.at[n, 0]).wait())

    for c in range(4):
        keep_all(y, c, c)
    for k in range(4):
        for m in range(4):
            oy_wait(k, m)
        off = 0 if k == 0 else ways[k - 1]
        keep_all(other, lax.rem(z + ZED - off, 4), 4 + k)
    for wait in sent:
        wait()


def train(codes, bag, book, w_in, w_out, labels):
    hbm = pl.BlockSpec(memory_space=pl.ANY)
    V, D = pltpu.VMEM, pltpu.SemaphoreType.DMA
    rows = codes.shape[1]
    scratch = [
        V((2, 4, 4, BLOCK, 128), I16),
        V((SUB, rows), jnp.int32),
        V((1, rows), jnp.int32),
        V((CENT, D_FIELD), BF16),
        V((32, 128), F32),
        V((1, SAMP), F32),
        V((D_FIELD, CENT), F32),
        V((SAMP, rows), F8),
        V((D_FIELD, SAMP), F32),
        V((SUB * CENT, SAMP), BF16),
        V((SUB * CENT, SAMP), BF16),
        V((EMB, D_FIELD, WIDE), BF16),
        V((WIDE, EMB * D_FIELD), BF16),
        V((EMB, D_FIELD, SAMP), BF16),
        V((16, EMB, 8, SAMP), F32),
        V((4, 512, SAMP), BF16),
        V((EMB, 8, SAMP), F32),
        V((EMB, 8, 128), F32),
        V((8, D_FIELD, SAMP), F32),
        V((8, D_FIELD, SAMP), F32),
        V((8, D_FIELD, SAMP), F32),
        V((3, 2, D_FIELD + 16, SAMP), I16),
        V((3, 2, D_FIELD + 16, SAMP), I16),
        V((D_FIELD + 16, SAMP), I16),
        V((D_FIELD + 16, SAMP), I16),
        V((D_FIELD, SAMP), F32),
        V((4, 528, 128), I16),
        V((4, 528, 128), I16),
        V((4, 512, 128), F32),
        V((3, 528, 128), I16),
        V((3, 528, 128), I16),
        V((4, 128, 128), F32),
        V((3, 144, 128), I16),
        V((3, 144, 128), I16),
        V((EMB, 8, 128), F32),
        V((EMB, 8, 128), F32),
        V((CENT, D_FIELD), F32),
        V((2, 4, 4, 16, 128), F32),
        V((4, 4, 16, 128), F32),
        V((3, 4, 16, 128), F32),
        V((3, 16, 128), F32),
        D((6,)),
    ]
    sems = [(16,), (16,), (16,), (2, 8), (2, 8), (16,), (16,), (8,), (3,), (), (4,), (3,), (3,), (16,), (), (3,), (3,), (3,), (3, 4), (4, 4)]
    for shape in sems:
        scratch += [D(shape), D(shape)] if shape else [D, D]
    scratch += [D((8, 1))]
    return pl.pallas_call(
        step_kernel,
        out_shape=jax.ShapeDtypeStruct((2, 4, 4, BLOCK, 128), I16),
        in_specs=[hbm] * 6,
        out_specs=hbm,
        scratch_shapes=scratch,
        compiler_params=pltpu.CompilerParams(
            collective_id=1, has_side_effects=True, vmem_limit_bytes=56 << 20
        ),
        name="train_step",
    )(codes, bag, book, w_in, w_out, labels)


def spread_kernel(gathered, weight, table, head, parts, rows, load_s, store_s):
    def load(a):
        return pltpu.make_async_copy(gathered.at[:, :, a], parts.at[a], load_s.at[a])

    def store(a):
        return pltpu.make_async_copy(rows.at[a], weight.at[pl.ds(a * 32, 32)], store_s.at[a])

    for a in range(4):
        load(a).start()
    for a in range(4):
        load(a).wait()
        for c in range(4):
            for yy in range(2):
                tail = number(parts[a, yy, c, 128:])
                scales = jnp.exp2(tail[8:] - 15.0)
                whole = number(parts[a, yy, c, :128]) * scales[1:2]
                for f in range(EMB):
                    spot = f * WIDE + yy * 128
                    rows[a, c * 8 : c * 8 + 8, spot : spot + 128] = whole[f * 8 : f * 8 + 8]
                gg = yy * ZED + a * 4 + c
                table[gg * 8 : gg * 8 + 8, :] = tail[:8] * scales[2:3]
                head[gg : gg + 1, :] = tail[8:9] * scales[3:4]
        store(a).start()
    for a in range(4):
        store(a).wait()


def spread(gathered):
    hbm = pl.BlockSpec(memory_space=pl.ANY)
    vmem = pl.BlockSpec(memory_space=pltpu.VMEM)
    return pl.pallas_call(
        spread_kernel,
        out_shape=(
            jax.ShapeDtypeStruct((D_FIELD, HID), F32),
            jax.ShapeDtypeStruct((CENT, D_FIELD), F32),
            jax.ShapeDtypeStruct((DENSE, 128), F32),
        ),
        in_specs=[hbm],
        out_specs=(hbm, vmem, vmem),
        scratch_shapes=[
            pltpu.VMEM((4, 2, 4, BLOCK, 128), I16),
            pltpu.VMEM((4, 32, HID), F32),
            pltpu.SemaphoreType.DMA((4,)),
            pltpu.SemaphoreType.DMA((4,)),
        ],
        compiler_params=pltpu.CompilerParams(vmem_limit_bytes=60 << 20),
        name="spread",
    )(gathered)


def body(codes, row_bag, codebook, w_in, w_out, labels):
    gathered = train(
        codes[0].T, row_bag, codebook[0], w_in, w_out.reshape(32, 128), labels.reshape(1, SAMP)
    )
    weight, table, head = spread(gathered)
    return table[None], weight, head.reshape(HID)


def solution(mesh):
    in_specs = (
        P("emb", "dense", None),
        P("emb", "dense"),
        P("emb", None, None),
        P("emb", None),
        P(),
        P("dense"),
    )
    out_specs = (P("emb", None, None), P("emb", None), P())
    return jax.shard_map(body, mesh=mesh, in_specs=in_specs, out_specs=out_specs, check_vma=False)
```
